32 devices in a mesh: dp: 8 (over z, x), seq: 4 (over y, core).
Axes of the slice: x: 2, y: 2, z: 4, core: 2. Of those that a mesh axis runs over, the one named last changes fastest.
Arguments:
- xbc: bfloat16 [8, 1024, 2816], P('dp', 'seq'), may hold values from -6 to 6
- gate_input: bfloat16 [8, 1024, 2560], P('dp', 'seq'), may hold values from -6 to 6
- dt_raw: bfloat16 [8, 1024, 40], P('dp', 'seq'), may hold values from -3 to 3
- conv_weight: float32 [4, 2816], replicated, may hold values from -3 to 3
- conv_bias: float32 [2816], replicated, may hold values from -3 to 3
- dt_bias: float32 [40], replicated, may hold values from -0.5 to 0.5
- a_rate: float32 [40], replicated, may hold values from 0.0001953125 to 0.05
- d_skip: float32 [40], replicated, may hold values from 0.5 to 1.5
- norm_gain: float32 [2560], replicated, may hold values from 0.25 to 1.75
- labels: int32 [8], P('dp'), may hold values from 0 to 1, as said below
- readout: int32 [8, 4], P('dp'), may hold values from 0 to 1023
Outputs:
- layer_out: bfloat16 [8, 1024, 2560], P('dp', 'seq')
- steering: float32 [2560, 128], P(('dp', 'seq'))
The draws below stay inside these ranges and needn't reach their ends.
Inputs may be any that keep to these rules, and one draw needn't show every extreme that they name: `labels`: every label is 0 or 1, and both classes occur.
All inputs are finite; a program needn't handle non-finite values.
Results may differ from the reference program's by a relative error of at most 0.0034.
Values may be sent and summed in bfloat16 or wider, within the bound.
No kernel may reach another device: no remote copies, remote signals or barrier semaphores. Data moves between devices by JAX's collectives and lax.ppermute only.
A program may use at most 64 MiB of HBM per device.

```python
import math
import jax
import jax.numpy as jnp
from jax import lax

H = 40
P_SIZE = 64
N = 128
KW = 4
R = 4
L_DEV = 256
CH = 2816
BATCH = 8
SEQLEN = 1024


def draw_labels(key, part):
    values = jax.random.randint(key, (BATCH,), 0, 2, dtype=jnp.int32)
    return values.at[0].set(0).at[1].set(1)


def set_ends(array, key, low, largest):
    dims = array.shape
    spot = [jax.random.randint(jax.random.fold_in(key, axis), (), 0, dims[axis]) for axis in range(len(dims))]
    array = array.at[tuple(spot)].set(low)
    longest = dims.index(max(dims))
    spot[longest] = (spot[longest] + 1) % dims[longest]
    return array.at[tuple(spot)].set(largest)


def steps_of(key, shape, split, low, high):
    loudness = 1.0
    for position, shards_of in split:
        draws = jax.random.uniform(jax.random.fold_in(jax.random.fold_in(key, 6), position), (shards_of,), jnp.float32, low / len(split), high / len(split))
        loudness = loudness * jnp.repeat(jnp.exp(draws), shape[position] // shards_of).reshape((-1,) + (1,) * (len(shape) - 1 - position))
    return loudness


def noise(stream_key, shape, scale, bound, shards=(), kind=jnp.bfloat16):
    entries = jax.random.normal(stream_key, shape, jnp.float32) * scale
    if len(shards) > 0:
        entries = steps_of(stream_key, shape, shards, -0.22, 0.18) * entries
    return jnp.clip(entries, min=-bound, max=bound).astype(kind)


def setup_inputs(seed: int = 0) -> dict:
    seeds = jax.random.split(jax.random.key(seed), 12)
    xbc = noise(seeds[0], (BATCH, SEQLEN, CH), 1.0, 6.0, ((0, 8), (1, 4)))
    gate_input = noise(seeds[1], (BATCH, SEQLEN, H * P_SIZE), 1.0, 6.0, ((0, 8), (1, 4)))
    dt_raw = noise(seeds[2], (BATCH, SEQLEN, H), 0.5, 3.0, ((0, 8), (1, 4)))
    conv_weight = noise(seeds[3], (KW, CH), KW ** -0.5, 3.0, (), jnp.float32)
    conv_bias = noise(seeds[4], (CH,), 0.5, 3.0, (), jnp.float32)
    dt_bias = jnp.clip(jax.random.uniform(seeds[5], (H,), jnp.float32, -0.5, 0.5), -0.5, 0.5)
    a_rate = jnp.clip(jnp.exp(jax.random.uniform(seeds[6], (H,), jnp.float32, math.log(0.0001953125), math.log(0.05))), 0.0001953125, 0.05)
    d_skip = jnp.clip(jax.random.uniform(seeds[7], (H,), jnp.float32, 0.5, 1.5), 0.5, 1.5)
    norm_gain = jnp.clip(1.0 + 0.15 * jax.random.normal(seeds[8], (H * P_SIZE,), jnp.float32), 0.25, 1.75)
    labels = draw_labels(jax.random.fold_in(seeds[11], 71), 0)
    readout = set_ends(jax.random.randint(seeds[10], (BATCH, R), 0, SEQLEN), jax.random.fold_in(seeds[10], 1), 0, SEQLEN - 1).astype(jnp.int32)
    return {"xbc": xbc, "gate_input": gate_input, "dt_raw": dt_raw, "conv_weight": conv_weight, "conv_bias": conv_bias, "dt_bias": dt_bias, "a_rate": a_rate, "d_skip": d_skip, "norm_gain": norm_gain, "labels": labels, "readout": readout}


group_heads = 8
highest = lax.Precision.HIGHEST

def local_terms(x_vals, b_vals, c_vals, dt_vals, cumulative, points, offset):
    row_count = x_vals.shape[0]
    x_wide = x_vals.astype(jnp.float32).reshape(row_count, H, P_SIZE)
    b_wide = b_vals.astype(jnp.float32)
    c_wide = c_vals.astype(jnp.float32)
    scores = lax.dot_general(c_vals, b_vals, (((1,), (1,)), ((), ())), preferred_element_type=jnp.float32)
    positions = jnp.arange(row_count, dtype=jnp.int32)
    causal = positions[:, None] >= positions[None, :]
    cum_heads = cumulative.T
    dt_heads = dt_vals.T

    def group_step(group_index, buffer):
        head_start = group_index * group_heads
        cum_group = lax.dynamic_slice_in_dim(cum_heads, head_start, group_heads, 0)
        dt_group = lax.dynamic_slice_in_dim(dt_heads, head_start, group_heads, 0)
        x_group = lax.dynamic_slice_in_dim(x_wide, head_start, group_heads, 1)
        spread = jnp.where(causal[None], cum_group[:, :, None] - cum_group[:, None, :], -1e+30)
        weight = jnp.exp(spread) * dt_group[:, None, :] * scores[None]
        partial_value = jnp.einsum('hts,shp->thp', weight, x_group, precision=highest)
        return lax.dynamic_update_slice_in_dim(buffer, partial_value, head_start, 1)
    diagonal_part = lax.fori_loop(0, H // group_heads, group_step, jnp.zeros((row_count, H, P_SIZE), jnp.float32))
    final_log = cumulative[row_count - 1]
    to_end = jnp.exp(final_log[None, :] - cumulative) * dt_vals
    decay_total = jnp.exp(final_log)
    local_state = jnp.einsum('sk,sn->kn', (to_end[:, :, None] * x_wide).reshape(row_count, H * P_SIZE), b_wide, precision=highest).reshape(H, P_SIZE, N)
    local_index = (points - offset).astype(jnp.int32)
    owned_flag = ((local_index >= 0) & (local_index < row_count)).astype(jnp.float32)
    one_hot = (positions[None, :] == local_index[:, None]).astype(jnp.float32)
    cum_at = jnp.dot(one_hot, cumulative, precision=highest)
    before = positions[None, :] <= local_index[:, None]
    spread = jnp.where(before[:, :, None], cum_at[:, None, :] - cumulative[None], -1e+30)
    read_weight = lax.optimization_barrier(jnp.sum(owned_flag[:, None, None] * jnp.exp(spread), axis=0)) * dt_vals / R
    carry_weight = lax.optimization_barrier(jnp.sum(owned_flag[:, None] * jnp.exp(cum_at), axis=0)) / R
    read_local = jnp.einsum('sk,sn->kn', (read_weight[:, :, None] * x_wide).reshape(row_count, H * P_SIZE), b_wide, precision=highest).reshape(H, P_SIZE, N)
    return (diagonal_part, x_wide, c_wide, local_state, decay_total, read_local, carry_weight)

def finish_block(diagonal_part, x_wide, c_wide, cumulative, h_in, gate_rows, d_skip, norm_gain):
    row_count = x_wide.shape[0]
    incoming = jnp.einsum('tn,hpn->thp', c_wide, h_in, precision=highest)
    ssm_out = diagonal_part + jnp.exp(cumulative)[:, :, None] * incoming + d_skip[None, :, None] * x_wide
    gated_out = ssm_out.reshape(row_count, H * P_SIZE) * jax.nn.silu(gate_rows.astype(jnp.float32))
    inv_rms = lax.rsqrt(lax.optimization_barrier(jnp.mean(gated_out * gated_out, axis=-1, keepdims=True)) + 1e-05)
    return (gated_out * inv_rms * norm_gain).astype(jnp.bfloat16)

def reference(xbc, gate_input, dt_raw, conv_weight, conv_bias, dt_bias, a_rate, d_skip, norm_gain, labels, readout):
    n_one = jnp.sum(labels.astype(jnp.float32))
    n_zero = labels.shape[0] - n_one
    blocks = SEQLEN // L_DEV

    def one_sequence(sequence):
        seq_rows, gate_rows, raw_rows, class_label, points = sequence
        padded = jnp.concatenate([jnp.zeros((KW - 1, CH), jnp.bfloat16), seq_rows], axis=0).astype(jnp.float32)
        conv_sum = conv_bias
        for tap_index in range(KW):
            conv_sum = conv_sum + conv_weight[tap_index] * padded[tap_index:tap_index + SEQLEN]
        activated = jax.nn.silu(conv_sum).astype(jnp.bfloat16)
        dt_vals = jax.nn.softplus(raw_rows.astype(jnp.float32) + dt_bias)

        def block_step(scan_carry, block_in):
            carried, mean_state = scan_carry
            act_block, gate_block, dt_block, block_index = block_in
            cumulative = jnp.cumsum(-a_rate * dt_block, axis=0)
            diagonal_part, x_wide, c_wide, local_state, decay_total, read_local, carry_weight = local_terms(act_block[:, :H * P_SIZE], act_block[:, H * P_SIZE:H * P_SIZE + N], act_block[:, H * P_SIZE + N:], dt_block, cumulative, points, block_index * L_DEV)
            outputs = finish_block(diagonal_part, x_wide, c_wide, cumulative, carried, gate_block, d_skip, norm_gain)
            mean_state = mean_state + carry_weight[:, None, None] * carried + read_local
            carried = decay_total[:, None, None] * carried + local_state
            return ((carried, mean_state), outputs)
        start_state = jnp.zeros((H, P_SIZE, N), jnp.float32)
        block_ids = jnp.arange(blocks).astype(jnp.int32)
        (carried, mean_state), outputs = lax.scan(block_step, (start_state, start_state), (activated.reshape(blocks, L_DEV, CH), gate_rows.reshape(blocks, L_DEV, H * P_SIZE), dt_vals.reshape(blocks, L_DEV, H), block_ids))
        class_value = class_label.astype(jnp.float32)
        class_weight = class_value / n_one - (1.0 - class_value) / n_zero
        return (outputs.reshape(SEQLEN, H * P_SIZE), class_weight * mean_state)
    layer_out, partials = lax.map(one_sequence, (xbc, gate_input, dt_raw, labels, readout))
    return (layer_out, lax.optimization_barrier(jnp.sum(partials, axis=0)).reshape(H * P_SIZE, N))
```

```python
import functools

import jax
import jax.numpy as jnp
from jax import lax
from jax.experimental import pallas as pl
from jax.experimental.pallas import tpu as pltpu
from jax.sharding import PartitionSpec as P

H = 40
P_SIZE = 64
N = 128
KW = 4
R = 4
D = H * P_SIZE
HALF = D // 2
BC = 2 * N
SIDE = HALF + BC
CHUNK = 256
EDGE = 16
F32 = jnp.float32
BF16 = jnp.bfloat16
VMEM = pl.BlockSpec(memory_space=pltpu.VMEM)
SMEM = pl.BlockSpec(memory_space=pltpu.SMEM)
ANY = pl.BlockSpec(memory_space=pl.ANY)
MIB = 1024 * 1024


def params(mib):
    return pltpu.CompilerParams(vmem_limit_bytes=mib * MIB)


def cost(flops, read):
    return pl.CostEstimate(flops=flops, bytes_accessed=read, transcendentals=0)


def dot(a, b):
    return jnp.dot(a, b, preferred_element_type=F32)


def pack(w):
    high = w.astype(BF16).astype(F32)
    gap = jnp.zeros((w.shape[0], 64 - H), F32)
    return jnp.concatenate([high, gap, w - high, gap], axis=1).astype(BF16)


def spread_matrix(first_head):
    row = lax.broadcasted_iota(jnp.int32, (128, CHUNK), 0)
    lane = lax.broadcasted_iota(jnp.int32, (128, CHUNK), 1)
    hit = (row & 63) == first_head + lane // P_SIZE
    return jnp.where(hit, 1.0, 0.0).astype(BF16)


def silu(v):
    half = 0.5 * v
    return half + half * jnp.tanh(half)


def steps_kernel(own_ref, other_ref, bias_ref, rate_ref, skip_ref, points_ref, ws_ref, wr_ref, e_ref, eg_ref, rows_ref, small_ref):
    place = lax.axis_index("seq")
    core = lax.rem(place, 2)
    n = own_ref.shape[0]
    base = (place - core) * n
    own = own_ref[...].astype(F32)
    other = other_ref[...].astype(F32)
    first = core == 0
    row = lax.broadcasted_iota(jnp.int32, (n, n), 0)
    lane = lax.broadcasted_iota(jnp.int32, (n, n), 1)
    lower = jnp.where(row >= lane, 1.0, 0.0).astype(BF16)
    dts, cums = [], []
    for block in range(2):
        raw = jnp.where(first == (block == 0), own, other) + bias_ref[...]
        dt = jnp.maximum(raw, 0.0) + jnp.log1p(jnp.exp(-jnp.abs(raw)))
        step = -rate_ref[...] * dt
        high = step.astype(BF16)
        rest = step - high.astype(F32)
        middle = rest.astype(BF16)
        low = (rest - middle.astype(F32)).astype(BF16)
        dts.append(dt)
        cums.append(dot(lower, high) + (dot(lower, middle) + dot(lower, low)))
    ends = [cum[n - 1 : n] for cum in cums]
    for block in range(2):
        ws_ref[block * n : (block + 1) * n] = pack(dts[block] * jnp.exp(ends[block] - cums[block]))
    total = [cums[0], ends[0] + cums[1]]
    index = lax.broadcasted_iota(jnp.int32, (n, H), 0)
    weight = [jnp.zeros((n, H), F32), jnp.zeros((n, H), F32)]
    carry = jnp.zeros((1, H), F32)
    for r in range(R):
        at = points_ref[0, r] - base
        inside = jnp.where((at >= 0) & (at < 2 * n), 1.0, 0.0)
        level = jnp.zeros((1, H), F32)
        for block in range(2):
            level += jnp.sum(jnp.where(index + block * n == at, total[block], 0.0), axis=0, keepdims=True)
        for block in range(2):
            seen = jnp.where(index + block * n <= at, jnp.exp(jnp.minimum(level - total[block], 0.0)), 0.0)
            weight[block] += inside * seen
        carry += inside * jnp.exp(level)
    for block in range(2):
        wr_ref[block * n : (block + 1) * n] = pack(weight[block] * dts[block] * (1.0 / R))
    cum = jnp.where(first, cums[0], cums[1])
    e_ref[...] = pack(jnp.exp(cum))
    eg_ref[...] = pack(jnp.exp(cum - jnp.where(first, ends[0], ends[1])))
    decay = [jnp.exp(ends[0]), jnp.exp(ends[1])]
    zero = jnp.zeros((1, H), F32)
    table = [decay[0], decay[1], skip_ref[...], zero, zero, zero, zero, zero]
    rows_ref[...] = pack(jnp.concatenate(table + table, axis=0))
    whole = [carry * (1.0 / R), jnp.exp(ends[0] + ends[1])] + [zero] * 6
    small_ref[...] = jnp.concatenate(whole, axis=0)


def state_kernel(
    own_ref, other_ref, edge_a_ref, edge_b_ref, ws_ref, wr_ref, rows_ref, later_ref, conv_w_ref, conv_b_ref, ones_ref, label_ref,
    state_ref, early_ref, keep_ref, send_ref, act_own_ref, act_other_ref, bc_ref,
    x_ref, act_ref, taps_ref, bias_ref, read_ref, sems,
    *, sequences, split,
):
    place = lax.axis_index("seq")
    core = lax.rem(place, 2)
    n = own_ref.shape[1]
    col = pl.multiple_of(core * HALF, 128)
    copies = []
    for i, (source, to) in enumerate(((own_ref, core), (other_ref, 1 - core))):
        rows = pl.ds(pl.multiple_of(EDGE + to * n, 16), n)
        copies.append(pltpu.make_async_copy(source.at[0, :, pl.ds(D, BC)], x_ref.at[rows, pl.ds(HALF, BC)], sems.at[2 * i]))
        copies.append(pltpu.make_async_copy(source.at[0, :, pl.ds(col, HALF)], x_ref.at[rows, pl.ds(0, HALF)], sems.at[2 * i + 1]))
    for copy in (copies[0], copies[2], copies[1], copies[3]):
        copy.start()
    started = jnp.where(place >= 2, 1.0, 0.0)
    edge = jnp.where(core == 0, edge_a_ref[0].astype(F32), edge_b_ref[0].astype(F32)) * started
    taps_ref[:, :HALF] = conv_w_ref[:, pl.ds(col, HALF)]
    taps_ref[:, HALF:] = conv_w_ref[:, D:]
    bias_ref[:, :HALF] = conv_b_ref[:, pl.ds(col, HALF)]
    bias_ref[:, HALF:] = conv_b_ref[:, D:]
    x_ref[0:EDGE, HALF:] = edge[:, D:].astype(BF16)

    @pl.when(core == 0)
    def _():
        x_ref[0:EDGE, :HALF] = edge[:, :HALF].astype(BF16)

    @pl.when(core == 1)
    def _():
        x_ref[0:EDGE, :HALF] = edge[:, HALF:D].astype(BF16)

    tile = 128

    def convolve(at):
        cols = pl.ds(at, CHUNK)
        taps = taps_ref[:, cols]
        bias = bias_ref[:, cols]
        for t in range(2 * n // tile):
            seen = x_ref[t * tile : (t + 1) * tile + EDGE, cols].astype(F32)
            total = bias + taps[KW - 1 : KW] * seen[EDGE:]
            for back in range(1, KW):
                total += taps[KW - 1 - back : KW - back] * pltpu.roll(seen, back, 0)[EDGE:]
            act_ref[t * tile : (t + 1) * tile, cols] = silu(total).astype(BF16)

    copies[0].wait()
    copies[2].wait()
    convolve(HALF)
    b_turned = act_ref[:, HALF : HALF + N].astype(F32).T.astype(BF16)
    ones = ones_ref[0]
    label = label_ref[0].astype(F32)
    class_weight = label / ones - (1.0 - label) / (sequences - ones)
    after = jnp.where(place < lax.axis_size("seq") - 2, later_ref[0:1], 0.0)
    after = pack(jnp.concatenate([after] * 16, axis=0))
    copies[1].wait()
    copies[3].wait()

    @pl.loop(0, HALF // CHUNK)
    def _(j):
        at = pl.multiple_of(j * CHUNK, CHUNK)
        cols = pl.ds(at, CHUNK)
        convolve(at)
        spread = spread_matrix(core * (H // 2) + j * (CHUNK // P_SIZE))
        table = dot(rows_ref[...], spread)
        ahead = dot(after, spread)[0:1]
        act = act_ref[:, cols].astype(F32)
        weighted = (act * dot(ws_ref[...], spread)).astype(BF16)
        early = dot(b_turned[:, :n], weighted[:n])
        late = dot(b_turned[:, n:], weighted[n:])
        state = table[1:2] * early + late
        early_ref[:, cols] = early.astype(BF16)
        state_ref[:, cols] = state.astype(BF16)
        read = act * dot(wr_ref[...], spread)
        high = read.astype(BF16)
        low = (read - high.astype(F32)).astype(BF16)
        seen = dot(b_turned, high) + dot(b_turned, low) + ahead * state
        read_ref[pl.ds(at, CHUNK)] = (class_weight * seen).T

    if split:
        x_bit = lax.rem(lax.axis_index("dp"), 2)
        part = D // 8
        for q in range(2):
            keep_ref[q * part : (q + 1) * part] = read_ref[pl.ds(pl.multiple_of((2 * q + x_bit) * part, 8), part)]
            send_ref[q * part : (q + 1) * part] = read_ref[pl.ds(pl.multiple_of((2 * q + 1 - x_bit) * part, 8), part)]
    else:
        keep_ref[...] = read_ref[...]
        send_ref[...] = jnp.zeros_like(send_ref)
    mine = pl.ds(pl.multiple_of(core * n, 16), n)
    act_own_ref[...] = act_ref[mine, :HALF]
    bc_ref[...] = act_ref[mine, HALF:]
    act_other_ref[...] = act_ref[pl.ds(pl.multiple_of((1 - core) * n, 16), n), :HALF]


def diagonal_kernel(act_own_ref, act_other_ref, bc_ref, ws_ref, e_ref, eg_ref, rows_ref, gate_ref, near_ref, far_ref):
    core = lax.rem(lax.axis_index("seq"), 2)
    n = act_own_ref.shape[0]
    scores = lax.dot_general(bc_ref[:, N:], bc_ref[:, :N], (((1,), (1,)), ((), ())), preferred_element_type=F32)
    row = lax.broadcasted_iota(jnp.int32, (n, n), 0)
    lane = lax.broadcasted_iota(jnp.int32, (n, n), 1)
    masked = jnp.where(row >= lane, scores, 0.0).astype(BF16)
    ws = ws_ref[pl.ds(pl.multiple_of(core * n, 16), n)]
    for side, source in enumerate((act_own_ref, act_other_ref)):
        half = core if side == 0 else 1 - core

        @pl.loop(0, HALF // CHUNK)
        def _(j):
            at = pl.multiple_of(j * CHUNK, CHUNK)
            cols = pl.ds(at, CHUNK)
            spread = spread_matrix(half * (H // 2) + j * (CHUNK // P_SIZE))
            act = source[:, cols].astype(F32)
            weighted = (act * dot(ws, spread)).astype(BF16)
            value = dot(eg_ref[...], spread) * dot(masked, weighted)
            value += dot(rows_ref[...], spread)[2:3] * act
            gate = silu(gate_ref[0, :, pl.ds(pl.multiple_of(half * HALF + at, CHUNK), CHUNK)].astype(F32))
            near_ref[side, :, cols] = value * gate
            far_ref[side, :, cols] = dot(e_ref[...], spread) * gate


def finish_kernel(near_ref, far_ref, bc_ref, h_own_ref, h_other_ref, early_own_ref, early_other_ref, rows_ref, gain_ref, out_ref, g_ref):
    place = lax.axis_index("seq")
    core = lax.rem(place, 2)
    n = bc_ref.shape[0]
    second = core == 1
    started = place >= 2
    squares = jnp.zeros((n, CHUNK), F32)
    c_vals = bc_ref[:, N:]
    for side in range(2):
        half = core if side == 0 else 1 - core
        h_ref = (h_own_ref, h_other_ref)[side]
        early_ref = (early_own_ref, early_other_ref)[side]
        for j in range(HALF // CHUNK):
            cols = pl.ds(j * CHUNK, CHUNK)
            spread = spread_matrix(half * (H // 2) + j * (CHUNK // P_SIZE))
            decay = jnp.where(second, dot(rows_ref[...], spread)[0:1], 1.0)
            h = jnp.where(started, h_ref[:, cols].astype(F32), 0.0) * decay
            h += jnp.where(second, early_ref[:, cols].astype(F32), 0.0)
            g = near_ref[side, :, cols] + far_ref[side, :, cols] * dot(c_vals, h.astype(BF16))
            g_ref[side, :, cols] = g
            squares += g * g
    scale = lax.rsqrt(jnp.sum(squares, axis=-1, keepdims=True) * (1.0 / D) + 1e-05)
    for side in range(2):
        half = core if side == 0 else 1 - core
        for j in range(HALF // CHUNK):
            cols = pl.ds(pl.multiple_of(half * HALF + j * CHUNK, CHUNK), CHUNK)
            g = g_ref[side, :, pl.ds(j * CHUNK, CHUNK)]
            out_ref[0, :, cols] = (g * scale * gain_ref[:, cols]).astype(BF16)


def halve_kernel(kept_ref, came_ref, keep_ref, send_ref, *, axis, divide):
    bit = lax.rem(lax.axis_index(axis) // divide, 2)
    part = keep_ref.shape[0]
    mine = pl.ds(pl.multiple_of(bit * part, 8), part)
    yours = pl.ds(pl.multiple_of((1 - bit) * part, 8), part)
    send_ref[...] = kept_ref[yours] + came_ref[yours]
    keep_ref[...] = kept_ref[mine] + came_ref[mine]


def halve(kept, came, axis, divide):
    part = jax.ShapeDtypeStruct((kept.shape[0] // 2, N), F32)
    return pl.pallas_call(
        functools.partial(halve_kernel, axis=axis, divide=divide),
        out_shape=(part, part),
        in_specs=[VMEM] * 2,
        out_specs=(VMEM, VMEM),
        compiler_params=params(8),
        cost_estimate=cost(kept.size, kept.size * 12),
        name="halve",
    )(kept, came)


def last_kernel(kept_ref, came_ref, first_ref, second_ref, third_ref):
    part = first_ref.shape[0]
    z_bit = lax.rem(lax.axis_index("dp") // 4, 2)
    core = lax.rem(lax.axis_index("seq"), 2)
    zero = kept_ref[0:part] + came_ref[0:part]
    one = kept_ref[part:] + came_ref[part:]
    ring_one = z_bit == 0
    first_ref[...] = jnp.where(ring_one, one, zero)
    cross_one = core == 0
    second_ref[...] = jnp.where(cross_one, one, zero)
    third_ref[...] = jnp.where(core == 0, zero, one)


def last_sum_kernel(own_ref, ring_ref, cross_ref, out_ref):
    z_bit = lax.rem(lax.axis_index("dp") // 4, 2)
    core = lax.rem(lax.axis_index("seq"), 2)
    same = z_bit == core
    out_ref[...] = ring_ref[...] + jnp.where(same, own_ref[...], cross_ref[...])


def steering_sum(keep, send):
    swap = lambda k: [(i, i ^ k) for i in range(8)]
    came = lax.ppermute(send, "dp", swap(1))
    keep, send = halve(keep, came, "dp", 2)
    came = lax.ppermute(send, "dp", swap(2))
    keep, send = halve(keep, came, "seq", 2)
    came = lax.ppermute(send, "seq", [(i, i ^ 2) for i in range(4)])
    part = jax.ShapeDtypeStruct((keep.shape[0] // 2, N), F32)
    first, second, third = pl.pallas_call(
        last_kernel, out_shape=(part,) * 3, in_specs=[VMEM] * 2, out_specs=(VMEM,) * 3, compiler_params=params(8), name="last_parts"
    )(keep, came)
    ring, cross = [], []
    for dp in range(8):
        for seq in range(4):
            z, core = dp // 4, seq % 2
            place = lambda z_to, core_to: (dp % 4 + 4 * z_to) * 4 + seq - core + core_to
            ring.append((dp * 4 + seq, place(core, 1 if z == 0 else 0)))
            cross.append((dp * 4 + seq, place(core, 1 - core) if z != core else dp * 4 + seq))
    ring = lax.ppermute(first, ("dp", "seq"), ring)
    cross = lax.ppermute(second, ("dp", "seq"), cross)
    return pl.pallas_call(
        last_sum_kernel, out_shape=part, in_specs=[VMEM] * 3, out_specs=VMEM, compiler_params=params(8), name="last_sum"
    )(third, ring, cross)


def on_device(xbc, gate_input, dt_raw, conv_weight, conv_bias, dt_bias, a_rate, d_skip, norm_gain, labels, readout):
    n = xbc.shape[1]
    places = lax.axis_size("seq")
    sequences = lax.axis_size("dp")
    chips = places // 2
    place = lax.axis_index("seq")
    core = place % 2
    split = sequences == 8 and places == 4
    pair = [(i, i ^ 1) for i in range(places)]
    shape = jax.ShapeDtypeStruct

    dt_other = lax.ppermute(dt_raw[0], "seq", pair)
    xbc_other = lax.ppermute(xbc, "seq", pair)
    tail = xbc[:, n - EDGE :, :]
    edge_a = lax.ppermute(tail, "seq", [(i, (i + 1) % places) for i in range(places)])
    edge_b = lax.ppermute(tail, "seq", [(i, (i + 2) % places) for i in range(places)])

    ws, wr, e, eg, rows, small = pl.pallas_call(
        steps_kernel,
        out_shape=(
            shape((2 * n, 128), BF16), shape((2 * n, 128), BF16), shape((n, 128), BF16), shape((n, 128), BF16),
            shape((16, 128), BF16), shape((8, H), F32),
        ),
        in_specs=[VMEM] * 5 + [SMEM],
        out_specs=(VMEM,) * 6,
        compiler_params=params(16),
        cost_estimate=cost(2 * 6 * n * n * 128, 8 * n * 256),
        name="steps",
    )(dt_raw[0], dt_other, dt_bias[None], a_rate[None], d_skip[None], readout)

    later = jnp.zeros_like(small)
    for step in range(chips - 1):
        out = small if step == 0 else small.at[0:1].add(small[1:2] * later[0:1])
        later = lax.ppermute(out, "seq", [(i, (i - 2) % places) for i in range(places)])
        if chips > 2:
            later = jnp.where(place < places - 2, later, 0.0)

    ones = labels.astype(F32)
    reach = 1
    while reach < sequences:
        ones = ones + lax.ppermute(ones, "dp", [(i, i ^ reach) for i in range(sequences)])
        reach *= 2

    read_rows = HALF // 2 if split else HALF
    state, early, keep, send, act_own, act_other, bc = pl.pallas_call(
        functools.partial(state_kernel, sequences=float(sequences), split=split),
        out_shape=(
            shape((N, HALF), BF16), shape((N, HALF), BF16), shape((read_rows, N), F32),
            shape((read_rows if split else 8, N), F32),
            shape((n, HALF), BF16), shape((n, HALF), BF16), shape((n, BC), BF16),
        ),
        in_specs=[ANY, ANY] + [VMEM] * 8 + [SMEM, SMEM],
        out_specs=(VMEM,) * 7,
        scratch_shapes=[
            pltpu.VMEM((EDGE + 2 * n, SIDE), BF16),
            pltpu.VMEM((2 * n, SIDE), BF16),
            pltpu.VMEM((KW, SIDE), F32),
            pltpu.VMEM((1, SIDE), F32),
            pltpu.VMEM((HALF, N), F32),
            pltpu.SemaphoreType.DMA((4,)),
        ],
        compiler_params=params(24),
        cost_estimate=cost(10 * 2 * n * N * HALF, 4 * 2 * n * SIDE),
        name="states",
    )(xbc, xbc_other, edge_a, edge_b, ws, wr, rows, later, conv_weight, conv_bias[None], ones, labels)

    h = state
    for step in range(chips - 1):
        if step:
            scale = jnp.repeat(lax.dynamic_slice_in_dim(small[1], core * (H // 2), H // 2), P_SIZE)
            h = (h.astype(F32) * scale + state.astype(F32)).astype(BF16)
        h = lax.ppermute(h, "seq", [(i, (i + 2) % places) for i in range(places)])
        if chips > 2:
            h = jnp.where(place >= 2, h, jnp.zeros_like(h))
    act_in = lax.ppermute(act_other, "seq", pair)
    early_in = lax.ppermute(early, "seq", pair)

    if split:
        steering = steering_sum(keep, send)
    else:
        whole = lax.dynamic_update_slice_in_dim(jnp.zeros((D, N), F32), keep, core * HALF, 0)
        steering = lax.psum_scatter(whole, ("dp", "seq"), scatter_dimension=0, tiled=True)

    near, far = pl.pallas_call(
        diagonal_kernel,
        out_shape=(shape((2, n, HALF), F32), shape((2, n, HALF), F32)),
        in_specs=[VMEM] * 8,
        out_specs=(VMEM, VMEM),
        compiler_params=params(24),
        cost_estimate=cost(8 * n * n * D, 4 * n * D),
        name="diagonal",
    )(act_own, act_in, bc, ws, e, eg, rows, gate_input)
    h_other = lax.ppermute(h, "seq", pair)
    layer_out = pl.pallas_call(
        finish_kernel,
        out_shape=shape((1, n, D), BF16),
        in_specs=[VMEM] * 9,
        out_specs=VMEM,
        scratch_shapes=[pltpu.VMEM((2, n, HALF), F32)],
        compiler_params=params(24),
        cost_estimate=cost(2 * n * N * D, 12 * n * D),
        name="finish",
    )(near, far, bc, h, h_other, early, early_in, rows, norm_gain[None])
    return (layer_out, steering)


def solution(mesh):
    return jax.shard_map(
        on_device,
        mesh=mesh,
        in_specs=(
            P("dp", "seq", None),
            P("dp", "seq", None),
            P("dp", "seq", None),
            P(),
            P(),
            P(),
            P(),
            P(),
            P(),
            P("dp"),
            P("dp", None),
        ),
        out_specs=(P("dp", "seq", None), P(("dp", "seq"), None)),
        check_vma=False,
    )
```

```python
import functools

import jax
import jax.numpy as jnp
from jax import lax
from jax.experimental import pallas as pl
from jax.experimental.pallas import tpu as pltpu
from jax.sharding import PartitionSpec as P

H = 40
P_SIZE = 64
N = 128
KW = 4
R = 4
D = H * P_SIZE
HALF = D // 2
BC = 2 * N
SIDE = HALF + BC
CH = D + BC
CHUNK = 256
EDGE = 16
F32 = jnp.float32
BF16 = jnp.bfloat16
VMEM = pl.BlockSpec(memory_space=pltpu.VMEM)
SMEM = pl.BlockSpec(memory_space=pltpu.SMEM)
ANY = pl.BlockSpec(memory_space=pl.ANY)
HBM = pl.BlockSpec(memory_space=pltpu.HBM)
MIB = 1024 * 1024


def params(mib):
    return pltpu.CompilerParams(vmem_limit_bytes=mib * MIB)


def cost(flops, read):
    return pl.CostEstimate(flops=flops, bytes_accessed=read, transcendentals=0)


def in_hbm(x):
    return pltpu.with_memory_space_constraint(x, pltpu.HBM)


def tied(x, *others):
    return lax.optimization_barrier((x,) + others)[0]


def dot(a, b):
    return jnp.dot(a, b, preferred_element_type=F32)


def pack(w):
    high = w.astype(BF16).astype(F32)
    gap = jnp.zeros((64 - H, w.shape[1]), F32)
    return jnp.concatenate([high, gap, w - high, gap], axis=0).T.astype(BF16)


def beside(columns):
    lane = lax.broadcasted_iota(jnp.int32, (H, 128), 1)
    table = jnp.zeros((H, 128), F32)
    for i, column in enumerate(columns):
        table = jnp.where(lane == i, column, table)
    return table


def turned(rows):
    table = jnp.concatenate(list(rows) + [jnp.zeros((8 - len(rows), H), F32)], axis=0)
    return jnp.concatenate([table, jnp.zeros((8, 128 - H), F32)], axis=1).T[:H]


def spread_matrix(first_head):
    row = lax.broadcasted_iota(jnp.int32, (128, CHUNK), 0)
    lane = lax.broadcasted_iota(jnp.int32, (128, CHUNK), 1)
    hit = (row & 63) == first_head + lane // P_SIZE
    return jnp.where(hit, 1.0, 0.0).astype(BF16)


def silu(v):
    half = 0.5 * v
    return half + half * jnp.tanh(half)


def fetch(pairs, sems):
    copies = [pltpu.make_async_copy(source, to, sems.at[i]) for i, (source, to) in enumerate(pairs)]
    for copy in copies:
        copy.start()
    for copy in copies:
        copy.wait()


def step_sizes(raw, bias):
    raw = raw + bias
    return jnp.maximum(raw, 0.0) + jnp.log1p(jnp.exp(-jnp.abs(raw)))


def running_sums(steps):
    n = steps[0].shape[1]
    row = lax.broadcasted_iota(jnp.int32, (n, n), 0)
    lane = lax.broadcasted_iota(jnp.int32, (n, n), 1)
    upper = jnp.where(row <= lane, 1.0, 0.0).astype(BF16)
    parts = []
    for step in steps:
        high = step.astype(BF16).astype(F32)
        middle = (step - high).astype(BF16).astype(F32)
        parts += [high, middle, step - high - middle]
    sums = dot(jnp.concatenate(parts, axis=0).astype(BF16), upper)
    return [sums[i : i + H] + (sums[i + H : i + 2 * H] + sums[i + 2 * H : i + 3 * H]) for i in range(0, 3 * H * len(steps), 3 * H)]


def read_levels(points, base, total):
    n = total[0].shape[1]
    index = lax.broadcasted_iota(jnp.int32, (H, n), 1)
    found = []
    for r in range(R):
        at = points[r : r + 1, 0:1] - base
        inside = jnp.where((at >= 0) & (at < 2 * n), 1.0, 0.0)
        level = jnp.zeros((H, n), F32)
        for block in range(2):
            level += jnp.where(index + block * n == at, total[block], 0.0)
        found.append((at, inside, jnp.sum(level, axis=1, keepdims=True)))
    return found


def carry_of(found):
    carry = jnp.zeros((H, 1), F32)
    for _, inside, level in found:
        carry += inside * jnp.exp(level)
    return carry * (1.0 / R)


def tail_kernel(
    xbc_hbm, dt_hbm, bias_hbm, rate_hbm, skip_hbm, points_hbm, label_hbm, out_ref, mark_ref, dt_ref, columns_ref, points_ref,
    bias_ref, rate_ref, skip_ref, spot_ref, label_ref, sems,
):
    n = xbc_hbm.shape[1]
    width = xbc_hbm.shape[2]
    rows = xbc_hbm.at[0, pl.ds(n - EDGE, EDGE)]
    fetch(
        (
            (dt_hbm, dt_ref), (rows, out_ref.at[:, pl.ds(0, width)]), (label_hbm, label_ref), (points_hbm, spot_ref),
            (bias_hbm, bias_ref.at[0]), (rate_hbm, rate_ref.at[0]), (skip_hbm, skip_ref.at[0]),
        ),
        sems,
    )
    mark_ref[...] = jnp.zeros(mark_ref.shape, F32) + label_ref[0].astype(F32)
    steps = jnp.concatenate([dt_ref[0].astype(F32), jnp.zeros((-H % EDGE, n), F32)], axis=0).astype(BF16)
    for i in range(-(-H // EDGE)):
        out_ref[:, width + i * n : width + (i + 1) * n] = steps[i * EDGE : (i + 1) * EDGE]
    columns_ref[...] = turned((bias_ref[...], rate_ref[...], skip_ref[...]))
    spot = lax.broadcasted_iota(jnp.int32, points_ref.shape, 0)
    points = jnp.zeros(points_ref.shape, jnp.int32)
    for r in range(R):
        points = jnp.where(spot == r, spot_ref[0, r], points)
    points_ref[...] = points


def steps_kernel(own_ref, other_ref, columns_ref, points_ref, ws_ref, wr_ref, e_ref, rows_ref, small_ref):
    place = lax.axis_index("seq")
    core = lax.rem(place, 2)
    n = own_ref.shape[2]
    own = own_ref[0].astype(F32)
    other = other_ref[0].astype(F32)
    bias, rate, skip = columns_ref[:, 0:1], columns_ref[:, 1:2], columns_ref[:, 2:3]
    first = core == 0
    dts = [step_sizes(jnp.where(first == (block == 0), own, other), bias) for block in range(2)]
    cums = running_sums([-rate * dt for dt in dts])
    ends = [cum[:, n - 1 : n] for cum in cums]
    for block in range(2):
        ws_ref[block * n : (block + 1) * n] = pack(dts[block] * jnp.exp(ends[block] - cums[block]))
    total = [cums[0], ends[0] + cums[1]]
    index = lax.broadcasted_iota(jnp.int32, (H, n), 1)
    weight = [jnp.zeros((H, n), F32), jnp.zeros((H, n), F32)]
    found = read_levels(points_ref[...], (place - core) * n, total)
    for at, inside, level in found:
        for block in range(2):
            seen = jnp.where(index + block * n <= at, jnp.exp(jnp.minimum(level - total[block], 0.0)), 0.0)
            weight[block] += inside * seen
    for block in range(2):
        wr_ref[block * n : (block + 1) * n] = pack(weight[block] * dts[block] * (1.0 / R))
    e_ref[...] = pack(jnp.exp(jnp.where(first, cums[0], cums[1])))
    decay = [jnp.exp(end) for end in ends]
    back = jnp.exp(-jnp.where(first, ends[0], ends[1]))
    rows_ref[...] = pack(beside((decay[0], decay[1], skip, back)))[0:16]
    whole = beside((carry_of(found), jnp.exp(ends[0] + ends[1])))
    small_ref[...] = jnp.concatenate([whole, jnp.zeros((128 - H, 128), F32)], axis=0).T[0:8]


def later_kernel(same_ref, cross_ref, columns_ref, points_ref, later_ref):
    place = lax.axis_index("seq")
    core = lax.rem(place, 2)
    slabs = -(-H // EDGE)
    n = (same_ref.shape[1] - CH) // slabs

    def steps_of(ref):
        slab = [ref[:, CH + i * n : CH + (i + 1) * n].astype(F32) for i in range(slabs)]
        return jnp.concatenate(slab, axis=0)[:H]

    same, cross = steps_of(same_ref), steps_of(cross_ref)
    bias, rate = columns_ref[:, 0:1], columns_ref[:, 1:2]
    raws = [jnp.where((core == 0) == (block == 0), same, cross) for block in range(2)]
    cums = running_sums([-rate * step_sizes(raw, bias) for raw in raws])
    total = [cums[0], cums[0][:, n - 1 : n] + cums[1]]
    carry = carry_of(read_levels(points_ref[...], 2 * n, total))
    later_ref[...] = pack(beside((jnp.where(place < 2, carry, 0.0),)))[0:16]


def state_kernel(
    own_ref, other_ref, edge_a_ref, edge_b_ref, ws_ref, wr_ref, rows_ref, later_ref, conv_w_ref, conv_b_ref,
    state_ref, early_ref, act_own_ref, act_other_ref, bc_ref, *rest,
    split,
):
    reads = rest[:-6]
    x_ref, act_ref, taps_ref, bias_ref, read_ref, sems = rest[-6:]
    place = lax.axis_index("seq")
    core = lax.rem(place, 2)
    n = own_ref.shape[1]
    col = pl.multiple_of(core * HALF, 128)
    copies = []
    for i, (source, to) in enumerate(((own_ref, core), (other_ref, 1 - core))):
        rows = pl.ds(pl.multiple_of(EDGE + to * n, 16), n)
        copies.append(pltpu.make_async_copy(source.at[0, :, pl.ds(D, BC)], x_ref.at[rows, pl.ds(HALF, BC)], sems.at[2 * i]))
        copies.append(pltpu.make_async_copy(source.at[0, :, pl.ds(col, HALF)], x_ref.at[rows, pl.ds(0, HALF)], sems.at[2 * i + 1]))
    for i, (source, from_at, to_at, width) in enumerate(((conv_w_ref, D, HALF, BC), (conv_w_ref, col, 0, HALF))):
        copies.append(pltpu.make_async_copy(source.at[:, pl.ds(from_at, width)], taps_ref.at[:, pl.ds(to_at, width)], sems.at[4 + i]))
    for i, (from_at, to_at, width) in enumerate(((D, HALF, BC), (col, 0, HALF))):
        copies.append(pltpu.make_async_copy(conv_b_ref.at[pl.ds(from_at, width)], bias_ref.at[0, pl.ds(to_at, width)], sems.at[6 + i]))
    for i in (0, 2, 4, 6, 1, 3, 5, 7):
        copies[i].start()
    started = jnp.where(place >= 2, 1.0, 0.0)
    edge = jnp.where(core == 0, edge_a_ref[:, :CH].astype(F32), edge_b_ref[:, :CH].astype(F32)) * started
    x_ref[0:EDGE, HALF:] = edge[:, D:].astype(BF16)

    @pl.when(core == 0)
    def _():
        x_ref[0:EDGE, :HALF] = edge[:, :HALF].astype(BF16)

    @pl.when(core == 1)
    def _():
        x_ref[0:EDGE, :HALF] = edge[:, HALF:D].astype(BF16)

    tile = 128

    def convolve(at):
        cols = pl.ds(at, CHUNK)
        taps = taps_ref[:, cols]
        bias = bias_ref[:, cols]
        for t in range(2 * n // tile):
            seen = x_ref[t * tile : (t + 1) * tile + EDGE, cols].astype(F32)
            before = pltpu.roll(seen, 1, 0)
            pair = taps[1:2] * seen + taps[0:1] * before
            total = bias + taps[3:4] * seen[EDGE:] + taps[2:3] * before[EDGE:]
            total += pltpu.roll(pair, 2, 0)[EDGE:]
            act_ref[t * tile : (t + 1) * tile, cols] = silu(total).astype(BF16)

    for i in (0, 2, 4, 6):
        copies[i].wait()
    convolve(HALF)
    b_turned = act_ref[:, HALF : HALF + N].astype(F32).T.astype(BF16)
    for i in (1, 3, 5, 7):
        copies[i].wait()

    @pl.loop(0, HALF // CHUNK)
    def _(j):
        at = pl.multiple_of(j * CHUNK, CHUNK)
        cols = pl.ds(at, CHUNK)
        convolve(at)
        spread = spread_matrix(core * (H // 2) + j * (CHUNK // P_SIZE))
        table = dot(rows_ref[...], spread)
        ahead = dot(later_ref[...], spread)[0:1]
        act = act_ref[:, cols].astype(F32)
        weighted = (act * dot(ws_ref[...], spread)).astype(BF16)
        early = dot(b_turned[:, :n], weighted[:n])
        late = dot(b_turned[:, n:], weighted[n:])
        state = table[1:2] * early + late
        early_ref[:, cols] = early.astype(BF16)
        state_ref[:, cols] = state.astype(BF16)
        read = act * dot(wr_ref[...], spread)
        high = read.astype(BF16)
        low = (read - high.astype(F32)).astype(BF16)
        seen = dot(b_turned, high) + dot(b_turned, low) + ahead * state
        read_ref[pl.ds(at, CHUNK)] = seen.T

    if split:
        part = D // 16
        x_bit = lax.rem(lax.axis_index("dp"), 2)
        z_bit = lax.rem(lax.axis_index("dp") // 2, 2)

        def rows(z, x, y):
            return read_ref[pl.ds(pl.multiple_of((4 * z + 2 * x + y) * part, 8), part)]

        for q in range(2):
            here = slice(q * part, (q + 1) * part)
            reads[0][here] = rows(q, x_bit, 0)
            reads[1][here] = rows(q, 1 - x_bit, 0)
            reads[2][here] = rows(z_bit, q, 1)
            reads[3][here] = rows(1 - z_bit, q, 1)
    else:
        reads[0][...] = read_ref[...]
    mine = pl.ds(pl.multiple_of(core * n, 16), n)
    act_own_ref[...] = act_ref[mine, :HALF]
    bc_ref[...] = act_ref[mine, HALF:]
    act_other_ref[...] = act_ref[pl.ds(pl.multiple_of((1 - core) * n, 16), n), :HALF]


def diagonal_kernel(act_own_ref, act_other_ref, bc_ref, ws_ref, e_ref, rows_ref, gate_ref, near_ref, far_ref):
    core = lax.rem(lax.axis_index("seq"), 2)
    n = act_own_ref.shape[0]
    scores = lax.dot_general(bc_ref[:, N:], bc_ref[:, :N], (((1,), (1,)), ((), ())), preferred_element_type=F32)
    row = lax.broadcasted_iota(jnp.int32, (n, n), 0)
    lane = lax.broadcasted_iota(jnp.int32, (n, n), 1)
    masked = jnp.where(row >= lane, scores, 0.0).astype(BF16)
    ws = ws_ref[pl.ds(pl.multiple_of(core * n, 16), n)]
    for side, source in enumerate((act_own_ref, act_other_ref)):
        half = core if side == 0 else 1 - core

        @pl.loop(0, HALF // CHUNK)
        def _(j):
            at = pl.multiple_of(j * CHUNK, CHUNK)
            cols = pl.ds(at, CHUNK)
            spread = spread_matrix(half * (H // 2) + j * (CHUNK // P_SIZE))
            act = source[:, cols].astype(F32)
            weighted = (act * dot(ws, spread)).astype(BF16)
            table = dot(rows_ref[...], spread)
            decay = dot(e_ref[...], spread)
            value = decay * (table[3:4] * dot(masked, weighted)) + table[2:3] * act
            gate = silu(gate_ref[0, :, pl.ds(pl.multiple_of(half * HALF + at, CHUNK), CHUNK)].astype(F32))
            near_ref[side, :, cols] = value * gate
            far_ref[side, :, cols] = decay * gate


def finish_kernel(near_ref, far_ref, bc_ref, h_own_ref, h_other_ref, early_own_ref, early_other_ref, rows_ref, gain_hbm, out_ref, g_ref, gain_ref, sem):
    place = lax.axis_index("seq")
    core = lax.rem(place, 2)
    n = bc_ref.shape[0]
    second = core == 1
    started = place >= 2
    gain = pltpu.make_async_copy(gain_hbm, gain_ref.at[0], sem)
    gain.start()
    squares = jnp.zeros((n, CHUNK), F32)
    c_vals = bc_ref[:, N:]
    for side in range(2):
        half = core if side == 0 else 1 - core
        h_ref = (h_own_ref, h_other_ref)[side]
        early_ref = (early_own_ref, early_other_ref)[side]
        for j in range(HALF // CHUNK):
            cols = pl.ds(j * CHUNK, CHUNK)
            spread = spread_matrix(half * (H // 2) + j * (CHUNK // P_SIZE))
            decay = jnp.where(second, dot(rows_ref[...], spread)[0:1], 1.0)
            h = jnp.where(started, h_ref[:, cols].astype(F32), 0.0) * decay
            h += jnp.where(second, early_ref[:, cols].astype(F32), 0.0)
            g = near_ref[side, :, cols] + far_ref[side, :, cols] * dot(c_vals, h.astype(BF16))
            g_ref[side, :, cols] = g
            squares += g * g
    gain.wait()
    scale = lax.rsqrt(jnp.sum(squares, axis=-1, keepdims=True) * (1.0 / D) + 1e-05)
    for side in range(2):
        half = core if side == 0 else 1 - core
        for j in range(HALF // CHUNK):
            cols = pl.ds(pl.multiple_of(half * HALF + j * CHUNK, CHUNK), CHUNK)
            g = g_ref[side, :, pl.ds(j * CHUNK, CHUNK)]
            out_ref[0, :, cols] = (g * scale * gain_ref[:, cols]).astype(BF16)


def join_kernel(mark_ref, a_ref, b_ref, out_ref):
    row = lax.broadcasted_iota(jnp.int32, out_ref.shape, 0)
    out_ref[...] = jnp.where(row == 0, a_ref[...] + b_ref[...], mark_ref[...])


def join(mark, a, b):
    out = jax.ShapeDtypeStruct(a.shape, a.dtype)
    return pl.pallas_call(
        join_kernel, out_shape=out, in_specs=[VMEM] * 3, out_specs=VMEM, compiler_params=params(8), name="join"
    )(mark, a, b)


def halves_kernel(
    kept_x_ref, came_x_ref, kept_z_ref, came_z_ref, mark_ref, x_mark_ref, z_mark_ref, sum_ref,
    keep_a_ref, send_a_ref, keep_b_ref, send_b_ref,
    *, sequences,
):
    ones = sum_ref[0:1] + x_mark_ref[0:1]

    def weight(mark):
        return mark / ones - (1.0 - mark) / (sequences - ones)

    own = weight(mark_ref[1:2])
    part = keep_a_ref.shape[0]
    place = lax.axis_index("dp")
    x_bit = lax.rem(place, 2)
    z_bit = lax.rem(place // 2, 2)
    work = (
        (kept_x_ref, came_x_ref, x_mark_ref, z_bit, keep_a_ref, send_a_ref),
        (kept_z_ref, came_z_ref, z_mark_ref, x_bit, keep_b_ref, send_b_ref),
    )
    for kept, came, other_mark, bit, keep, send in work:
        other = weight(other_mark[1:2])
        mine = pl.ds(pl.multiple_of(bit * part, 8), part)
        yours = pl.ds(pl.multiple_of((1 - bit) * part, 8), part)
        send[...] = own * kept[yours] + other * came[yours]
        keep[...] = own * kept[mine] + other * came[mine]


def join_y_kernel(keep_a_ref, came_a_ref, keep_b_ref, came_b_ref, keep_ref, send_ref):
    first = lax.rem(lax.axis_index("seq") // 2, 2) == 0
    a = keep_a_ref[...] + came_a_ref[...]
    b = keep_b_ref[...] + came_b_ref[...]
    keep_ref[...] = jnp.where(first, a, b)
    send_ref[...] = jnp.where(first, b, a)


def last_kernel(kept_ref, came_ref, sum_ref):
    sum_ref[...] = kept_ref[...] + came_ref[...]


def core_kernel(kept_ref, came_ref, own_ref, send_ref):
    part = own_ref.shape[0]
    zero = kept_ref[0:part] + came_ref[0:part]
    one = kept_ref[part:] + came_ref[part:]
    first = lax.rem(lax.axis_index("seq"), 2) == 0
    own_ref[...] = jnp.where(first, zero, one)
    send_ref[...] = jnp.where(first, one, zero)


def owner_kernel(own_ref, came_ref, out_ref):
    z_bit = lax.rem(lax.axis_index("dp") // 4, 2)
    out_ref[...] = jnp.where(z_bit == lax.rem(lax.axis_index("seq"), 2), own_ref[...], came_ref[...])


def swap(k):
    return [(i, i ^ k) for i in range(8)]


def small_call(kernel, name, count, rows, *args):
    part = jax.ShapeDtypeStruct((rows, N), F32)
    return pl.pallas_call(
        kernel, out_shape=(part,) * count, in_specs=[VMEM] * len(args), out_specs=(VMEM,) * count, compiler_params=params(8), name=name
    )(*args)


def on_device(xbc, gate_input, dt_raw, conv_weight, conv_bias, dt_bias, a_rate, d_skip, norm_gain, labels, readout):
    n = xbc.shape[1]
    places = lax.axis_size("seq")
    sequences = lax.axis_size("dp")
    chips = places // 2
    place = lax.axis_index("seq")
    core = place % 2
    split = sequences == 8 and places == 4
    pair = [(i, i ^ 1) for i in range(places)]
    shape = jax.ShapeDtypeStruct

    one_back = [(i, i ^ 3) for i in range(4)] if chips == 2 else [(i, (i + 1) % places) for i in range(places)]
    two_back = [(i, (i + 2) % places) for i in range(places)]
    dt_turned = jnp.swapaxes(dt_raw, 1, 2)
    dt_other = lax.ppermute(dt_turned, "seq", pair)
    xbc_other = lax.ppermute(xbc, "seq", pair)
    xbc_here = in_hbm(xbc)
    tail, mark, dt_own, columns, points = pl.pallas_call(
        tail_kernel,
        out_shape=(
            shape((EDGE, CH + -(-H // EDGE) * n), BF16), shape((8, N), F32), shape((1, H, n), BF16),
            shape((H, 8), F32), shape((8, 128), jnp.int32),
        ),
        in_specs=[HBM] * 7,
        out_specs=(VMEM,) * 5,
        scratch_shapes=[pltpu.VMEM((1, H), F32)] * 3
        + [pltpu.SMEM((1, R), jnp.int32), pltpu.SMEM((1,), jnp.int32), pltpu.SemaphoreType.DMA((7,))],
        compiler_params=params(8),
        name="tail",
    )(xbc_here, in_hbm(dt_turned), in_hbm(dt_bias), in_hbm(a_rate), in_hbm(d_skip), in_hbm(readout), labels)
    edge_a = lax.ppermute(tail, "seq", one_back)
    edge_b = lax.ppermute(tail, "seq", two_back)

    ws, wr, e, rows, small = pl.pallas_call(
        steps_kernel,
        out_shape=(
            shape((2 * n, 128), BF16), shape((2 * n, 128), BF16), shape((n, 128), BF16), shape((16, 128), BF16), shape((8, 128), F32),
        ),
        in_specs=[VMEM] * 4,
        out_specs=(VMEM,) * 5,
        compiler_params=params(16),
        cost_estimate=cost(2 * 6 * n * n * 128, 8 * n * 256),
        name="steps",
    )(dt_own, dt_other, columns, points)

    if chips == 2:
        later = pl.pallas_call(
            later_kernel,
            out_shape=shape((16, 128), BF16),
            in_specs=[VMEM] * 4,
            out_specs=VMEM,
            compiler_params=params(16),
            cost_estimate=cost(2 * 6 * n * n * 128, 8 * n * 256),
            name="later",
        )(edge_b, edge_a, columns, points)
    else:
        later = jnp.zeros_like(small)
        for step in range(chips - 1):
            out = small.at[0:1].add(small[1:2] * later[0:1])
            later = lax.ppermute(out, "seq", [(i, (i - 2) % places) for i in range(places)])
            later = jnp.where(place < places - 2, later, 0.0)
        later = pack(jnp.broadcast_to(later[0, :H, None], (H, 16)))

    if split:
        z_mark = lax.ppermute(mark, "dp", swap(2))
        half = join(tied(mark, ws), mark, z_mark)
        quarter = join(tied(mark, later), half, lax.ppermute(half, "dp", swap(4)))
        later = tied(later, quarter)

    read_rows = D // 8 if split else HALF
    state, early, act_own, act_other, bc, *reads = pl.pallas_call(
        functools.partial(state_kernel, split=split),
        out_shape=(
            shape((N, HALF), BF16), shape((N, HALF), BF16),
            shape((n, HALF), BF16), shape((n, HALF), BF16), shape((n, BC), BF16),
        ) + (shape((read_rows, N), F32),) * (4 if split else 1),
        in_specs=[HBM, ANY] + [VMEM] * 6 + [HBM, HBM],
        out_specs=(VMEM,) * (9 if split else 6),
        scratch_shapes=[
            pltpu.VMEM((EDGE + 2 * n, SIDE), BF16),
            pltpu.VMEM((2 * n, SIDE), BF16),
            pltpu.VMEM((KW, SIDE), F32),
            pltpu.VMEM((1, SIDE), F32),
            pltpu.VMEM((HALF, N), F32),
            pltpu.SemaphoreType.DMA((8,)),
        ],
        compiler_params=params(24),
        cost_estimate=cost(50 * n * n * D, 4 * 2 * n * SIDE),
        name="states",
    )(xbc_here, xbc_other, edge_a, edge_b, ws, wr, rows, later, in_hbm(conv_weight), in_hbm(conv_bias))

    h = state
    for step in range(chips - 1):
        if step:
            scale = jnp.repeat(lax.dynamic_slice_in_dim(small[1, :H], core * (H // 2), H // 2), P_SIZE)
            h = (h.astype(F32) * scale + state.astype(F32)).astype(BF16)
        h = lax.ppermute(h, "seq", two_back)
        if chips > 2:
            h = jnp.where(place >= 2, h, jnp.zeros_like(h))
    act_in = lax.ppermute(act_other, "seq", pair)
    early_in = lax.ppermute(early, "seq", pair)
    if split:
        keep_x, send_x, keep_z, send_z = reads
        x_mark = lax.ppermute(tied(quarter, send_x), "dp", swap(1))
        came_x = lax.ppermute(send_x, "dp", swap(1))
        came_z = lax.ppermute(send_z, "dp", swap(2))

    near, reach = pl.pallas_call(
        diagonal_kernel,
        out_shape=(shape((2, n, HALF), F32), shape((2, n, HALF), F32)),
        in_specs=[VMEM] * 7,
        out_specs=(VMEM, VMEM),
        compiler_params=params(24),
        cost_estimate=cost(28 * n * n * D, 4 * n * D),
        name="diagonal",
    )(act_own, act_in, bc, ws, e, rows, gate_input)
    if split:
        keep_x, near, reach = lax.optimization_barrier((keep_x, near, reach))
        keep_a, send_a, keep_b, send_b = small_call(
            functools.partial(halves_kernel, sequences=float(sequences)), "halves", 4, D // 16,
            keep_x, came_x, keep_z, came_z, mark, x_mark, z_mark, quarter,
        )
        came_a = lax.ppermute(send_a, "dp", swap(2))
        came_b = lax.ppermute(send_b, "dp", swap(1))
        keep, send = small_call(join_y_kernel, "join_y", 2, D // 16, keep_a, came_a, keep_b, came_b)
        came = lax.ppermute(send, "seq", [(i, i ^ 2) for i in range(places)])
    h = tied(h, keep) if split else h
    h_other = lax.ppermute(h, "seq", pair)
    layer_out = pl.pallas_call(
        finish_kernel,
        out_shape=shape((1, n, D), BF16),
        in_specs=[VMEM] * 8 + [ANY],
        out_specs=VMEM,
        scratch_shapes=[pltpu.VMEM((2, n, HALF), F32), pltpu.VMEM((1, D), F32), pltpu.SemaphoreType.DMA(())],
        compiler_params=params(24),
        cost_estimate=cost(20 * n * n * D, 12 * n * D),
        name="finish",
    )(near, reach, bc, h, h_other, early, early_in, rows, norm_gain)
    if split:
        (total,) = small_call(last_kernel, "last_y", 1, D // 16, keep, came)
        came = lax.ppermute(total, "dp", swap(4))
        total, layer_out = lax.optimization_barrier((total, layer_out))
        own, send = small_call(core_kernel, "cores", 2, D // 32, total, came)
        came = lax.ppermute(send, "seq", pair)
        steering = small_call(owner_kernel, "owner", 1, D // 32, own, came)[0]
    else:
        ones = lax.psum(mark[0, 0], "dp")
        weight = mark[0, 0] / ones - (1.0 - mark[0, 0]) / (sequences - ones)
        whole = lax.dynamic_update_slice_in_dim(jnp.zeros((D, N), F32), weight * reads[0], core * HALF, 0)
        steering = lax.psum_scatter(whole, ("dp", "seq"), scatter_dimension=0, tiled=True)
    return (layer_out, steering)


def solution(mesh):
    return jax.shard_map(
        on_device,
        mesh=mesh,
        in_specs=(
            P("dp", "seq", None),
            P("dp", "seq", None),
            P("dp", "seq", None),
            P(),
            P(),
            P(),
            P(),
            P(),
            P(),
            P("dp"),
            P("dp", None),
        ),
        out_specs=(P("dp", "seq", None), P(("dp", "seq"), None)),
        check_vma=False,
    )
```

```python
import functools

import jax
import jax.numpy as jnp
from jax import lax
from jax.experimental import pallas as pl
from jax.experimental.pallas import tpu as pltpu
from jax.sharding import PartitionSpec as P

H = 40
P_SIZE = 64
N = 128
KW = 4
R = 4
D = H * P_SIZE
HALF = D // 2
BC = 2 * N
SIDE = HALF + BC
CH = D + BC
CHUNK = 256
EDGE = 16
F32 = jnp.float32
BF16 = jnp.bfloat16
VMEM = pl.BlockSpec(memory_space=pltpu.VMEM)
SMEM = pl.BlockSpec(memory_space=pltpu.SMEM)
ANY = pl.BlockSpec(memory_space=pl.ANY)
HBM = pl.BlockSpec(memory_space=pltpu.HBM)
MIB = 1024 * 1024


def params(mib):
    return pltpu.CompilerParams(vmem_limit_bytes=mib * MIB)


def cost(flops, read):
    return pl.CostEstimate(flops=flops, bytes_accessed=read, transcendentals=0)


def in_hbm(x):
    return pltpu.with_memory_space_constraint(x, pltpu.HBM)


def tied(x, *others):
    return lax.optimization_barrier((x,) + others)[0]


def dot(a, b):
    return jnp.dot(a, b, preferred_element_type=F32)


def pack(w):
    high = w.astype(BF16).astype(F32)
    gap = jnp.zeros((64 - H, w.shape[1]), F32)
    return jnp.concatenate([high, gap, w - high, gap], axis=0).T.astype(BF16)


def beside(columns):
    lane = lax.broadcasted_iota(jnp.int32, (H, 128), 1)
    table = jnp.zeros((H, 128), F32)
    for i, column in enumerate(columns):
        table = jnp.where(lane == i, column, table)
    return table


def turned(rows):
    table = jnp.concatenate(list(rows) + [jnp.zeros((8 - len(rows), H), F32)], axis=0)
    return jnp.concatenate([table, jnp.zeros((8, 128 - H), F32)], axis=1).T[:H]


def spread_matrix(first_head):
    row = lax.broadcasted_iota(jnp.int32, (128, CHUNK), 0)
    lane = lax.broadcasted_iota(jnp.int32, (128, CHUNK), 1)
    hit = (row & 63) == first_head + lane // P_SIZE
    return jnp.where(hit, 1.0, 0.0).astype(BF16)


def silu(v):
    half = 0.5 * v
    return half + half * jnp.tanh(half)


def fetch(pairs, sems):
    copies = [pltpu.make_async_copy(source, to, sems.at[i]) for i, (source, to) in enumerate(pairs)]
    for copy in copies:
        copy.start()
    for copy in copies:
        copy.wait()


def step_sizes(raw, bias):
    raw = raw + bias
    return jnp.maximum(raw, 0.0) + jnp.log1p(jnp.exp(-jnp.abs(raw)))


def running_sums(steps):
    n = steps[0].shape[1]
    row = lax.broadcasted_iota(jnp.int32, (n, n), 0)
    lane = lax.broadcasted_iota(jnp.int32, (n, n), 1)
    upper = jnp.where(row <= lane, 1.0, 0.0).astype(BF16)
    parts = []
    for step in steps:
        high = step.astype(BF16).astype(F32)
        middle = (step - high).astype(BF16).astype(F32)
        parts += [high, middle, step - high - middle]
    sums = dot(jnp.concatenate(parts, axis=0).astype(BF16), upper)
    return [sums[i : i + H] + (sums[i + H : i + 2 * H] + sums[i + 2 * H : i + 3 * H]) for i in range(0, 3 * H * len(steps), 3 * H)]


def read_levels(points, base, total):
    n = total[0].shape[1]
    index = lax.broadcasted_iota(jnp.int32, (H, n), 1)
    found = []
    for r in range(R):
        at = points[r : r + 1, 0:1] - base
        inside = jnp.where((at >= 0) & (at < 2 * n), 1.0, 0.0)
        level = jnp.zeros((H, n), F32)
        for block in range(2):
            level += jnp.where(index + block * n == at, total[block], 0.0)
        found.append((at, inside, jnp.sum(level, axis=1, keepdims=True)))
    return found


def carry_of(found):
    carry = jnp.zeros((H, 1), F32)
    for _, inside, level in found:
        carry += inside * jnp.exp(level)
    return carry * (1.0 / R)


def tail_kernel(
    xbc_hbm, dt_hbm, bias_hbm, rate_hbm, skip_hbm, points_hbm, label_hbm, out_ref, mark_ref, dt_ref, columns_ref, points_ref,
    bias_ref, rate_ref, skip_ref, spot_ref, label_ref, sems,
):
    n = xbc_hbm.shape[1]
    width = xbc_hbm.shape[2]
    rows = xbc_hbm.at[0, pl.ds(n - EDGE, EDGE)]
    fetch(
        (
            (dt_hbm, dt_ref), (rows, out_ref.at[:, pl.ds(0, width)]), (label_hbm, label_ref), (points_hbm, spot_ref),
            (bias_hbm, bias_ref.at[0]), (rate_hbm, rate_ref.at[0]), (skip_hbm, skip_ref.at[0]),
        ),
        sems,
    )
    mark_ref[...] = jnp.zeros(mark_ref.shape, F32) + label_ref[0].astype(F32)
    steps = jnp.concatenate([dt_ref[0].astype(F32), jnp.zeros((-H % EDGE, n), F32)], axis=0).astype(BF16)
    for i in range(-(-H // EDGE)):
        out_ref[:, width + i * n : width + (i + 1) * n] = steps[i * EDGE : (i + 1) * EDGE]
    columns_ref[...] = turned((bias_ref[...], rate_ref[...], skip_ref[...]))
    spot = lax.broadcasted_iota(jnp.int32, points_ref.shape, 0)
    points = jnp.zeros(points_ref.shape, jnp.int32)
    for r in range(R):
        points = jnp.where(spot == r, spot_ref[0, r], points)
    points_ref[...] = points


def steps_kernel(
    own_ref, other_ref, columns_ref, points_ref, xbc_hbm, xbc_other_ref, conv_w_hbm, conv_b_hbm,
    ws_ref, wr_ref, e_ref, rows_ref, small_ref, x_ref, taps_ref, bias_ref, sems,
):
    place = lax.axis_index("seq")
    core = lax.rem(place, 2)
    n = own_ref.shape[2]
    col = pl.multiple_of(core * HALF, 128)
    copies = []
    for from_at, to_at, width in ((D, HALF, BC), (col, 0, HALF)):
        here, there = pl.ds(from_at, width), pl.ds(to_at, width)
        for source, to in ((xbc_hbm, core), (xbc_other_ref, 1 - core)):
            copies.append((source.at[0, :, here], x_ref.at[pl.ds(pl.multiple_of(to * n, 16), n), there]))
        copies.append((conv_w_hbm.at[:, here], taps_ref.at[:, there]))
        copies.append((conv_b_hbm.at[here], bias_ref.at[0, there]))
    copies = [pltpu.make_async_copy(source, to, sems.at[i]) for i, (source, to) in enumerate(copies)]
    for copy in copies:
        copy.start()
    own = own_ref[0].astype(F32)
    other = other_ref[0].astype(F32)
    bias, rate, skip = columns_ref[:, 0:1], columns_ref[:, 1:2], columns_ref[:, 2:3]
    first = core == 0
    dts = [step_sizes(jnp.where(first == (block == 0), own, other), bias) for block in range(2)]
    cums = running_sums([-rate * dt for dt in dts])
    ends = [cum[:, n - 1 : n] for cum in cums]
    for block in range(2):
        ws_ref[block * n : (block + 1) * n] = pack(dts[block] * jnp.exp(ends[block] - cums[block]))
    total = [cums[0], ends[0] + cums[1]]
    index = lax.broadcasted_iota(jnp.int32, (H, n), 1)
    weight = [jnp.zeros((H, n), F32), jnp.zeros((H, n), F32)]
    found = read_levels(points_ref[...], (place - core) * n, total)
    for at, inside, level in found:
        for block in range(2):
            seen = jnp.where(index + block * n <= at, jnp.exp(jnp.minimum(level - total[block], 0.0)), 0.0)
            weight[block] += inside * seen
    for block in range(2):
        wr_ref[block * n : (block + 1) * n] = pack(weight[block] * dts[block] * (1.0 / R))
    e_ref[...] = pack(jnp.exp(jnp.where(first, cums[0], cums[1])))
    decay = [jnp.exp(end) for end in ends]
    back = jnp.exp(-jnp.where(first, ends[0], ends[1]))
    rows_ref[...] = pack(beside((decay[0], decay[1], skip, back)))[0:16]
    whole = beside((carry_of(found), jnp.exp(ends[0] + ends[1])))
    small_ref[...] = jnp.concatenate([whole, jnp.zeros((128 - H, 128), F32)], axis=0).T[0:8]
    for copy in copies:
        copy.wait()


def later_kernel(same_ref, cross_ref, columns_ref, points_ref, later_ref):
    place = lax.axis_index("seq")
    core = lax.rem(place, 2)
    slabs = -(-H // EDGE)
    n = (same_ref.shape[1] - CH) // slabs

    def steps_of(ref):
        slab = [ref[:, CH + i * n : CH + (i + 1) * n].astype(F32) for i in range(slabs)]
        return jnp.concatenate(slab, axis=0)[:H]

    same, cross = steps_of(same_ref), steps_of(cross_ref)
    bias, rate = columns_ref[:, 0:1], columns_ref[:, 1:2]
    raws = [jnp.where((core == 0) == (block == 0), same, cross) for block in range(2)]
    cums = running_sums([-rate * step_sizes(raw, bias) for raw in raws])
    total = [cums[0], cums[0][:, n - 1 : n] + cums[1]]
    carry = carry_of(read_levels(points_ref[...], 2 * n, total))
    later_ref[...] = pack(beside((jnp.where(place < 2, carry, 0.0),)))[0:16]


def state_kernel(
    x_ref, edge_a_ref, edge_b_ref, ws_ref, wr_ref, rows_ref, later_ref, taps_ref, bias_ref,
    state_ref, early_ref, act_own_ref, act_other_ref, bc_ref, *rest,
    split,
):
    reads = rest[:-3]
    edge_ref, act_ref, read_ref = rest[-3:]
    place = lax.axis_index("seq")
    core = lax.rem(place, 2)
    n = x_ref.shape[0] // 2
    started = jnp.where(place >= 2, 1.0, 0.0)
    edge = jnp.where(core == 0, edge_a_ref[:, :CH].astype(F32), edge_b_ref[:, :CH].astype(F32)) * started
    edge_ref[:, HALF:] = edge[:, D:].astype(BF16)
    edge_ref[:, :HALF] = jnp.where(core == 0, edge[:, :HALF], edge[:, HALF:D]).astype(BF16)
    tile = 128

    def convolve(at):
        cols = pl.ds(at, CHUNK)
        taps = taps_ref[:, cols]
        bias = bias_ref[:, cols]
        for t in range(2 * n // tile):
            if t == 0:
                seen = jnp.concatenate([edge_ref[:, cols], x_ref[:tile, cols]], axis=0).astype(F32)
            else:
                seen = x_ref[t * tile - EDGE : (t + 1) * tile, cols].astype(F32)
            before = pltpu.roll(seen, 1, 0)
            pair = taps[1:2] * seen + taps[0:1] * before
            total = bias + taps[3:4] * seen[EDGE:] + taps[2:3] * before[EDGE:]
            total += pltpu.roll(pair, 2, 0)[EDGE:]
            act_ref[t * tile : (t + 1) * tile, cols] = silu(total).astype(BF16)

    convolve(HALF)
    b_turned = act_ref[:, HALF : HALF + N].astype(F32).T.astype(BF16)
    @pl.loop(0, HALF // CHUNK, unroll=True)
    def _(j):
        at = pl.multiple_of(j * CHUNK, CHUNK)
        cols = pl.ds(at, CHUNK)
        convolve(at)
        spread = spread_matrix(core * (H // 2) + j * (CHUNK // P_SIZE))
        table = dot(rows_ref[...], spread)
        ahead = dot(later_ref[...], spread)[0:1]
        act = act_ref[:, cols].astype(F32)
        weighted = (act * dot(ws_ref[...], spread)).astype(BF16)
        early = dot(b_turned[:, :n], weighted[:n])
        late = dot(b_turned[:, n:], weighted[n:])
        state = table[1:2] * early + late
        early_ref[:, cols] = early.astype(BF16)
        state_ref[:, cols] = state.astype(BF16)
        read = act * dot(wr_ref[...], spread)
        high = read.astype(BF16)
        low = (read - high.astype(F32)).astype(BF16)
        seen = dot(b_turned, high) + dot(b_turned, low) + ahead * state
        read_ref[pl.ds(at, CHUNK)] = seen.T

    if split:
        part = D // 16
        x_bit = lax.rem(lax.axis_index("dp"), 2)
        z_bit = lax.rem(lax.axis_index("dp") // 2, 2)

        def rows(z, x, y):
            return read_ref[pl.ds(pl.multiple_of((4 * z + 2 * x + y) * part, 8), part)]

        for q in range(2):
            here = slice(q * part, (q + 1) * part)
            reads[0][here] = rows(q, x_bit, 0)
            reads[1][here] = rows(q, 1 - x_bit, 0)
            reads[2][here] = rows(z_bit, q, 1)
            reads[3][here] = rows(1 - z_bit, q, 1)
    else:
        reads[0][...] = read_ref[...]
    mine = pl.ds(pl.multiple_of(core * n, 16), n)
    act_own_ref[...] = act_ref[mine, :HALF]
    bc_ref[...] = act_ref[mine, HALF:]
    act_other_ref[...] = act_ref[pl.ds(pl.multiple_of((1 - core) * n, 16), n), :HALF]


def diagonal_kernel(act_own_ref, act_other_ref, bc_ref, ws_ref, e_ref, rows_ref, gate_ref, near_ref, far_ref):
    core = lax.rem(lax.axis_index("seq"), 2)
    n = act_own_ref.shape[0]
    scores = lax.dot_general(bc_ref[:, N:], bc_ref[:, :N], (((1,), (1,)), ((), ())), preferred_element_type=F32)
    row = lax.broadcasted_iota(jnp.int32, (n, n), 0)
    lane = lax.broadcasted_iota(jnp.int32, (n, n), 1)
    masked = jnp.where(row >= lane, scores, 0.0).astype(BF16)
    ws = ws_ref[pl.ds(pl.multiple_of(core * n, 16), n)]
    for side, source in enumerate((act_own_ref, act_other_ref)):
        half = core if side == 0 else 1 - core

        @pl.loop(0, HALF // CHUNK, unroll=True)
        def _(j):
            at = pl.multiple_of(j * CHUNK, CHUNK)
            cols = pl.ds(at, CHUNK)
            spread = spread_matrix(half * (H // 2) + j * (CHUNK // P_SIZE))
            act = source[:, cols].astype(F32)
            weighted = (act * dot(ws, spread)).astype(BF16)
            table = dot(rows_ref[...], spread)
            decay = dot(e_ref[...], spread)
            value = decay * (table[3:4] * dot(masked, weighted)) + table[2:3] * act
            gate = silu(gate_ref[0, :, pl.ds(pl.multiple_of(half * HALF + at, CHUNK), CHUNK)].astype(F32))
            near_ref[side, :, cols] = value * gate
            far_ref[side, :, cols] = decay * gate


def carry_kernel(h_ref, early_ref, rows_ref, keep_ref, send_ref):
    place = lax.axis_index("seq")
    first = lax.rem(place, 2) == 0
    for j in range(HALF // CHUNK):
        cols = pl.ds(j * CHUNK, CHUNK)
        spread = spread_matrix(lax.rem(place, 2) * (H // 2) + j * (CHUNK // P_SIZE))
        chip = jnp.where(place >= 2, h_ref[:, cols].astype(F32), 0.0)
        middle = dot(rows_ref[...], spread)[0:1] * chip + early_ref[:, cols].astype(F32)
        keep_ref[:, cols] = jnp.where(first, chip, middle).astype(BF16)
        send_ref[:, cols] = jnp.where(first, middle, chip).astype(BF16)


def finish_kernel(near_ref, far_ref, bc_ref, h_own_ref, h_other_ref, gain_ref, out_hbm, g_ref, out_ref, sems):
    core = lax.rem(lax.axis_index("seq"), 2)
    n = bc_ref.shape[0]
    squares = jnp.zeros((n, CHUNK), F32)
    c_vals = bc_ref[:, N:]
    for side in range(2):
        h_ref = (h_own_ref, h_other_ref)[side]
        for j in range(HALF // CHUNK):
            cols = pl.ds(j * CHUNK, CHUNK)
            g = near_ref[side, :, cols] + far_ref[side, :, cols] * dot(c_vals, h_ref[:, cols])
            g_ref[side, :, cols] = g
            squares += g * g
    scale = lax.rsqrt(jnp.sum(squares, axis=-1, keepdims=True) * (1.0 / D) + 1e-05)
    tile = n // 4
    copies = []
    for t in range(4):
        rows = pl.ds(t * tile, tile)
        for side in range(2):
            half = core if side == 0 else 1 - core
            for j in range(HALF // CHUNK):
                cols = pl.ds(pl.multiple_of(half * HALF + j * CHUNK, CHUNK), CHUNK)
                g = g_ref[side, rows, pl.ds(j * CHUNK, CHUNK)]
                out_ref[rows, cols] = (g * scale[t * tile : (t + 1) * tile] * gain_ref[:, cols]).astype(BF16)
        copies.append(pltpu.make_async_copy(out_ref.at[rows], out_hbm.at[0, rows], sems.at[t]))
        copies[t].start()
    for copy in copies:
        copy.wait()


def join_kernel(mark_ref, a_ref, b_ref, out_ref):
    row = lax.broadcasted_iota(jnp.int32, out_ref.shape, 0)
    out_ref[...] = jnp.where(row == 0, a_ref[...] + b_ref[...], mark_ref[...])


def join(mark, a, b):
    out = jax.ShapeDtypeStruct(a.shape, a.dtype)
    return pl.pallas_call(
        join_kernel, out_shape=out, in_specs=[VMEM] * 3, out_specs=VMEM, compiler_params=params(8), name="join"
    )(mark, a, b)


def halves_kernel(
    kept_x_ref, came_x_ref, kept_z_ref, came_z_ref, mark_ref, x_mark_ref, z_mark_ref, sum_ref,
    keep_a_ref, send_a_ref, keep_b_ref, send_b_ref,
    *, sequences,
):
    ones = sum_ref[0:1] + z_mark_ref[0:1]

    def weight(mark):
        return mark / ones - (1.0 - mark) / (sequences - ones)

    own = weight(mark_ref[1:2])
    part = keep_a_ref.shape[0]
    place = lax.axis_index("dp")
    x_bit = lax.rem(place, 2)
    z_bit = lax.rem(place // 2, 2)
    work = (
        (kept_x_ref, came_x_ref, x_mark_ref, z_bit, keep_a_ref, send_a_ref),
        (kept_z_ref, came_z_ref, z_mark_ref, x_bit, keep_b_ref, send_b_ref),
    )
    for kept, came, other_mark, bit, keep, send in work:
        other = weight(other_mark[1:2])
        mine = pl.ds(pl.multiple_of(bit * part, 8), part)
        yours = pl.ds(pl.multiple_of((1 - bit) * part, 8), part)
        send[...] = own * kept[yours] + other * came[yours]
        keep[...] = own * kept[mine] + other * came[mine]


def join_y_kernel(keep_a_ref, came_a_ref, keep_b_ref, came_b_ref, keep_ref, send_ref):
    first = lax.rem(lax.axis_index("seq") // 2, 2) == 0
    a = keep_a_ref[...] + came_a_ref[...]
    b = keep_b_ref[...] + came_b_ref[...]
    keep_ref[...] = jnp.where(first, a, b)
    send_ref[...] = jnp.where(first, b, a)


def last_kernel(kept_ref, came_ref, sum_ref):
    sum_ref[...] = kept_ref[...] + came_ref[...]


def core_kernel(kept_ref, came_ref, own_ref, send_ref):
    part = own_ref.shape[0]
    zero = kept_ref[0:part] + came_ref[0:part]
    one = kept_ref[part:] + came_ref[part:]
    first = lax.rem(lax.axis_index("seq"), 2) == 0
    own_ref[...] = jnp.where(first, zero, one)
    send_ref[...] = jnp.where(first, one, zero)


def owner_kernel(own_ref, came_ref, out_ref):
    z_bit = lax.rem(lax.axis_index("dp") // 4, 2)
    out_ref[...] = jnp.where(z_bit == lax.rem(lax.axis_index("seq"), 2), own_ref[...], came_ref[...])


def swap(k):
    return [(i, i ^ k) for i in range(8)]


def small_call(kernel, name, count, rows, *args):
    part = jax.ShapeDtypeStruct((rows, N), F32)
    return pl.pallas_call(
        kernel, out_shape=(part,) * count, in_specs=[VMEM] * len(args), out_specs=(VMEM,) * count, compiler_params=params(8), name=name
    )(*args)


def on_device(xbc, gate_input, dt_raw, conv_weight, conv_bias, dt_bias, a_rate, d_skip, norm_gain, labels, readout):
    n = xbc.shape[1]
    places = lax.axis_size("seq")
    sequences = lax.axis_size("dp")
    chips = places // 2
    place = lax.axis_index("seq")
    core = place % 2
    split = sequences == 8 and places == 4
    pair = [(i, i ^ 1) for i in range(places)]
    shape = jax.ShapeDtypeStruct

    one_back = [(i, i ^ 3) for i in range(4)] if chips == 2 else [(i, (i + 1) % places) for i in range(places)]
    two_back = [(i, (i + 2) % places) for i in range(places)]
    dt_turned = jnp.swapaxes(dt_raw, 1, 2)
    dt_other = lax.ppermute(dt_turned, "seq", pair)
    xbc_other = lax.ppermute(xbc, "seq", pair)
    xbc_here = in_hbm(xbc)
    tail, mark, dt_own, columns, points = pl.pallas_call(
        tail_kernel,
        out_shape=(
            shape((EDGE, CH + -(-H // EDGE) * n), BF16), shape((8, N), F32), shape((1, H, n), BF16),
            shape((H, 8), F32), shape((8, 128), jnp.int32),
        ),
        in_specs=[HBM] * 7,
        out_specs=(VMEM,) * 5,
        scratch_shapes=[pltpu.VMEM((1, H), F32)] * 3
        + [pltpu.SMEM((1, R), jnp.int32), pltpu.SMEM((1,), jnp.int32), pltpu.SemaphoreType.DMA((7,))],
        compiler_params=params(8),
        name="tail",
    )(xbc_here, in_hbm(dt_turned), in_hbm(dt_bias), in_hbm(a_rate), in_hbm(d_skip), in_hbm(readout), labels)
    edge_a = lax.ppermute(tail, "seq", one_back)
    edge_b = lax.ppermute(tail, "seq", two_back)

    ws, wr, e, rows, small, x, taps, bias = pl.pallas_call(
        steps_kernel,
        out_shape=(
            shape((2 * n, 128), BF16), shape((2 * n, 128), BF16), shape((n, 128), BF16), shape((16, 128), BF16), shape((8, 128), F32),
            shape((2 * n, SIDE), BF16), shape((KW, SIDE), F32), shape((1, SIDE), F32),
        ),
        in_specs=[VMEM] * 4 + [HBM, ANY, HBM, HBM],
        out_specs=(VMEM,) * 8,
        scratch_shapes=[pltpu.SemaphoreType.DMA((8,))],
        compiler_params=params(16),
        cost_estimate=cost(2 * 6 * n * n * 128, 8 * n * 256),
        name="steps",
    )(dt_own, dt_other, columns, points, xbc_here, xbc_other, in_hbm(conv_weight), in_hbm(conv_bias))

    if chips == 2:
        later = pl.pallas_call(
            later_kernel,
            out_shape=shape((16, 128), BF16),
            in_specs=[VMEM] * 4,
            out_specs=VMEM,
            compiler_params=params(16),
            cost_estimate=cost(2 * 6 * n * n * 128, 8 * n * 256),
            name="later",
        )(edge_b, edge_a, tied(columns, ws), points)
    else:
        later = jnp.zeros_like(small)
        for step in range(chips - 1):
            out = small.at[0:1].add(small[1:2] * later[0:1])
            later = lax.ppermute(out, "seq", [(i, (i - 2) % places) for i in range(places)])
            later = jnp.where(place < places - 2, later, 0.0)
        later = pack(jnp.broadcast_to(later[0, :H, None], (H, 16)))

    if split:
        ones = join(tied(mark, later), mark, lax.ppermute(mark, "dp", swap(4)))
        later = tied(later, ones)

    read_rows = D // 8 if split else HALF
    state, early, act_own, act_other, bc, *reads = pl.pallas_call(
        functools.partial(state_kernel, split=split),
        out_shape=(
            shape((N, HALF), BF16), shape((N, HALF), BF16),
            shape((n, HALF), BF16), shape((n, HALF), BF16), shape((n, BC), BF16),
        ) + (shape((read_rows, N), F32),) * (4 if split else 1),
        in_specs=[VMEM] * 9,
        out_specs=(VMEM,) * (9 if split else 6),
        scratch_shapes=[pltpu.VMEM((EDGE, SIDE), BF16), pltpu.VMEM((2 * n, SIDE), BF16), pltpu.VMEM((HALF, N), F32)],
        compiler_params=params(24),
        cost_estimate=cost(50 * n * n * D, 4 * 2 * n * SIDE),
        name="states",
    )(x, edge_a, edge_b, ws, wr, rows, later, taps, bias)

    h = state
    for step in range(chips - 1):
        if step:
            scale = jnp.repeat(lax.dynamic_slice_in_dim(small[1, :H], core * (H // 2), H // 2), P_SIZE)
            h = (h.astype(F32) * scale + state.astype(F32)).astype(BF16)
        h = lax.ppermute(h, "seq", two_back)
        if chips > 2:
            h = jnp.where(place >= 2, h, jnp.zeros_like(h))
    act_in = lax.ppermute(act_other, "seq", pair)
    if split:
        keep_x, send_x, keep_z, send_z = reads
        x_mark = lax.ppermute(tied(ones, send_x), "dp", swap(1))
        came_x = lax.ppermute(send_x, "dp", swap(1))
        came_z = lax.ppermute(send_z, "dp", swap(2))
        ones = join(mark, ones, x_mark)
        z_mark = lax.ppermute(ones, "dp", swap(2))

    near, reach = pl.pallas_call(
        diagonal_kernel,
        out_shape=(shape((2, n, HALF), F32), shape((2, n, HALF), F32)),
        in_specs=[VMEM] * 7,
        out_specs=(VMEM, VMEM),
        compiler_params=params(24),
        cost_estimate=cost(28 * n * n * D, 4 * n * D),
        name="diagonal",
    )(act_own, act_in, bc, ws, e, rows, gate_input)
    if split:
        keep_x, near, reach = lax.optimization_barrier((keep_x, near, reach))
        keep_a, send_a, keep_b, send_b = small_call(
            functools.partial(halves_kernel, sequences=float(sequences)), "halves", 4, D // 16,
            keep_x, came_x, keep_z, came_z, mark, x_mark, z_mark, ones,
        )
        came_a = lax.ppermute(send_a, "dp", swap(2))
        came_b = lax.ppermute(send_b, "dp", swap(1))
        keep, send = small_call(join_y_kernel, "join_y", 2, D // 16, keep_a, came_a, keep_b, came_b)
        came = lax.ppermute(send, "seq", [(i, i ^ 2) for i in range(places)])
    h = tied(h, keep) if split else h
    h_own, h_send = pl.pallas_call(
        carry_kernel, out_shape=(shape((N, HALF), BF16),) * 2, in_specs=[VMEM] * 3, out_specs=(VMEM,) * 2, compiler_params=params(8), name="carry"
    )(h, early, rows)
    h_other = lax.ppermute(h_send, "seq", pair)
    layer_out = pl.pallas_call(
        finish_kernel,
        out_shape=shape((1, n, D), BF16),
        in_specs=[VMEM] * 6,
        out_specs=HBM,
        scratch_shapes=[pltpu.VMEM((2, n, HALF), F32), pltpu.VMEM((n, D), BF16), pltpu.SemaphoreType.DMA((4,))],
        compiler_params=params(24),
        cost_estimate=cost(20 * n * n * D, 12 * n * D),
        name="finish",
    )(near, reach, bc, h_own, h_other, norm_gain[None])
    if split:
        (total,) = small_call(last_kernel, "last_y", 1, D // 16, keep, came)
        came = lax.ppermute(total, "dp", swap(4))
        total, layer_out = lax.optimization_barrier((total, layer_out))
        own, send = small_call(core_kernel, "cores", 2, D // 32, total, came)
        came = lax.ppermute(send, "seq", pair)
        steering = small_call(owner_kernel, "owner", 1, D // 32, own, came)[0]
    else:
        ones = lax.psum(mark[0, 0], "dp")
        weight = mark[0, 0] / ones - (1.0 - mark[0, 0]) / (sequences - ones)
        whole = lax.dynamic_update_slice_in_dim(jnp.zeros((D, N), F32), weight * reads[0], core * HALF, 0)
        steering = lax.psum_scatter(whole, ("dp", "seq"), scatter_dimension=0, tiled=True)
    return (layer_out, steering)


def solution(mesh):
    return jax.shard_map(
        on_device,
        mesh=mesh,
        in_specs=(
            P("dp", "seq", None),
            P("dp", "seq", None),
            P("dp", "seq", None),
            P(),
            P(),
            P(),
            P(),
            P(),
            P(),
            P("dp"),
            P("dp", None),
        ),
        out_specs=(P("dp", "seq", None), P(("dp", "seq"), None)),
        check_vma=False,
    )
```

```python
import functools

import jax
import jax.numpy as jnp
from jax import lax
from jax.experimental import pallas as pl
from jax.experimental.pallas import tpu as pltpu
from jax.sharding import PartitionSpec as P

H = 40
P_SIZE = 64
N = 128
KW = 4
R = 4
D = H * P_SIZE
HALF = D // 2
BC = 2 * N
SIDE = HALF + BC
CH = D + BC
CHUNK = 256
EDGE = 16
LEAD = 176
F32 = jnp.float32
BF16 = jnp.bfloat16
VMEM = pl.BlockSpec(memory_space=pltpu.VMEM)
SMEM = pl.BlockSpec(memory_space=pltpu.SMEM)
ANY = pl.BlockSpec(memory_space=pl.ANY)
HBM = pl.BlockSpec(memory_space=pltpu.HBM)
MIB = 1024 * 1024


def params(mib):
    return pltpu.CompilerParams(vmem_limit_bytes=mib * MIB)


def cost(flops, read):
    return pl.CostEstimate(flops=flops, bytes_accessed=read, transcendentals=0)


def in_hbm(x):
    return pltpu.with_memory_space_constraint(x, pltpu.HBM)


def tied(x, *others):
    return lax.optimization_barrier((x,) + others)[0]


def dot(a, b):
    return jnp.dot(a, b, preferred_element_type=F32)


def pack(w):
    high = w.astype(BF16).astype(F32)
    gap = jnp.zeros((64 - H, w.shape[1]), F32)
    return jnp.concatenate([high, gap, w - high, gap], axis=0).astype(BF16).T


def beside(columns):
    lane = lax.broadcasted_iota(jnp.int32, (H, 128), 1)
    table = jnp.zeros((H, 128), F32)
    for i, column in enumerate(columns):
        table = jnp.where(lane == i, column, table)
    return table


def turned(rows):
    table = jnp.concatenate(list(rows) + [jnp.zeros((8 - len(rows), H), F32)], axis=0)
    return jnp.concatenate([table, jnp.zeros((8, 128 - H), F32)], axis=1).T[:H]


def spread_matrix(first_head):
    row = lax.broadcasted_iota(jnp.int32, (128, CHUNK), 0)
    lane = lax.broadcasted_iota(jnp.int32, (128, CHUNK), 1)
    hit = (row & 63) == first_head + lane // P_SIZE
    return jnp.where(hit, 1.0, 0.0).astype(BF16)


def silu(v):
    half = 0.5 * v
    return half + half * jnp.tanh(half)


def fetch(pairs, sems):
    copies = [pltpu.make_async_copy(source, to, sems.at[i]) for i, (source, to) in enumerate(pairs)]
    for copy in copies:
        copy.start()
    for copy in copies:
        copy.wait()


def step_sizes(raw, bias):
    raw = raw + bias
    return jnp.maximum(raw, 0.0) + jnp.log1p(jnp.exp(-jnp.abs(raw)))


def running_sums(steps):
    n = steps[0].shape[1]
    row = lax.broadcasted_iota(jnp.int32, (n, n), 0)
    lane = lax.broadcasted_iota(jnp.int32, (n, n), 1)
    upper = jnp.where(row <= lane, 1.0, 0.0).astype(BF16)
    parts = []
    for step in steps:
        high = step.astype(BF16).astype(F32)
        middle = (step - high).astype(BF16).astype(F32)
        parts += [high, middle, step - high - middle]
    sums = dot(jnp.concatenate(parts, axis=0).astype(BF16), upper)
    return [sums[i : i + H] + (sums[i + H : i + 2 * H] + sums[i + 2 * H : i + 3 * H]) for i in range(0, 3 * H * len(steps), 3 * H)]


def read_levels(points, base, total):
    n = total[0].shape[1]
    index = lax.broadcasted_iota(jnp.int32, (H, n), 1)
    found = []
    for r in range(R):
        at = points[r : r + 1, 0:1] - base
        inside = jnp.where((at >= 0) & (at < 2 * n), 1.0, 0.0)
        level = jnp.zeros((H, n), F32)
        for block in range(2):
            level += jnp.where(index + block * n == at, total[block], 0.0)
        found.append((at, inside, jnp.sum(level, axis=1, keepdims=True)))
    return found


def carry_of(found):
    carry = jnp.zeros((H, 1), F32)
    for _, inside, level in found:
        carry += inside * jnp.exp(level)
    return carry * (1.0 / R)


def tail_kernel(
    xbc_hbm, dt_hbm, bias_hbm, rate_hbm, skip_hbm, points_hbm, out_a_ref, out_b_ref, dt_ref, columns_ref, points_ref,
    rows_ref, bias_ref, rate_ref, skip_ref, spot_ref, sems,
):
    n = xbc_hbm.shape[1]
    rows = xbc_hbm.at[0, pl.ds(n - EDGE, EDGE)]
    fetch(
        (
            (dt_hbm, dt_ref), (rows, rows_ref), (points_hbm, spot_ref),
            (bias_hbm, bias_ref.at[0]), (rate_hbm, rate_ref.at[0]), (skip_hbm, skip_ref.at[0]),
        ),
        sems,
    )
    tail = rows_ref[...].astype(F32)[EDGE - 8 :]
    steps = jnp.concatenate([dt_ref[0].astype(F32), jnp.zeros((4 * SIDE // 128 - H, n), F32)], axis=0).astype(BF16)
    upper = lax.broadcasted_iota(jnp.int32, (8, 128), 0) < 4
    for half, out_ref in enumerate((out_a_ref, out_b_ref)):
        pieces = [half * HALF + i for i in range(0, HALF, 128)] + [D + i for i in range(0, BC, 128)]
        pieces = [tail[:, i : i + 128] for i in pieces]
        stack = [jnp.where(upper, pltpu.roll(pieces[i], 4, 0), pieces[i + 1]) for i in range(0, len(pieces), 2)]
        out_ref[:, :128] = jnp.concatenate(stack, axis=0).astype(BF16)
        out_ref[:, 128:] = steps
    columns_ref[...] = turned((bias_ref[...], rate_ref[...], skip_ref[...]))
    spot = lax.broadcasted_iota(jnp.int32, points_ref.shape, 0)
    points = jnp.zeros(points_ref.shape, jnp.int32)
    for r in range(R):
        points = jnp.where(spot == r, spot_ref[0, r], points)
    points_ref[...] = points


def mark_kernel(label_ref, mark_ref):
    mark_ref[...] = jnp.zeros(mark_ref.shape, F32) + label_ref[0].astype(F32)


def steps_kernel(
    own_ref, other_ref, columns_ref, points_ref, xbc_hbm, conv_w_hbm, conv_b_hbm,
    ws_ref, wr_ref, e_ref, rows_ref, x_ref, taps_ref, bias_ref, *rest,
):
    place = lax.axis_index("seq")
    core = lax.rem(place, 2)
    n = own_ref.shape[2]
    sems = rest[-1]
    col = pl.multiple_of(core * HALF, 128)
    copies = []
    for from_at, to_at, width in ((D, HALF, BC), (col, 0, HALF)):
        here, there = pl.ds(from_at, width), pl.ds(to_at, width)
        copies.append((xbc_hbm.at[0, :, here], x_ref.at[:, there]))
        copies.append((conv_w_hbm.at[:, here], taps_ref.at[:, there]))
        copies.append((conv_b_hbm.at[here], bias_ref.at[0, there]))
    copies = [pltpu.make_async_copy(source, to, sems.at[i]) for i, (source, to) in enumerate(copies)]
    for copy in copies:
        copy.start()
    own = own_ref[0].astype(F32)
    other = other_ref[0].astype(F32)
    bias, rate, skip = columns_ref[:, 0:1], columns_ref[:, 1:2], columns_ref[:, 2:3]
    first = core == 0
    dts = [step_sizes(jnp.where(first == (block == 0), own, other), bias) for block in range(2)]
    cums = running_sums([-rate * dt for dt in dts])
    ends = [cum[:, n - 1 : n] for cum in cums]

    def store(ref, values):
        ref[:n] = pack(jnp.where(first, values[0], values[1]))
        ref[n:] = pack(jnp.where(first, values[1], values[0]))

    store(ws_ref, [dts[block] * jnp.exp(ends[block] - cums[block]) for block in range(2)])
    total = [cums[0], ends[0] + cums[1]]
    index = lax.broadcasted_iota(jnp.int32, (H, n), 1)
    weight = [jnp.zeros((H, n), F32), jnp.zeros((H, n), F32)]
    found = read_levels(points_ref[...], (place - core) * n, total)
    for at, inside, level in found:
        for block in range(2):
            seen = jnp.where(index + block * n <= at, jnp.exp(jnp.minimum(level - total[block], 0.0)), 0.0)
            weight[block] += inside * seen
    store(wr_ref, [weight[block] * dts[block] * (1.0 / R) for block in range(2)])
    e_ref[...] = pack(jnp.exp(jnp.where(first, cums[0], cums[1])))
    decay = [jnp.exp(end) for end in ends]
    back = jnp.exp(-jnp.where(first, ends[0], ends[1]))
    rows_ref[...] = pack(beside((decay[0], decay[1], skip, back)))[0:16]
    if len(rest) > 1:
        whole = beside((carry_of(found), jnp.exp(ends[0] + ends[1])))
        rest[0][...] = jnp.concatenate([whole, jnp.zeros((128 - H, 128), F32)], axis=0).T[0:8]
    for copy in copies:
        copy.wait()


def later_kernel(same_ref, cross_ref, columns_ref, points_ref, later_ref):
    place = lax.axis_index("seq")
    core = lax.rem(place, 2)
    n = same_ref.shape[1] - 128
    same, cross = same_ref[:, 128:].astype(F32)[:H], cross_ref[:, 128:].astype(F32)[:H]
    bias, rate = columns_ref[:, 0:1], columns_ref[:, 1:2]
    raws = [jnp.where((core == 0) == (block == 0), same, cross) for block in range(2)]
    cums = running_sums([-rate * step_sizes(raw, bias) for raw in raws])
    total = [cums[0], cums[0][:, n - 1 : n] + cums[1]]
    carry = carry_of(read_levels(points_ref[...], 2 * n, total))
    later_ref[...] = pack(beside((jnp.where(place < 2, carry, 0.0),)))[0:16]


def state_kernel(
    x_ref, other_ref, edge_a_ref, edge_b_ref, ws_ref, wr_ref, rows_ref, later_ref, taps_ref, bias_ref,
    state_ref, early_ref, act_own_ref, act_other_ref, bc_ref, *rest,
    split,
):
    reads = rest[:-2]
    bc_other_ref, read_ref = rest[-2:]
    place = lax.axis_index("seq")
    core = lax.rem(place, 2)
    first = core == 0
    n = x_ref.shape[0]
    started = jnp.where(place >= 2, 1.0, 0.0)
    edge = jnp.where(first, edge_a_ref[:, :128].astype(F32), edge_b_ref[:, :128].astype(F32)) * started
    tile = 128

    def before(at):
        pieces = []
        for i in range(at // 128, (at + CHUNK) // 128):
            piece = edge[i // 2 * 8 : i // 2 * 8 + 8]
            pieces.append(pltpu.roll(piece, 4, 0) if i % 2 == 0 else piece)
        return jnp.concatenate(pieces, axis=1)

    def convolve(at, act_refs, to):
        cols = pl.ds(at, CHUNK)
        from_cols = pl.ds(D + at - HALF if at >= HALF else pl.multiple_of(core * HALF + at, 128), CHUNK)
        taps = taps_ref[:, cols]
        bias = bias_ref[:, cols]

        def rows(side, start, count):
            return (x_ref[start : start + count, cols] if side == 0 else other_ref[0, start : start + count, from_cols]).astype(F32)

        ends = [rows(side, n - EDGE, EDGE)[EDGE - 8 :] for side in range(2)]
        chip = before(at)
        for side, act_ref in enumerate(act_refs):
            ahead = jnp.where(first == (side == 0), chip, ends[1 - side])
            for t in range(n // tile):
                if t == 0:
                    seen = jnp.concatenate([ahead, rows(side, 0, tile)], axis=0)
                else:
                    seen = rows(side, t * tile - EDGE, tile + EDGE)[EDGE - 8 :]
                last = pltpu.roll(seen, 1, 0)
                pair = taps[1:2] * seen + taps[0:1] * last
                total = bias + taps[3:4] * seen[8:] + taps[2:3] * last[8:]
                total += pltpu.roll(pair, 2, 0)[8:]
                act_ref[t * tile : (t + 1) * tile, to : to + CHUNK] = silu(total).astype(BF16)

    convolve(HALF, (bc_ref, bc_other_ref), 0)
    b_turned = [ref[:, :N].T for ref in (bc_ref, bc_other_ref)]
    both = jnp.concatenate(b_turned, axis=1)

    for j in range(HALF // CHUNK):
        at = j * CHUNK
        cols = pl.ds(at, CHUNK)
        convolve(at, (act_own_ref, act_other_ref), at)
        spread = spread_matrix(core * (H // 2) + j * (CHUNK // P_SIZE))
        table = dot(rows_ref[...], spread)
        ahead = dot(later_ref[...], spread)[0:1]
        act = jnp.concatenate([act_own_ref[:, cols], act_other_ref[:, cols]], axis=0).astype(F32)
        weighted = (act * dot(ws_ref[...], spread)).astype(BF16)
        own = dot(b_turned[0], weighted[:n])
        other = dot(b_turned[1], weighted[n:])
        state = jnp.where(first, table[1:2], 1.0) * own + jnp.where(first, 1.0, table[1:2]) * other
        early_ref[:, cols] = jnp.where(first, own, other).astype(BF16)
        state_ref[:, cols] = state.astype(BF16)
        read = act * dot(wr_ref[...], spread)
        high = read.astype(BF16)
        low = (read - high.astype(F32)).astype(BF16)
        seen = dot(both, high) + dot(both, low) + ahead * state
        read_ref[pl.ds(at, CHUNK)] = seen.T

    if split:
        part = D // 8
        x_bit = lax.rem(lax.axis_index("dp"), 2)
        z_bit = lax.rem(lax.axis_index("dp") // 2, 2)

        def rows(z, x, start, count):
            return read_ref[pl.ds(pl.multiple_of((2 * z + x) * part + start, 8), count)]

        rest = part - LEAD
        for q in range(2):
            here = slice(q * LEAD, (q + 1) * LEAD)
            reads[0][here] = rows(q, x_bit, 0, LEAD)
            reads[1][here] = rows(q, 1 - x_bit, 0, LEAD)
            here = slice(q * rest, (q + 1) * rest)
            reads[2][here] = rows(z_bit, q, LEAD, rest)
            reads[3][here] = rows(1 - z_bit, q, LEAD, rest)
    else:
        reads[0][...] = read_ref[...]


def diagonal_kernel(act_own_ref, act_other_ref, bc_ref, ws_ref, e_ref, rows_ref, gate_ref, near_ref, far_ref):
    core = lax.rem(lax.axis_index("seq"), 2)
    n = act_own_ref.shape[0]
    scores = lax.dot_general(bc_ref[:, N:], bc_ref[:, :N], (((1,), (1,)), ((), ())), preferred_element_type=F32)
    row = lax.broadcasted_iota(jnp.int32, (n, n), 0)
    lane = lax.broadcasted_iota(jnp.int32, (n, n), 1)
    masked = jnp.where(row >= lane, scores, 0.0).astype(BF16)
    ws = ws_ref[:n]
    for side, source in enumerate((act_own_ref, act_other_ref)):
        half = core if side == 0 else 1 - core

        @pl.loop(0, HALF // CHUNK, unroll=True)
        def _(j):
            at = pl.multiple_of(j * CHUNK, CHUNK)
            cols = pl.ds(at, CHUNK)
            spread = spread_matrix(half * (H // 2) + j * (CHUNK // P_SIZE))
            act = source[:, cols].astype(F32)
            weighted = (act * dot(ws, spread)).astype(BF16)
            table = dot(rows_ref[...], spread)
            decay = dot(e_ref[...], spread)
            value = decay * (table[3:4] * dot(masked, weighted)) + table[2:3] * act
            gate = silu(gate_ref[0, :, pl.ds(pl.multiple_of(half * HALF + at, CHUNK), CHUNK)].astype(F32))
            near_ref[side, :, cols] = value * gate
            far_ref[side, :, cols] = decay * gate


def carry_kernel(h_ref, early_ref, rows_ref, keep_ref, send_ref):
    place = lax.axis_index("seq")
    first = lax.rem(place, 2) == 0
    for j in range(HALF // CHUNK):
        cols = pl.ds(j * CHUNK, CHUNK)
        spread = spread_matrix(lax.rem(place, 2) * (H // 2) + j * (CHUNK // P_SIZE))
        chip = jnp.where(place >= 2, h_ref[:, cols].astype(F32), 0.0)
        middle = dot(rows_ref[...], spread)[0:1] * chip + early_ref[:, cols].astype(F32)
        keep_ref[:, cols] = jnp.where(first, chip, middle).astype(BF16)
        send_ref[:, cols] = jnp.where(first, middle, chip).astype(BF16)


def finish_kernel(near_ref, far_ref, bc_ref, h_own_ref, h_other_ref, gain_ref, out_hbm, g_ref, out_ref, sems):
    core = lax.rem(lax.axis_index("seq"), 2)
    n = bc_ref.shape[0]
    squares = jnp.zeros((n, CHUNK), F32)
    c_vals = bc_ref[:, N:]
    for side in range(2):
        h_ref = (h_own_ref, h_other_ref)[side]
        for j in range(HALF // CHUNK):
            cols = pl.ds(j * CHUNK, CHUNK)
            g = near_ref[side, :, cols] + far_ref[side, :, cols] * dot(c_vals, h_ref[:, cols])
            g_ref[side, :, cols] = g
            squares += g * g
    scale = lax.rsqrt(jnp.sum(squares, axis=-1, keepdims=True) * (1.0 / D) + 1e-05)
    tile = n // 4
    copies = []
    for t in range(4):
        rows = pl.ds(t * tile, tile)
        for side in range(2):
            half = core if side == 0 else 1 - core
            for j in range(HALF // CHUNK):
                cols = pl.ds(pl.multiple_of(half * HALF + j * CHUNK, CHUNK), CHUNK)
                g = g_ref[side, rows, pl.ds(j * CHUNK, CHUNK)]
                out_ref[rows, cols] = (g * scale[t * tile : (t + 1) * tile] * gain_ref[:, cols]).astype(BF16)
        copies.append(pltpu.make_async_copy(out_ref.at[rows], out_hbm.at[0, rows], sems.at[t]))
        copies[t].start()
    for copy in copies:
        copy.wait()


def join_kernel(mark_ref, a_ref, b_ref, out_ref):
    row = lax.broadcasted_iota(jnp.int32, out_ref.shape, 0)
    out_ref[...] = jnp.where(row == 0, a_ref[...] + b_ref[...], mark_ref[...])


def join(mark, a, b):
    out = jax.ShapeDtypeStruct(a.shape, a.dtype)
    return pl.pallas_call(
        join_kernel, out_shape=out, in_specs=[VMEM] * 3, out_specs=VMEM, compiler_params=params(8), name="join"
    )(mark, a, b)


def halves_kernel(
    kept_x_ref, came_x_ref, kept_z_ref, came_z_ref, mark_ref, x_mark_ref, z_mark_ref, sum_ref,
    keep_a_ref, send_a_ref, keep_b_ref, send_b_ref,
    *, sequences,
):
    ones = sum_ref[0:1] + z_mark_ref[0:1]

    def weight(mark):
        return mark / ones - (1.0 - mark) / (sequences - ones)

    own = weight(mark_ref[1:2])
    place = lax.axis_index("dp")
    x_bit = lax.rem(place, 2)
    z_bit = lax.rem(place // 2, 2)
    work = (
        (kept_x_ref, came_x_ref, x_mark_ref, z_bit, keep_a_ref, send_a_ref),
        (kept_z_ref, came_z_ref, z_mark_ref, x_bit, keep_b_ref, send_b_ref),
    )
    for kept, came, other_mark, bit, keep, send in work:
        other = weight(other_mark[1:2])
        part = keep.shape[0]
        mine = pl.ds(pl.multiple_of(bit * part, 8), part)
        yours = pl.ds(pl.multiple_of((1 - bit) * part, 8), part)
        send[...] = own * kept[yours] + other * came[yours]
        keep[...] = own * kept[mine] + other * came[mine]


def chunks_kernel(keep_a_ref, came_a_ref, keep_b_ref, came_b_ref, keep_ref, core_ref, same_ref, cross_ref):
    place = lax.axis_index("seq")
    part = keep_ref.shape[0]
    upper = lax.rem(place // 2, 2) == 0
    first = lax.rem(place, 2) == 0
    rows = jnp.concatenate([keep_a_ref[...] + came_a_ref[...], keep_b_ref[...] + came_b_ref[...]], axis=0)
    here = jnp.where(upper, rows[: 2 * part], rows[2 * part :])
    there = jnp.where(upper, rows[2 * part :], rows[: 2 * part])
    keep_ref[...] = jnp.where(first, here[:part], here[part:])
    core_ref[...] = jnp.where(first, here[part:], here[:part])
    same_ref[...] = jnp.where(first, there[:part], there[part:])
    cross_ref[...] = jnp.where(first, there[part:], there[:part])


def planes_kernel(own_ref, same_ref, core_ref, cross_ref, keep_ref, send_ref):
    stays = lax.rem(lax.axis_index("dp") // 4, 2) == lax.rem(lax.axis_index("seq"), 2)
    own = own_ref[...] + same_ref[...]
    other = core_ref[...] + cross_ref[...]
    keep_ref[...] = jnp.where(stays, own, other)
    send_ref[...] = jnp.where(stays, other, own)


def sum_kernel(keep_ref, came_ref, out_ref):
    out_ref[...] = keep_ref[...] + came_ref[...]


def swap(k):
    return [(i, i ^ k) for i in range(8)]


def small_call(kernel, name, counts, *args):
    parts = tuple(jax.ShapeDtypeStruct((rows, N), F32) for rows in counts)
    return pl.pallas_call(
        kernel, out_shape=parts, in_specs=[VMEM] * len(args), out_specs=(VMEM,) * len(parts), compiler_params=params(8), name=name
    )(*args)


def on_device(xbc, gate_input, dt_raw, conv_weight, conv_bias, dt_bias, a_rate, d_skip, norm_gain, labels, readout):
    n = xbc.shape[1]
    places = lax.axis_size("seq")
    sequences = lax.axis_size("dp")
    chips = places // 2
    place = lax.axis_index("seq")
    core = place % 2
    split = sequences == 8 and places == 4
    pair = [(i, i ^ 1) for i in range(places)]
    shape = jax.ShapeDtypeStruct

    one_back = [(i, i ^ 3) for i in range(4)] if chips == 2 else [(i, (i + 1) % places) for i in range(places)]
    two_back = [(i, (i + 2) % places) for i in range(places)]
    dt_turned = jnp.swapaxes(dt_raw, 1, 2)
    dt_other = lax.ppermute(dt_turned, "seq", pair)
    xbc_other = lax.ppermute(xbc, "seq", pair)
    xbc_here = in_hbm(xbc)
    payload = shape((4 * SIDE // 128, 128 + n), BF16)
    tail_a, tail_b, dt_own, columns, points = pl.pallas_call(
        tail_kernel,
        out_shape=(payload, payload, shape((1, H, n), BF16), shape((H, 8), F32), shape((8, 128), jnp.int32)),
        in_specs=[HBM] * 6,
        out_specs=(VMEM,) * 5,
        scratch_shapes=[pltpu.VMEM((EDGE, CH), BF16)]
        + [pltpu.VMEM((1, H), F32)] * 3
        + [pltpu.SMEM((1, R), jnp.int32), pltpu.SemaphoreType.DMA((6,))],
        compiler_params=params(8),
        name="tail",
    )(xbc_here, in_hbm(dt_turned), in_hbm(dt_bias), in_hbm(a_rate), in_hbm(d_skip), in_hbm(readout))
    edge_a = lax.ppermute(tail_a, "seq", one_back)
    edge_b = lax.ppermute(tail_b, "seq", two_back)
    mark = pl.pallas_call(
        mark_kernel, out_shape=shape((8, N), F32), in_specs=[SMEM], out_specs=VMEM, compiler_params=params(8), name="mark"
    )(tied(labels, points))

    ws, wr, e, rows, x, taps, bias, *small = pl.pallas_call(
        steps_kernel,
        out_shape=(
            shape((2 * n, 128), BF16), shape((2 * n, 128), BF16), shape((n, 128), BF16), shape((16, 128), BF16),
            shape((n, SIDE), BF16), shape((KW, SIDE), F32), shape((1, SIDE), F32),
        ) + ((shape((8, 128), F32),) if chips != 2 else ()),
        in_specs=[VMEM] * 4 + [HBM] * 3,
        out_specs=(VMEM,) * (8 if chips != 2 else 7),
        scratch_shapes=[pltpu.SemaphoreType.DMA((6,))],
        compiler_params=params(16),
        cost_estimate=cost(2 * 6 * n * n * 128, 8 * n * 256),
        name="steps",
    )(dt_own, dt_other, columns, points, xbc_here, in_hbm(conv_weight), in_hbm(conv_bias))

    if chips == 2:
        later = pl.pallas_call(
            later_kernel,
            out_shape=shape((16, 128), BF16),
            in_specs=[VMEM] * 4,
            out_specs=VMEM,
            compiler_params=params(16),
            cost_estimate=cost(2 * 6 * n * n * 128, 8 * n * 256),
            name="later",
        )(edge_b, edge_a, tied(columns, ws), points)
    else:
        small = small[0]
        later = jnp.zeros_like(small)
        for step in range(chips - 1):
            out = small.at[0:1].add(small[1:2] * later[0:1])
            later = lax.ppermute(out, "seq", [(i, (i - 2) % places) for i in range(places)])
            later = jnp.where(place < places - 2, later, 0.0)
        later = pack(jnp.broadcast_to(later[0, :H, None], (H, 16)))

    if split:
        ones = join(tied(mark, later), mark, lax.ppermute(mark, "dp", swap(4)))
        later = tied(later, ones)

    read_rows = (2 * LEAD, 2 * LEAD, D // 4 - 2 * LEAD, D // 4 - 2 * LEAD) if split else (HALF,)
    state, early, act_own, act_other, bc, *reads = pl.pallas_call(
        functools.partial(state_kernel, split=split),
        out_shape=(
            shape((N, HALF), BF16), shape((N, HALF), BF16),
            shape((n, HALF), BF16), shape((n, HALF), BF16), shape((n, BC), BF16),
        ) + tuple(shape((count, N), F32) for count in read_rows),
        in_specs=[VMEM] * 10,
        out_specs=(VMEM,) * (5 + len(read_rows)),
        scratch_shapes=[pltpu.VMEM((n, BC), BF16), pltpu.VMEM((HALF, N), F32)],
        compiler_params=params(24),
        cost_estimate=cost(50 * n * n * D, 4 * 2 * n * SIDE),
        name="states",
    )(x, xbc_other, edge_a, edge_b, ws, wr, rows, later, taps, bias)

    h = state
    for step in range(chips - 1):
        if step:
            scale = jnp.repeat(lax.dynamic_slice_in_dim(small[1, :H], core * (H // 2), H // 2), P_SIZE)
            h = (h.astype(F32) * scale + state.astype(F32)).astype(BF16)
        h = lax.ppermute(h, "seq", two_back)
        if chips > 2:
            h = jnp.where(place >= 2, h, jnp.zeros_like(h))
    act_in = lax.ppermute(act_other, "seq", pair)
    if split:
        keep_x, send_x, keep_z, send_z = reads
        x_mark = lax.ppermute(tied(ones, send_x), "dp", swap(1))
        came_x = lax.ppermute(send_x, "dp", swap(1))
        came_z = lax.ppermute(send_z, "dp", swap(2))
        ones = join(mark, ones, x_mark)
        z_mark = lax.ppermute(ones, "dp", swap(2))

    near, reach = pl.pallas_call(
        diagonal_kernel,
        out_shape=(shape((2, n, HALF), F32), shape((2, n, HALF), F32)),
        in_specs=[VMEM] * 7,
        out_specs=(VMEM, VMEM),
        compiler_params=params(24),
        cost_estimate=cost(28 * n * n * D, 4 * n * D),
        name="diagonal",
    )(act_own, act_in, bc, ws, e, rows, gate_input)
    if split:
        keep_x, near, reach = lax.optimization_barrier((keep_x, near, reach))
        keep_a, send_a, keep_b, send_b = small_call(
            functools.partial(halves_kernel, sequences=float(sequences)), "halves", (LEAD, LEAD, D // 8 - LEAD, D // 8 - LEAD),
            keep_x, came_x, keep_z, came_z, mark, x_mark, z_mark, ones,
        )
        came_a = lax.ppermute(send_a, "dp", swap(2))
        came_b = lax.ppermute(send_b, "dp", swap(1))
        keep, to_core, to_same, to_cross = small_call(chunks_kernel, "chunks", (D // 32,) * 4, keep_a, came_a, keep_b, came_b)
        from_core = lax.ppermute(to_core, "seq", pair)
        from_same = lax.ppermute(to_same, "seq", [(i, i ^ 2) for i in range(places)])
        from_cross = lax.ppermute(to_cross, "seq", [(i, i ^ 3) for i in range(places)])
    h = tied(h, keep) if split else h
    h_own, h_send = pl.pallas_call(
        carry_kernel, out_shape=(shape((N, HALF), BF16),) * 2, in_specs=[VMEM] * 3, out_specs=(VMEM,) * 2, compiler_params=params(8), name="carry",
        cost_estimate=cost(8 * n * n * D, 4 * N * D),
    )(h, early, rows)
    h_other = lax.ppermute(h_send, "seq", pair)
    layer_out = pl.pallas_call(
        finish_kernel,
        out_shape=shape((1, n, D), BF16),
        in_specs=[VMEM] * 6,
        out_specs=HBM,
        scratch_shapes=[pltpu.VMEM((2, n, HALF), F32), pltpu.VMEM((n, D), BF16), pltpu.SemaphoreType.DMA((4,))],
        compiler_params=params(24),
        cost_estimate=cost(20 * n * n * D, 12 * n * D),
        name="finish",
    )(near, reach, bc, h_own, h_other, norm_gain[None])
    if split:
        keep, send = small_call(planes_kernel, "planes", (D // 32,) * 2, keep, from_same, from_core, from_cross)
        came = lax.ppermute(send, "dp", swap(4))
        keep, layer_out = lax.optimization_barrier((keep, layer_out))
        steering = small_call(sum_kernel, "sum", (D // 32,), keep, came)[0]
    else:
        ones = lax.psum(mark[0, 0], "dp")
        weight = mark[0, 0] / ones - (1.0 - mark[0, 0]) / (sequences - ones)
        whole = lax.dynamic_update_slice_in_dim(jnp.zeros((D, N), F32), weight * reads[0], core * HALF, 0)
        steering = lax.psum_scatter(whole, ("dp", "seq"), scatter_dimension=0, tiled=True)
    return (layer_out, steering)


def solution(mesh):
    return jax.shard_map(
        on_device,
        mesh=mesh,
        in_specs=(
            P("dp", "seq", None),
            P("dp", "seq", None),
            P("dp", "seq", None),
            P(),
            P(),
            P(),
            P(),
            P(),
            P(),
            P("dp"),
            P("dp", None),
        ),
        out_specs=(P("dp", "seq", None), P(("dp", "seq"), None)),
        check_vma=False,
    )
```

```python
import functools

import jax
import jax.numpy as jnp
from jax import lax
from jax.experimental import pallas as pl
from jax.experimental.pallas import tpu as pltpu
from jax.sharding import PartitionSpec as P

H = 40
P_SIZE = 64
N = 128
KW = 4
R = 4
D = H * P_SIZE
HALF = D // 2
BC = 2 * N
SIDE = HALF + BC
CH = D + BC
CHUNK = 256
EDGE = 16
LEAD = 176
F32 = jnp.float32
BF16 = jnp.bfloat16
VMEM = pl.BlockSpec(memory_space=pltpu.VMEM)
SMEM = pl.BlockSpec(memory_space=pltpu.SMEM)
ANY = pl.BlockSpec(memory_space=pl.ANY)
HBM = pl.BlockSpec(memory_space=pltpu.HBM)
MIB = 1024 * 1024


def params(mib):
    return pltpu.CompilerParams(vmem_limit_bytes=mib * MIB)


def cost(flops, read):
    return pl.CostEstimate(flops=flops, bytes_accessed=read, transcendentals=0)


def in_hbm(x):
    return pltpu.with_memory_space_constraint(x, pltpu.HBM)


def tied(x, *others):
    return lax.optimization_barrier((x,) + others)[0]


def dot(a, b):
    return jnp.dot(a, b, preferred_element_type=F32)


def pack(w):
    high = w.astype(BF16).astype(F32)
    gap = jnp.zeros((64 - H, w.shape[1]), F32)
    return jnp.concatenate([high, gap, w - high, gap], axis=0).astype(BF16).T


def stand(w):
    return jnp.concatenate([w, jnp.zeros((128 - H, w.shape[1]), F32)], axis=0).T


def widen(w, first_head):
    head = lax.broadcasted_iota(jnp.int32, w.shape, 1) // P_SIZE + first_head
    picked = [jnp.take_along_axis(w, head + i, axis=1) for i in range(0, CHUNK // P_SIZE, 128 // P_SIZE)]
    return jnp.concatenate(picked, axis=1)


def beside(columns):
    lane = lax.broadcasted_iota(jnp.int32, (H, 128), 1)
    table = jnp.zeros((H, 128), F32)
    for i, column in enumerate(columns):
        table = jnp.where(lane == i, column, table)
    return table


def turned(rows):
    table = jnp.concatenate(list(rows) + [jnp.zeros((8 - len(rows), H), F32)], axis=0)
    return jnp.concatenate([table, jnp.zeros((8, 128 - H), F32)], axis=1).T[:H]


def spread_matrix(first_head):
    row = lax.broadcasted_iota(jnp.int32, (128, CHUNK), 0)
    lane = lax.broadcasted_iota(jnp.int32, (128, CHUNK), 1)
    hit = (row & 63) == first_head + lane // P_SIZE
    return jnp.where(hit, 1.0, 0.0).astype(BF16)


def silu(v):
    half = 0.5 * v
    return half + half * jnp.tanh(half)


def fetch(pairs, sems):
    copies = [pltpu.make_async_copy(source, to, sems.at[i]) for i, (source, to) in enumerate(pairs)]
    for copy in copies:
        copy.start()
    for copy in copies:
        copy.wait()


def step_sizes(raw, bias):
    raw = raw + bias
    return jnp.maximum(raw, 0.0) + jnp.log1p(jnp.exp(-jnp.abs(raw)))


def running_sums(steps):
    n = steps[0].shape[1]
    row = lax.broadcasted_iota(jnp.int32, (n, n), 0)
    lane = lax.broadcasted_iota(jnp.int32, (n, n), 1)
    upper = jnp.where(row <= lane, 1.0, 0.0).astype(BF16)
    parts = []
    for step in steps:
        high = step.astype(BF16).astype(F32)
        middle = (step - high).astype(BF16).astype(F32)
        parts += [high, middle, step - high - middle]
    sums = dot(jnp.concatenate(parts, axis=0).astype(BF16), upper)
    return [sums[i : i + H] + (sums[i + H : i + 2 * H] + sums[i + 2 * H : i + 3 * H]) for i in range(0, 3 * H * len(steps), 3 * H)]


def read_levels(points, base, total):
    n = total[0].shape[1]
    index = lax.broadcasted_iota(jnp.int32, (H, n), 1)
    found = []
    for r in range(R):
        at = points[r : r + 1, 0:1] - base
        inside = jnp.where((at >= 0) & (at < 2 * n), 1.0, 0.0)
        level = jnp.zeros((H, n), F32)
        for block in range(2):
            level += jnp.where(index + block * n == at, total[block], 0.0)
        found.append((at, inside, jnp.sum(level, axis=1, keepdims=True)))
    return found


def carry_of(found):
    carry = jnp.zeros((H, 1), F32)
    for _, inside, level in found:
        carry += inside * jnp.exp(level)
    return carry * (1.0 / R)


def tail_kernel(
    xbc_hbm, dt_hbm, bias_hbm, rate_hbm, skip_hbm, points_hbm, out_a_ref, out_b_ref, dt_ref, columns_ref, points_ref,
    rows_ref, bias_ref, rate_ref, skip_ref, spot_ref, sems,
):
    n = xbc_hbm.shape[1]
    rows = xbc_hbm.at[0, pl.ds(n - EDGE, EDGE)]
    fetch(
        (
            (dt_hbm, dt_ref), (rows, rows_ref), (points_hbm, spot_ref),
            (bias_hbm, bias_ref.at[0]), (rate_hbm, rate_ref.at[0]), (skip_hbm, skip_ref.at[0]),
        ),
        sems,
    )
    tail = rows_ref[...].astype(F32)[EDGE - 8 :]
    steps = jnp.concatenate([dt_ref[0].astype(F32), jnp.zeros((4 * SIDE // 128 - H, n), F32)], axis=0).astype(BF16)
    upper = lax.broadcasted_iota(jnp.int32, (8, 128), 0) < 4
    for half, out_ref in enumerate((out_a_ref, out_b_ref)):
        pieces = [half * HALF + i for i in range(0, HALF, 128)] + [D + i for i in range(0, BC, 128)]
        pieces = [tail[:, i : i + 128] for i in pieces]
        stack = [jnp.where(upper, pltpu.roll(pieces[i], 4, 0), pieces[i + 1]) for i in range(0, len(pieces), 2)]
        out_ref[:, :128] = jnp.concatenate(stack, axis=0).astype(BF16)
        out_ref[:, 128:] = steps
    columns_ref[...] = turned((bias_ref[...], rate_ref[...], skip_ref[...]))
    spot = lax.broadcasted_iota(jnp.int32, points_ref.shape, 0)
    points = jnp.zeros(points_ref.shape, jnp.int32)
    for r in range(R):
        points = jnp.where(spot == r, spot_ref[0, r], points)
    points_ref[...] = points


def mark_kernel(label_ref, mark_ref):
    mark_ref[...] = jnp.zeros(mark_ref.shape, F32) + label_ref[0].astype(F32)


def steps_kernel(
    own_ref, other_ref, columns_ref, points_ref, xbc_hbm, conv_w_hbm, conv_b_hbm,
    ws_ref, wr_ref, e_ref, rows_ref, x_ref, taps_ref, bias_ref, *rest,
):
    place = lax.axis_index("seq")
    core = lax.rem(place, 2)
    n = own_ref.shape[2]
    sems = rest[-1]
    col = pl.multiple_of(core * HALF, 128)
    copies = []
    for from_at, to_at, width in ((D, HALF, BC), (col, 0, HALF)):
        here, there = pl.ds(from_at, width), pl.ds(to_at, width)
        copies.append((xbc_hbm.at[0, :, here], x_ref.at[:, there]))
        copies.append((conv_w_hbm.at[:, here], taps_ref.at[:, there]))
        copies.append((conv_b_hbm.at[here], bias_ref.at[0, there]))
    copies = [pltpu.make_async_copy(source, to, sems.at[i]) for i, (source, to) in enumerate(copies)]
    for copy in copies:
        copy.start()
    own = own_ref[0].astype(F32)
    other = other_ref[0].astype(F32)
    bias, rate, skip = columns_ref[:, 0:1], columns_ref[:, 1:2], columns_ref[:, 2:3]
    first = core == 0
    dts = [step_sizes(jnp.where(first == (block == 0), own, other), bias) for block in range(2)]
    cums = running_sums([-rate * dt for dt in dts])
    ends = [cum[:, n - 1 : n] for cum in cums]

    def store(ref, values):
        ref[:n] = stand(jnp.where(first, values[0], values[1]))
        ref[n:] = stand(jnp.where(first, values[1], values[0]))

    store(ws_ref, [dts[block] * jnp.exp(ends[block] - cums[block]) for block in range(2)])
    total = [cums[0], ends[0] + cums[1]]
    index = lax.broadcasted_iota(jnp.int32, (H, n), 1)
    weight = [jnp.zeros((H, n), F32), jnp.zeros((H, n), F32)]
    found = read_levels(points_ref[...], (place - core) * n, total)
    for at, inside, level in found:
        for block in range(2):
            seen = jnp.where(index + block * n <= at, jnp.exp(jnp.minimum(level - total[block], 0.0)), 0.0)
            weight[block] += inside * seen
    store(wr_ref, [weight[block] * dts[block] * (1.0 / R) for block in range(2)])
    e_ref[...] = stand(jnp.exp(jnp.where(first, cums[0], cums[1])))
    decay = [jnp.exp(end) for end in ends]
    back = jnp.exp(-jnp.where(first, ends[0], ends[1]))
    rows_ref[...] = pack(beside((decay[0], decay[1], skip, back)))[0:16]
    if len(rest) > 1:
        whole = beside((carry_of(found), jnp.exp(ends[0] + ends[1])))
        rest[0][...] = jnp.concatenate([whole, jnp.zeros((128 - H, 128), F32)], axis=0).T[0:8]
    for copy in copies:
        copy.wait()


def later_kernel(same_ref, cross_ref, columns_ref, points_ref, later_ref):
    place = lax.axis_index("seq")
    core = lax.rem(place, 2)
    n = same_ref.shape[1] - 128
    same, cross = same_ref[:, 128:].astype(F32)[:H], cross_ref[:, 128:].astype(F32)[:H]
    bias, rate = columns_ref[:, 0:1], columns_ref[:, 1:2]
    raws = [jnp.where((core == 0) == (block == 0), same, cross) for block in range(2)]
    cums = running_sums([-rate * step_sizes(raw, bias) for raw in raws])
    total = [cums[0], cums[0][:, n - 1 : n] + cums[1]]
    carry = carry_of(read_levels(points_ref[...], 2 * n, total))
    later_ref[...] = pack(beside((jnp.where(place < 2, carry, 0.0),)))[0:16]


def state_kernel(
    x_ref, other_ref, edge_a_ref, edge_b_ref, ws_ref, wr_ref, rows_ref, later_ref, taps_ref, bias_ref,
    state_ref, early_ref, act_own_ref, act_other_ref, bc_ref, *rest,
    split,
):
    reads = rest[:-2]
    bc_other_ref, read_ref = rest[-2:]
    place = lax.axis_index("seq")
    core = lax.rem(place, 2)
    first = core == 0
    n = x_ref.shape[0]
    started = jnp.where(place >= 2, 1.0, 0.0)
    edge = jnp.where(first, edge_a_ref[:, :128].astype(F32), edge_b_ref[:, :128].astype(F32)) * started
    tile = 128

    def before(at):
        pieces = []
        for i in range(at // 128, (at + CHUNK) // 128):
            piece = edge[i // 2 * 8 : i // 2 * 8 + 8]
            pieces.append(pltpu.roll(piece, 4, 0) if i % 2 == 0 else piece)
        return jnp.concatenate(pieces, axis=1)

    def convolve(at, act_refs, to):
        cols = pl.ds(at, CHUNK)
        from_cols = pl.ds(D + at - HALF if at >= HALF else pl.multiple_of(core * HALF + at, 128), CHUNK)
        taps = taps_ref[:, cols]
        bias = bias_ref[:, cols]

        def rows(side, start, count):
            return (x_ref[start : start + count, cols] if side == 0 else other_ref[0, start : start + count, from_cols]).astype(F32)

        ends = [rows(side, n - EDGE, EDGE)[EDGE - 8 :] for side in range(2)]
        chip = before(at)
        for side, act_ref in enumerate(act_refs):
            ahead = jnp.where(first == (side == 0), chip, ends[1 - side])
            for t in range(n // tile):
                if t == 0:
                    seen = jnp.concatenate([ahead, rows(side, 0, tile)], axis=0)
                else:
                    seen = rows(side, t * tile - EDGE, tile + EDGE)[EDGE - 8 :]
                last = pltpu.roll(seen, 1, 0)
                pair = taps[1:2] * seen + taps[0:1] * last
                total = bias + taps[3:4] * seen[8:] + taps[2:3] * last[8:]
                total += pltpu.roll(pair, 2, 0)[8:]
                act_ref[t * tile : (t + 1) * tile, to : to + CHUNK] = silu(total).astype(BF16)

    convolve(HALF, (bc_ref, bc_other_ref), 0)
    b_turned = [ref[:, :N].T for ref in (bc_ref, bc_other_ref)]
    both = jnp.concatenate(b_turned, axis=1)
    rows = jnp.concatenate([rows_ref[...], later_ref[...]], axis=0)

    for j in range(HALF // CHUNK):
        at = j * CHUNK
        cols = pl.ds(at, CHUNK)
        convolve(at, (act_own_ref, act_other_ref), at)
        head = core * (H // 2) + j * (CHUNK // P_SIZE)
        spread = spread_matrix(head)
        wide = dot(rows, spread)
        table, ahead = wide[:16], wide[16:17]
        act = jnp.concatenate([act_own_ref[:, cols], act_other_ref[:, cols]], axis=0).astype(F32)
        weighted = (act * widen(ws_ref[...], head)).astype(BF16)
        own = dot(b_turned[0], weighted[:n])
        other = dot(b_turned[1], weighted[n:])
        state = jnp.where(first, table[1:2], 1.0) * own + jnp.where(first, 1.0, table[1:2]) * other
        early_ref[:, cols] = jnp.where(first, own, other).astype(BF16)
        state_ref[:, cols] = state.astype(BF16)
        read = act * widen(wr_ref[...], head)
        high = read.astype(BF16)
        low = (read - high.astype(F32)).astype(BF16)
        seen = dot(both, high) + dot(both, low) + ahead * state
        read_ref[pl.ds(at, CHUNK)] = seen.T

    if split:
        part = D // 8
        x_bit = lax.rem(lax.axis_index("dp"), 2)
        z_bit = lax.rem(lax.axis_index("dp") // 2, 2)

        def rows(z, x, start, count):
            return read_ref[pl.ds(pl.multiple_of((2 * z + x) * part + start, 8), count)]

        rest = part - LEAD
        for q in range(2):
            here = slice(q * LEAD, (q + 1) * LEAD)
            reads[0][here] = rows(q, x_bit, 0, LEAD)
            reads[1][here] = rows(q, 1 - x_bit, 0, LEAD)
            here = slice(q * rest, (q + 1) * rest)
            reads[2][here] = rows(z_bit, q, LEAD, rest)
            reads[3][here] = rows(1 - z_bit, q, LEAD, rest)
    else:
        reads[0][...] = read_ref[...]


def diagonal_kernel(act_own_ref, act_other_ref, bc_ref, ws_ref, e_ref, rows_ref, gate_ref, near_ref, far_ref):
    core = lax.rem(lax.axis_index("seq"), 2)
    n = act_own_ref.shape[0]
    scores = lax.dot_general(bc_ref[:, N:], bc_ref[:, :N], (((1,), (1,)), ((), ())), preferred_element_type=F32)
    row = lax.broadcasted_iota(jnp.int32, (n, n), 0)
    lane = lax.broadcasted_iota(jnp.int32, (n, n), 1)
    masked = jnp.where(row >= lane, scores, 0.0).astype(BF16)
    ws = ws_ref[:n]
    for side, source in enumerate((act_own_ref, act_other_ref)):
        half = core if side == 0 else 1 - core

        @pl.loop(0, HALF // CHUNK, unroll=True)
        def _(j):
            at = pl.multiple_of(j * CHUNK, CHUNK)
            cols = pl.ds(at, CHUNK)
            head = half * (H // 2) + j * (CHUNK // P_SIZE)
            spread = spread_matrix(head)
            act = source[:, cols].astype(F32)
            weighted = (act * widen(ws, head)).astype(BF16)
            table = dot(rows_ref[...], spread)
            decay = widen(e_ref[...], head)
            value = decay * (table[3:4] * dot(masked, weighted)) + table[2:3] * act
            gate = silu(gate_ref[0, :, pl.ds(pl.multiple_of(half * HALF + at, CHUNK), CHUNK)].astype(F32))
            near_ref[side, :, cols] = value * gate
            far_ref[side, :, cols] = decay * gate


def carry_kernel(h_ref, early_ref, rows_ref, keep_ref, send_ref):
    place = lax.axis_index("seq")
    first = lax.rem(place, 2) == 0
    for j in range(HALF // CHUNK):
        cols = pl.ds(j * CHUNK, CHUNK)
        spread = spread_matrix(lax.rem(place, 2) * (H // 2) + j * (CHUNK // P_SIZE))
        chip = jnp.where(place >= 2, h_ref[:, cols].astype(F32), 0.0)
        middle = dot(rows_ref[...], spread)[0:1] * chip + early_ref[:, cols].astype(F32)
        keep_ref[:, cols] = jnp.where(first, chip, middle).astype(BF16)
        send_ref[:, cols] = jnp.where(first, middle, chip).astype(BF16)


def finish_kernel(near_ref, far_ref, bc_ref, h_own_ref, h_other_ref, gain_ref, out_hbm, g_ref, out_ref, sems):
    core = lax.rem(lax.axis_index("seq"), 2)
    n = bc_ref.shape[0]
    squares = jnp.zeros((n, CHUNK), F32)
    c_vals = bc_ref[:, N:]
    for side in range(2):
        h_ref = (h_own_ref, h_other_ref)[side]
        for j in range(HALF // CHUNK):
            cols = pl.ds(j * CHUNK, CHUNK)
            g = near_ref[side, :, cols] + far_ref[side, :, cols] * dot(c_vals, h_ref[:, cols])
            g_ref[side, :, cols] = g
            squares += g * g
    scale = lax.rsqrt(jnp.sum(squares, axis=-1, keepdims=True) * (1.0 / D) + 1e-05)
    tile = n // 4
    copies = []
    for t in range(4):
        rows = pl.ds(t * tile, tile)
        for side in range(2):
            half = core if side == 0 else 1 - core
            for j in range(HALF // CHUNK):
                cols = pl.ds(pl.multiple_of(half * HALF + j * CHUNK, CHUNK), CHUNK)
                g = g_ref[side, rows, pl.ds(j * CHUNK, CHUNK)]
                out_ref[rows, cols] = (g * scale[t * tile : (t + 1) * tile] * gain_ref[:, cols]).astype(BF16)
        copies.append(pltpu.make_async_copy(out_ref.at[rows], out_hbm.at[0, rows], sems.at[t]))
        copies[t].start()
    for copy in copies:
        copy.wait()


def join_kernel(mark_ref, a_ref, b_ref, out_ref):
    row = lax.broadcasted_iota(jnp.int32, out_ref.shape, 0)
    out_ref[...] = jnp.where(row == 0, a_ref[...] + b_ref[...], mark_ref[...])


def join(mark, a, b):
    out = jax.ShapeDtypeStruct(a.shape, a.dtype)
    return pl.pallas_call(
        join_kernel, out_shape=out, in_specs=[VMEM] * 3, out_specs=VMEM, compiler_params=params(8), name="join"
    )(mark, a, b)


def halves_kernel(
    kept_x_ref, came_x_ref, kept_z_ref, came_z_ref, mark_ref, x_mark_ref, z_mark_ref, sum_ref,
    keep_a_ref, send_a_ref, keep_b_ref, send_b_ref,
    *, sequences,
):
    ones = sum_ref[0:1] + z_mark_ref[0:1]

    def weight(mark):
        return mark / ones - (1.0 - mark) / (sequences - ones)

    own = weight(mark_ref[1:2])
    place = lax.axis_index("dp")
    x_bit = lax.rem(place, 2)
    z_bit = lax.rem(place // 2, 2)
    work = (
        (kept_x_ref, came_x_ref, x_mark_ref, z_bit, keep_a_ref, send_a_ref),
        (kept_z_ref, came_z_ref, z_mark_ref, x_bit, keep_b_ref, send_b_ref),
    )
    for kept, came, other_mark, bit, keep, send in work:
        other = weight(other_mark[1:2])
        part = keep.shape[0]
        mine = pl.ds(pl.multiple_of(bit * part, 8), part)
        yours = pl.ds(pl.multiple_of((1 - bit) * part, 8), part)
        send[...] = own * kept[yours] + other * came[yours]
        keep[...] = own * kept[mine] + other * came[mine]


def chunks_kernel(keep_a_ref, came_a_ref, keep_b_ref, came_b_ref, keep_ref, core_ref, same_ref, cross_ref):
    place = lax.axis_index("seq")
    part = keep_ref.shape[0]
    upper = lax.rem(place // 2, 2) == 0
    first = lax.rem(place, 2) == 0
    rows = jnp.concatenate([keep_a_ref[...] + came_a_ref[...], keep_b_ref[...] + came_b_ref[...]], axis=0)
    here = jnp.where(upper, rows[: 2 * part], rows[2 * part :])
    there = jnp.where(upper, rows[2 * part :], rows[: 2 * part])
    keep_ref[...] = jnp.where(first, here[:part], here[part:])
    core_ref[...] = jnp.where(first, here[part:], here[:part])
    same_ref[...] = jnp.where(first, there[:part], there[part:])
    cross_ref[...] = jnp.where(first, there[part:], there[:part])


def planes_kernel(own_ref, same_ref, core_ref, cross_ref, keep_ref, send_ref):
    stays = lax.rem(lax.axis_index("dp") // 4, 2) == lax.rem(lax.axis_index("seq"), 2)
    own = own_ref[...] + same_ref[...]
    other = core_ref[...] + cross_ref[...]
    keep_ref[...] = jnp.where(stays, own, other)
    send_ref[...] = jnp.where(stays, other, own)


def sum_kernel(keep_ref, came_ref, out_ref):
    out_ref[...] = keep_ref[...] + came_ref[...]


def swap(k):
    return [(i, i ^ k) for i in range(8)]


def small_call(kernel, name, counts, *args):
    parts = tuple(jax.ShapeDtypeStruct((rows, N), F32) for rows in counts)
    return pl.pallas_call(
        kernel, out_shape=parts, in_specs=[VMEM] * len(args), out_specs=(VMEM,) * len(parts), compiler_params=params(8), name=name
    )(*args)


def on_device(xbc, gate_input, dt_raw, conv_weight, conv_bias, dt_bias, a_rate, d_skip, norm_gain, labels, readout):
    n = xbc.shape[1]
    places = lax.axis_size("seq")
    sequences = lax.axis_size("dp")
    chips = places // 2
    place = lax.axis_index("seq")
    core = place % 2
    split = sequences == 8 and places == 4
    pair = [(i, i ^ 1) for i in range(places)]
    shape = jax.ShapeDtypeStruct

    one_back = [(i, i ^ 3) for i in range(4)] if chips == 2 else [(i, (i + 1) % places) for i in range(places)]
    two_back = [(i, (i + 2) % places) for i in range(places)]
    dt_turned = jnp.swapaxes(dt_raw, 1, 2)
    dt_other = lax.ppermute(dt_turned, "seq", pair)
    xbc_other = lax.ppermute(xbc, "seq", pair)
    xbc_here = in_hbm(xbc)
    payload = shape((4 * SIDE // 128, 128 + n), BF16)
    tail_a, tail_b, dt_own, columns, points = pl.pallas_call(
        tail_kernel,
        out_shape=(payload, payload, shape((1, H, n), BF16), shape((H, 8), F32), shape((8, 128), jnp.int32)),
        in_specs=[HBM] * 6,
        out_specs=(VMEM,) * 5,
        scratch_shapes=[pltpu.VMEM((EDGE, CH), BF16)]
        + [pltpu.VMEM((1, H), F32)] * 3
        + [pltpu.SMEM((1, R), jnp.int32), pltpu.SemaphoreType.DMA((6,))],
        compiler_params=params(8),
        name="tail",
    )(xbc_here, in_hbm(dt_turned), in_hbm(dt_bias), in_hbm(a_rate), in_hbm(d_skip), in_hbm(readout))
    edge_a = lax.ppermute(tail_a, "seq", one_back)
    edge_b = lax.ppermute(tail_b, "seq", two_back)
    mark = pl.pallas_call(
        mark_kernel, out_shape=shape((8, N), F32), in_specs=[SMEM], out_specs=VMEM, compiler_params=params(8), name="mark"
    )(tied(labels, points))

    ws, wr, e, rows, x, taps, bias, *small = pl.pallas_call(
        steps_kernel,
        out_shape=(
            shape((2 * n, 128), F32), shape((2 * n, 128), F32), shape((n, 128), F32), shape((16, 128), BF16),
            shape((n, SIDE), BF16), shape((KW, SIDE), F32), shape((1, SIDE), F32),
        ) + ((shape((8, 128), F32),) if chips != 2 else ()),
        in_specs=[VMEM] * 4 + [HBM] * 3,
        out_specs=(VMEM,) * (8 if chips != 2 else 7),
        scratch_shapes=[pltpu.SemaphoreType.DMA((6,))],
        compiler_params=params(16),
        cost_estimate=cost(30 * n * n * 1024, 8 * n * 256),
        name="steps",
    )(dt_own, dt_other, columns, points, xbc_here, in_hbm(conv_weight), in_hbm(conv_bias))

    if chips == 2:
        later = pl.pallas_call(
            later_kernel,
            out_shape=shape((16, 128), BF16),
            in_specs=[VMEM] * 4,
            out_specs=VMEM,
            compiler_params=params(16),
            cost_estimate=cost(10 * n * n * 1024, 8 * n * 256),
            name="later",
        )(edge_b, edge_a, tied(columns, ws), points)
    else:
        small = small[0]
        later = jnp.zeros_like(small)
        for step in range(chips - 1):
            out = small.at[0:1].add(small[1:2] * later[0:1])
            later = lax.ppermute(out, "seq", [(i, (i - 2) % places) for i in range(places)])
            later = jnp.where(place < places - 2, later, 0.0)
        later = pack(jnp.broadcast_to(later[0, :H, None], (H, 16)))

    if split:
        ones = join(tied(mark, later), mark, lax.ppermute(mark, "dp", swap(4)))
        later = tied(later, ones)

    read_rows = (2 * LEAD, 2 * LEAD, D // 4 - 2 * LEAD, D // 4 - 2 * LEAD) if split else (HALF,)
    state, early, act_own, act_other, bc, *reads = pl.pallas_call(
        functools.partial(state_kernel, split=split),
        out_shape=(
            shape((N, HALF), BF16), shape((N, HALF), BF16),
            shape((n, HALF), BF16), shape((n, HALF), BF16), shape((n, BC), BF16),
        ) + tuple(shape((count, N), F32) for count in read_rows),
        in_specs=[VMEM] * 10,
        out_specs=(VMEM,) * (5 + len(read_rows)),
        scratch_shapes=[pltpu.VMEM((n, BC), BF16), pltpu.VMEM((HALF, N), F32)],
        compiler_params=params(24),
        cost_estimate=cost(50 * n * n * D, 4 * 2 * n * SIDE),
        name="states",
    )(x, xbc_other, edge_a, edge_b, ws, wr, rows, later, taps, bias)

    h = state
    for step in range(chips - 1):
        if step:
            scale = jnp.repeat(lax.dynamic_slice_in_dim(small[1, :H], core * (H // 2), H // 2), P_SIZE)
            h = (h.astype(F32) * scale + state.astype(F32)).astype(BF16)
        h = lax.ppermute(h, "seq", two_back)
        if chips > 2:
            h = jnp.where(place >= 2, h, jnp.zeros_like(h))
    act_in = lax.ppermute(act_other, "seq", pair)
    if split:
        keep_x, send_x, keep_z, send_z = reads
        x_mark = lax.ppermute(tied(ones, send_x), "dp", swap(1))
        came_x = lax.ppermute(send_x, "dp", swap(1))
        came_z = lax.ppermute(send_z, "dp", swap(2))
        ones = join(mark, ones, x_mark)
        z_mark = lax.ppermute(ones, "dp", swap(2))

    near, reach = pl.pallas_call(
        diagonal_kernel,
        out_shape=(shape((2, n, HALF), F32), shape((2, n, HALF), F32)),
        in_specs=[VMEM] * 7,
        out_specs=(VMEM, VMEM),
        compiler_params=params(24),
        cost_estimate=cost(28 * n * n * D, 4 * n * D),
        name="diagonal",
    )(act_own, act_in, bc, ws, e, rows, gate_input)
    if split:
        keep_x, near, reach = lax.optimization_barrier((keep_x, near, reach))
        keep_a, send_a, keep_b, send_b = small_call(
            functools.partial(halves_kernel, sequences=float(sequences)), "halves", (LEAD, LEAD, D // 8 - LEAD, D // 8 - LEAD),
            keep_x, came_x, keep_z, came_z, mark, x_mark, z_mark, ones,
        )
        came_a = lax.ppermute(send_a, "dp", swap(2))
        came_b = lax.ppermute(send_b, "dp", swap(1))
        keep, to_core, to_same, to_cross = small_call(chunks_kernel, "chunks", (D // 32,) * 4, keep_a, came_a, keep_b, came_b)
        from_core = lax.ppermute(to_core, "seq", pair)
        from_same = lax.ppermute(to_same, "seq", [(i, i ^ 2) for i in range(places)])
        from_cross = lax.ppermute(to_cross, "seq", [(i, i ^ 3) for i in range(places)])
    h = tied(h, keep) if split else h
    h_own, h_send = pl.pallas_call(
        carry_kernel, out_shape=(shape((N, HALF), BF16),) * 2, in_specs=[VMEM] * 3, out_specs=(VMEM,) * 2, compiler_params=params(8), name="carry",
        cost_estimate=cost(8 * n * n * D, 4 * N * D),
    )(h, early, rows)
    h_other = lax.ppermute(h_send, "seq", pair)
    layer_out = pl.pallas_call(
        finish_kernel,
        out_shape=shape((1, n, D), BF16),
        in_specs=[VMEM] * 6,
        out_specs=HBM,
        scratch_shapes=[pltpu.VMEM((2, n, HALF), F32), pltpu.VMEM((n, D), BF16), pltpu.SemaphoreType.DMA((4,))],
        compiler_params=params(24),
        cost_estimate=cost(20 * n * n * D, 12 * n * D),
        name="finish",
    )(near, reach, bc, h_own, h_other, norm_gain[None])
    if split:
        keep, send = small_call(planes_kernel, "planes", (D // 32,) * 2, keep, from_same, from_core, from_cross)
        came = lax.ppermute(send, "dp", swap(4))
        keep, layer_out = lax.optimization_barrier((keep, layer_out))
        steering = small_call(sum_kernel, "sum", (D // 32,), keep, came)[0]
    else:
        ones = lax.psum(mark[0, 0], "dp")
        weight = mark[0, 0] / ones - (1.0 - mark[0, 0]) / (sequences - ones)
        whole = lax.dynamic_update_slice_in_dim(jnp.zeros((D, N), F32), weight * reads[0], core * HALF, 0)
        steering = lax.psum_scatter(whole, ("dp", "seq"), scatter_dimension=0, tiled=True)
    return (layer_out, steering)


def solution(mesh):
    return jax.shard_map(
        on_device,
        mesh=mesh,
        in_specs=(
            P("dp", "seq", None),
            P("dp", "seq", None),
            P("dp", "seq", None),
            P(),
            P(),
            P(),
            P(),
            P(),
            P(),
            P("dp"),
            P("dp", None),
        ),
        out_specs=(P("dp", "seq", None), P(("dp", "seq"), None)),
        check_vma=False,
    )
```

```python
import functools

import jax
import jax.numpy as jnp
from jax import lax
from jax.experimental import pallas as pl
from jax.experimental.pallas import tpu as pltpu
from jax.sharding import PartitionSpec as P

H = 40
P_SIZE = 64
N = 128
KW = 4
R = 4
D = H * P_SIZE
HALF = D // 2
BC = 2 * N
SIDE = HALF + BC
CH = D + BC
CHUNK = 256
EDGE = 16
LEAD = 192
F32 = jnp.float32
BF16 = jnp.bfloat16
VMEM = pl.BlockSpec(memory_space=pltpu.VMEM)
SMEM = pl.BlockSpec(memory_space=pltpu.SMEM)
ANY = pl.BlockSpec(memory_space=pl.ANY)
HBM = pl.BlockSpec(memory_space=pltpu.HBM)
MIB = 1024 * 1024


def params(mib):
    return pltpu.CompilerParams(vmem_limit_bytes=mib * MIB)


def cost(flops, read):
    return pl.CostEstimate(flops=flops, bytes_accessed=read, transcendentals=0)


def in_hbm(x):
    return pltpu.with_memory_space_constraint(x, pltpu.HBM)


def tied(x, *others):
    return lax.optimization_barrier((x,) + others)[0]


def dot(a, b):
    return jnp.dot(a, b, preferred_element_type=F32)


def pack(w):
    high = w.astype(BF16).astype(F32)
    gap = jnp.zeros((64 - H, w.shape[1]), F32)
    return jnp.concatenate([high, gap, w - high, gap], axis=0).astype(BF16).T


def stand(w):
    return jnp.concatenate([w, jnp.zeros((128 - H, w.shape[1]), F32)], axis=0).T


def widen(w, first_head):
    head = lax.broadcasted_iota(jnp.int32, w.shape, 1) // P_SIZE + first_head
    picked = [jnp.take_along_axis(w, head + i, axis=1) for i in range(0, CHUNK // P_SIZE, 128 // P_SIZE)]
    return jnp.concatenate(picked, axis=1)


def beside(columns):
    lane = lax.broadcasted_iota(jnp.int32, (H, 128), 1)
    table = jnp.zeros((H, 128), F32)
    for i, column in enumerate(columns):
        table = jnp.where(lane == i, column, table)
    return table


def turned(rows):
    table = jnp.concatenate(list(rows) + [jnp.zeros((8 - len(rows), H), F32)], axis=0)
    return jnp.concatenate([table, jnp.zeros((8, 128 - H), F32)], axis=1).T[:H]


def spread_matrix(first_head):
    row = lax.broadcasted_iota(jnp.int32, (128, CHUNK), 0)
    lane = lax.broadcasted_iota(jnp.int32, (128, CHUNK), 1)
    hit = (row & 63) == first_head + lane // P_SIZE
    return jnp.where(hit, 1.0, 0.0).astype(BF16)


def silu(v):
    half = 0.5 * v
    return half + half * jnp.tanh(half)


def fetch(pairs, sems):
    copies = [pltpu.make_async_copy(source, to, sems.at[i]) for i, (source, to) in enumerate(pairs)]
    for copy in copies:
        copy.start()
    for copy in copies:
        copy.wait()


def step_sizes(raw, bias):
    raw = raw + bias
    return jnp.maximum(raw, 0.0) + jnp.log1p(jnp.exp(-jnp.abs(raw)))


def running_sums(steps):
    n = steps[0].shape[1]
    row = lax.broadcasted_iota(jnp.int32, (n, n), 0)
    lane = lax.broadcasted_iota(jnp.int32, (n, n), 1)
    upper = jnp.where(row <= lane, 1.0, 0.0).astype(BF16)
    parts = []
    for step in steps:
        high = step.astype(BF16).astype(F32)
        middle = (step - high).astype(BF16).astype(F32)
        parts += [high, middle, step - high - middle]
    sums = dot(jnp.concatenate(parts, axis=0).astype(BF16), upper)
    return [sums[i : i + H] + (sums[i + H : i + 2 * H] + sums[i + 2 * H : i + 3 * H]) for i in range(0, 3 * H * len(steps), 3 * H)]


def read_levels(points, base, total):
    n = total[0].shape[1]
    index = lax.broadcasted_iota(jnp.int32, (H, n), 1)
    found = []
    for r in range(R):
        at = points[r : r + 1, 0:1] - base
        inside = jnp.where((at >= 0) & (at < 2 * n), 1.0, 0.0)
        level = jnp.zeros((H, n), F32)
        for block in range(2):
            level += jnp.where(index + block * n == at, total[block], 0.0)
        found.append((at, inside, jnp.sum(level, axis=1, keepdims=True)))
    return found


def carry_of(found):
    carry = jnp.zeros((H, 1), F32)
    for _, inside, level in found:
        carry += inside * jnp.exp(level)
    return carry * (1.0 / R)


def tail_kernel(
    xbc_hbm, dt_hbm, bias_hbm, rate_hbm, skip_hbm, points_hbm, out_a_ref, out_b_ref, dt_ref, columns_ref, points_ref,
    rows_ref, bias_ref, rate_ref, skip_ref, spot_ref, sems,
):
    n = xbc_hbm.shape[1]
    rows = xbc_hbm.at[0, pl.ds(n - EDGE, EDGE)]
    fetch(
        (
            (dt_hbm, dt_ref), (rows, rows_ref), (points_hbm, spot_ref),
            (bias_hbm, bias_ref.at[0]), (rate_hbm, rate_ref.at[0]), (skip_hbm, skip_ref.at[0]),
        ),
        sems,
    )
    tail = rows_ref[...].astype(F32)[EDGE - 8 :]
    steps = jnp.concatenate([dt_ref[0].astype(F32), jnp.zeros((4 * SIDE // 128 - H, n), F32)], axis=0).astype(BF16)
    upper = lax.broadcasted_iota(jnp.int32, (8, 128), 0) < 4
    for half, out_ref in enumerate((out_a_ref, out_b_ref)):
        pieces = [half * HALF + i for i in range(0, HALF, 128)] + [D + i for i in range(0, BC, 128)]
        pieces = [tail[:, i : i + 128] for i in pieces]
        stack = [jnp.where(upper, pltpu.roll(pieces[i], 4, 0), pieces[i + 1]) for i in range(0, len(pieces), 2)]
        out_ref[:, :128] = jnp.concatenate(stack, axis=0).astype(BF16)
        out_ref[:, 128:] = steps
    columns_ref[...] = turned((bias_ref[...], rate_ref[...], skip_ref[...]))
    spot = lax.broadcasted_iota(jnp.int32, points_ref.shape, 0)
    points = jnp.zeros(points_ref.shape, jnp.int32)
    for r in range(R):
        points = jnp.where(spot == r, spot_ref[0, r], points)
    points_ref[...] = points


def mark_kernel(label_ref, mark_ref):
    mark_ref[...] = jnp.zeros(mark_ref.shape, F32) + label_ref[0].astype(F32)


def steps_kernel(
    own_ref, other_ref, columns_ref, points_ref, xbc_hbm, conv_w_hbm, conv_b_hbm,
    ws_ref, wr_ref, e_ref, rows_ref, x_ref, taps_ref, bias_ref, *rest,
):
    place = lax.axis_index("seq")
    core = lax.rem(place, 2)
    n = own_ref.shape[2]
    sems = rest[-1]
    col = pl.multiple_of(core * HALF, 128)
    copies = []
    for from_at, to_at, width in ((D, HALF, BC), (col, 0, HALF)):
        here, there = pl.ds(from_at, width), pl.ds(to_at, width)
        copies.append((xbc_hbm.at[0, :, here], x_ref.at[:, there]))
        copies.append((conv_w_hbm.at[:, here], taps_ref.at[:, there]))
        copies.append((conv_b_hbm.at[here], bias_ref.at[0, there]))
    copies = [pltpu.make_async_copy(source, to, sems.at[i]) for i, (source, to) in enumerate(copies)]
    for copy in copies:
        copy.start()
    own = own_ref[0].astype(F32)
    other = other_ref[0].astype(F32)
    bias, rate, skip = columns_ref[:, 0:1], columns_ref[:, 1:2], columns_ref[:, 2:3]
    first = core == 0
    dts = [step_sizes(jnp.where(first == (block == 0), own, other), bias) for block in range(2)]
    cums = running_sums([-rate * dt for dt in dts])
    ends = [cum[:, n - 1 : n] for cum in cums]

    def store(ref, values):
        ref[:n] = stand(jnp.where(first, values[0], values[1]))
        ref[n:] = stand(jnp.where(first, values[1], values[0]))

    store(ws_ref, [dts[block] * jnp.exp(ends[block] - cums[block]) for block in range(2)])
    total = [cums[0], ends[0] + cums[1]]
    index = lax.broadcasted_iota(jnp.int32, (H, n), 1)
    weight = [jnp.zeros((H, n), F32), jnp.zeros((H, n), F32)]
    found = read_levels(points_ref[...], (place - core) * n, total)
    for at, inside, level in found:
        for block in range(2):
            seen = jnp.where(index + block * n <= at, jnp.exp(jnp.minimum(level - total[block], 0.0)), 0.0)
            weight[block] += inside * seen
    store(wr_ref, [weight[block] * dts[block] * (1.0 / R) for block in range(2)])
    e_ref[...] = stand(jnp.exp(jnp.where(first, cums[0], cums[1])))
    decay = [jnp.exp(end) for end in ends]
    back = jnp.exp(-jnp.where(first, ends[0], ends[1]))
    rows_ref[...] = pack(beside((decay[0], decay[1], skip, back)))[0:16]
    if len(rest) > 1:
        whole = beside((carry_of(found), jnp.exp(ends[0] + ends[1])))
        rest[0][...] = jnp.concatenate([whole, jnp.zeros((128 - H, 128), F32)], axis=0).T[0:8]
    for copy in copies:
        copy.wait()


def later_kernel(same_ref, cross_ref, columns_ref, points_ref, later_ref):
    place = lax.axis_index("seq")
    core = lax.rem(place, 2)
    n = same_ref.shape[1] - 128
    same, cross = same_ref[:, 128:].astype(F32)[:H], cross_ref[:, 128:].astype(F32)[:H]
    bias, rate = columns_ref[:, 0:1], columns_ref[:, 1:2]
    raws = [jnp.where((core == 0) == (block == 0), same, cross) for block in range(2)]
    cums = running_sums([-rate * step_sizes(raw, bias) for raw in raws])
    total = [cums[0], cums[0][:, n - 1 : n] + cums[1]]
    carry = carry_of(read_levels(points_ref[...], 2 * n, total))
    later_ref[...] = pack(beside((jnp.where(place < 2, carry, 0.0),)))[0:16]


def state_kernel(
    x_ref, other_ref, edge_a_ref, edge_b_ref, ws_ref, wr_ref, rows_ref, later_ref, taps_ref, bias_ref, mark_ref,
    state_ref, early_ref, act_own_ref, act_other_ref, bc_ref, *rest,
    split,
):
    reads = rest[:-2]
    bc_other_ref, read_ref = rest[-2:]
    place = lax.axis_index("seq")
    core = lax.rem(place, 2)
    first = core == 0
    n = x_ref.shape[0]
    started = jnp.where(place >= 2, 1.0, 0.0)
    edge = jnp.where(first, edge_a_ref[:, :128].astype(F32), edge_b_ref[:, :128].astype(F32)) * started
    tile = 128

    def before(at):
        pieces = []
        for i in range(at // 128, (at + CHUNK) // 128):
            piece = edge[i // 2 * 8 : i // 2 * 8 + 8]
            pieces.append(pltpu.roll(piece, 4, 0) if i % 2 == 0 else piece)
        return jnp.concatenate(pieces, axis=1)

    def convolve(at, act_refs, to):
        cols = pl.ds(at, CHUNK)
        from_cols = pl.ds(D + at - HALF if at >= HALF else pl.multiple_of(core * HALF + at, 128), CHUNK)
        taps = taps_ref[:, cols]
        bias = bias_ref[:, cols]

        def rows(side, start, count):
            return (x_ref[start : start + count, cols] if side == 0 else other_ref[0, start : start + count, from_cols]).astype(F32)

        ends = [rows(side, n - EDGE, EDGE)[EDGE - 8 :] for side in range(2)]
        chip = before(at)
        for side, act_ref in enumerate(act_refs):
            ahead = jnp.where(first == (side == 0), chip, ends[1 - side])
            for t in range(n // tile):
                if t == 0:
                    seen = jnp.concatenate([ahead, rows(side, 0, tile)], axis=0)
                else:
                    seen = rows(side, t * tile - EDGE, tile + EDGE)[EDGE - 8 :]
                last = pltpu.roll(seen, 1, 0)
                pair = taps[1:2] * seen + taps[0:1] * last
                total = bias + taps[3:4] * seen[8:] + taps[2:3] * last[8:]
                total += pltpu.roll(pair, 2, 0)[8:]
                act_ref[t * tile : (t + 1) * tile, to : to + CHUNK] = silu(total).astype(BF16)

    convolve(HALF, (bc_ref, bc_other_ref), 0)
    b_turned = [ref[:, :N].T for ref in (bc_ref, bc_other_ref)]
    both = jnp.concatenate(b_turned, axis=1)
    rows = jnp.concatenate([rows_ref[...], later_ref[...]], axis=0)

    for j in range(HALF // CHUNK):
        at = j * CHUNK
        cols = pl.ds(at, CHUNK)
        convolve(at, (act_own_ref, act_other_ref), at)
        head = core * (H // 2) + j * (CHUNK // P_SIZE)
        spread = spread_matrix(head)
        wide = dot(rows, spread)
        table, ahead = wide[:16], wide[16:17]
        act = jnp.concatenate([act_own_ref[:, cols], act_other_ref[:, cols]], axis=0).astype(F32)
        weighted = (act * widen(ws_ref[...], head)).astype(BF16)
        own = dot(b_turned[0], weighted[:n])
        other = dot(b_turned[1], weighted[n:])
        state = jnp.where(first, table[1:2], 1.0) * own + jnp.where(first, 1.0, table[1:2]) * other
        early_ref[:, cols] = jnp.where(first, own, other).astype(BF16)
        state_ref[:, cols] = state.astype(BF16)
        read = act * widen(wr_ref[...], head)
        high = read.astype(BF16)
        low = (read - high.astype(F32)).astype(BF16)
        seen = dot(both, high) + dot(both, low) + ahead * state
        read_ref[pl.ds(at, CHUNK)] = seen.T

    if split:
        part = D // 8
        x_bit = lax.rem(lax.axis_index("dp"), 2)
        z_bit = lax.rem(lax.axis_index("dp") // 2, 2)

        def rows(z, x, start, count):
            return read_ref[pl.ds(pl.multiple_of((2 * z + x) * part + start, 8), count)]

        rest = part - LEAD
        for q in range(2):
            here = slice(q * LEAD, (q + 1) * LEAD)
            reads[0][here] = rows(q, x_bit, 0, LEAD)
            reads[1][here] = rows(q, 1 - x_bit, 0, LEAD)
            here = slice(q * rest, (q + 1) * rest)
            reads[2][here] = rows(z_bit, q, LEAD, rest)
            reads[3][here] = rows(1 - z_bit, q, LEAD, rest)
        reads[1][2 * LEAD :] = mark_ref[...]
        reads[3][2 * rest :] = mark_ref[...]
    else:
        reads[0][...] = read_ref[...]


def diagonal_kernel(act_own_ref, act_other_ref, bc_ref, ws_ref, e_ref, rows_ref, gate_ref, near_ref, far_ref):
    core = lax.rem(lax.axis_index("seq"), 2)
    n = act_own_ref.shape[0]
    scores = lax.dot_general(bc_ref[:, N:], bc_ref[:, :N], (((1,), (1,)), ((), ())), preferred_element_type=F32)
    row = lax.broadcasted_iota(jnp.int32, (n, n), 0)
    lane = lax.broadcasted_iota(jnp.int32, (n, n), 1)
    masked = jnp.where(row >= lane, scores, 0.0).astype(BF16)
    ws = ws_ref[:n]
    for side, source in enumerate((act_own_ref, act_other_ref)):
        half = core if side == 0 else 1 - core

        @pl.loop(0, HALF // CHUNK, unroll=True)
        def _(j):
            at = pl.multiple_of(j * CHUNK, CHUNK)
            cols = pl.ds(at, CHUNK)
            head = half * (H // 2) + j * (CHUNK // P_SIZE)
            spread = spread_matrix(head)
            act = source[:, cols].astype(F32)
            weighted = (act * widen(ws, head)).astype(BF16)
            table = dot(rows_ref[...], spread)
            decay = widen(e_ref[...], head)
            value = decay * (table[3:4] * dot(masked, weighted)) + table[2:3] * act
            gate = silu(gate_ref[0, :, pl.ds(pl.multiple_of(half * HALF + at, CHUNK), CHUNK)].astype(F32))
            near_ref[side, :, cols] = value * gate
            far_ref[side, :, cols] = decay * gate


def carry_kernel(h_ref, early_ref, rows_ref, keep_ref, send_ref):
    place = lax.axis_index("seq")
    first = lax.rem(place, 2) == 0
    for j in range(HALF // CHUNK):
        cols = pl.ds(j * CHUNK, CHUNK)
        spread = spread_matrix(lax.rem(place, 2) * (H // 2) + j * (CHUNK // P_SIZE))
        chip = jnp.where(place >= 2, h_ref[:, cols].astype(F32), 0.0)
        middle = dot(rows_ref[...], spread)[0:1] * chip + early_ref[:, cols].astype(F32)
        keep_ref[:, cols] = jnp.where(first, chip, middle).astype(BF16)
        send_ref[:, cols] = jnp.where(first, middle, chip).astype(BF16)


def finish_kernel(near_ref, far_ref, bc_ref, h_own_ref, h_other_ref, gain_ref, out_hbm, g_ref, out_ref, sems):
    core = lax.rem(lax.axis_index("seq"), 2)
    n = bc_ref.shape[0]
    squares = jnp.zeros((n, CHUNK), F32)
    c_vals = bc_ref[:, N:]
    for side in range(2):
        h_ref = (h_own_ref, h_other_ref)[side]
        for j in range(HALF // CHUNK):
            cols = pl.ds(j * CHUNK, CHUNK)
            g = near_ref[side, :, cols] + far_ref[side, :, cols] * dot(c_vals, h_ref[:, cols])
            g_ref[side, :, cols] = g
            squares += g * g
    scale = lax.rsqrt(jnp.sum(squares, axis=-1, keepdims=True) * (1.0 / D) + 1e-05)
    tile = n // 4
    copies = []
    for t in range(4):
        rows = pl.ds(t * tile, tile)
        for side in range(2):
            half = core if side == 0 else 1 - core
            for j in range(HALF // CHUNK):
                cols = pl.ds(pl.multiple_of(half * HALF + j * CHUNK, CHUNK), CHUNK)
                g = g_ref[side, rows, pl.ds(j * CHUNK, CHUNK)]
                out_ref[rows, cols] = (g * scale[t * tile : (t + 1) * tile] * gain_ref[:, cols]).astype(BF16)
        copies.append(pltpu.make_async_copy(out_ref.at[rows], out_hbm.at[0, rows], sems.at[t]))
        copies[t].start()
    for copy in copies:
        copy.wait()


def join_kernel(mark_ref, a_ref, b_ref, out_ref):
    row = lax.broadcasted_iota(jnp.int32, out_ref.shape, 0)
    out_ref[...] = jnp.where(row == 0, a_ref[...] + b_ref[...], mark_ref[...])


def join(mark, a, b):
    out = jax.ShapeDtypeStruct(a.shape, a.dtype)
    return pl.pallas_call(
        join_kernel, out_shape=out, in_specs=[VMEM] * 3, out_specs=VMEM, compiler_params=params(8), name="join"
    )(mark, a, b)


def halves_kernel(
    kept_x_ref, came_x_ref, kept_z_ref, came_z_ref, mark_ref, across_ref,
    keep_a_ref, send_a_ref, keep_b_ref, send_b_ref,
    *, sequences,
):
    x_mark_ref = came_x_ref.at[kept_x_ref.shape[0] :]
    z_mark_ref = came_z_ref.at[kept_z_ref.shape[0] :]
    ones = (mark_ref[0:1] + x_mark_ref[0:1]) + (z_mark_ref[0:1] + across_ref[0:1])

    def weight(mark):
        return mark / ones - (1.0 - mark) / (sequences - ones)

    own = weight(mark_ref[1:2])
    place = lax.axis_index("dp")
    x_bit = lax.rem(place, 2)
    z_bit = lax.rem(place // 2, 2)
    work = (
        (kept_x_ref, came_x_ref, x_mark_ref, z_bit, keep_a_ref, send_a_ref),
        (kept_z_ref, came_z_ref, z_mark_ref, x_bit, keep_b_ref, send_b_ref),
    )
    for kept, came, other_mark, bit, keep, send in work:
        other = weight(other_mark[1:2])
        part = keep.shape[0]
        mine = pl.ds(pl.multiple_of(bit * part, 8), part)
        yours = pl.ds(pl.multiple_of((1 - bit) * part, 8), part)
        send[...] = own * kept[yours] + other * came[yours]
        keep[...] = own * kept[mine] + other * came[mine]


def chunks_kernel(keep_a_ref, came_a_ref, keep_b_ref, came_b_ref, keep_ref, core_ref, same_ref, cross_ref):
    place = lax.axis_index("seq")
    part = keep_ref.shape[0]
    upper = lax.rem(place // 2, 2) == 0
    first = lax.rem(place, 2) == 0
    rows = jnp.concatenate([keep_a_ref[...] + came_a_ref[...], keep_b_ref[...] + came_b_ref[...]], axis=0)
    here = jnp.where(upper, rows[: 2 * part], rows[2 * part :])
    there = jnp.where(upper, rows[2 * part :], rows[: 2 * part])
    keep_ref[...] = jnp.where(first, here[:part], here[part:])
    core_ref[...] = jnp.where(first, here[part:], here[:part])
    same_ref[...] = jnp.where(first, there[:part], there[part:])
    cross_ref[...] = jnp.where(first, there[part:], there[:part])


def planes_kernel(own_ref, same_ref, core_ref, cross_ref, keep_ref, send_ref):
    stays = lax.rem(lax.axis_index("dp") // 4, 2) == lax.rem(lax.axis_index("seq"), 2)
    own = own_ref[...] + same_ref[...]
    other = core_ref[...] + cross_ref[...]
    keep_ref[...] = jnp.where(stays, own, other)
    send_ref[...] = jnp.where(stays, other, own)


def sum_kernel(keep_ref, came_ref, out_ref):
    out_ref[...] = keep_ref[...] + came_ref[...]


def swap(k):
    return [(i, i ^ k) for i in range(8)]


def small_call(kernel, name, counts, *args):
    parts = tuple(jax.ShapeDtypeStruct((rows, N), F32) for rows in counts)
    return pl.pallas_call(
        kernel, out_shape=parts, in_specs=[VMEM] * len(args), out_specs=(VMEM,) * len(parts), compiler_params=params(8), name=name
    )(*args)


def on_device(xbc, gate_input, dt_raw, conv_weight, conv_bias, dt_bias, a_rate, d_skip, norm_gain, labels, readout):
    n = xbc.shape[1]
    places = lax.axis_size("seq")
    sequences = lax.axis_size("dp")
    chips = places // 2
    place = lax.axis_index("seq")
    core = place % 2
    split = sequences == 8 and places == 4
    pair = [(i, i ^ 1) for i in range(places)]
    shape = jax.ShapeDtypeStruct

    one_back = [(i, i ^ 3) for i in range(4)] if chips == 2 else [(i, (i + 1) % places) for i in range(places)]
    two_back = [(i, (i + 2) % places) for i in range(places)]
    dt_turned = jnp.swapaxes(dt_raw, 1, 2)
    dt_other = lax.ppermute(dt_turned, "seq", pair)
    xbc_other = lax.ppermute(xbc, "seq", pair)
    xbc_here = in_hbm(xbc)
    payload = shape((4 * SIDE // 128, 128 + n), BF16)
    tail_a, tail_b, dt_own, columns, points = pl.pallas_call(
        tail_kernel,
        out_shape=(payload, payload, shape((1, H, n), BF16), shape((H, 8), F32), shape((8, 128), jnp.int32)),
        in_specs=[HBM] * 6,
        out_specs=(VMEM,) * 5,
        scratch_shapes=[pltpu.VMEM((EDGE, CH), BF16)]
        + [pltpu.VMEM((1, H), F32)] * 3
        + [pltpu.SMEM((1, R), jnp.int32), pltpu.SemaphoreType.DMA((6,))],
        compiler_params=params(8),
        name="tail",
    )(xbc_here, in_hbm(dt_turned), in_hbm(dt_bias), in_hbm(a_rate), in_hbm(d_skip), in_hbm(readout))
    edge_a = lax.ppermute(tail_a, "seq", one_back)
    edge_b = lax.ppermute(tail_b, "seq", two_back)
    mark = pl.pallas_call(
        mark_kernel, out_shape=shape((8, N), F32), in_specs=[SMEM], out_specs=VMEM, compiler_params=params(8), name="mark"
    )(tied(labels, points))

    ws, wr, e, rows, x, taps, bias, *small = pl.pallas_call(
        steps_kernel,
        out_shape=(
            shape((2 * n, 128), F32), shape((2 * n, 128), F32), shape((n, 128), F32), shape((16, 128), BF16),
            shape((n, SIDE), BF16), shape((KW, SIDE), F32), shape((1, SIDE), F32),
        ) + ((shape((8, 128), F32),) if chips != 2 else ()),
        in_specs=[VMEM] * 4 + [HBM] * 3,
        out_specs=(VMEM,) * (8 if chips != 2 else 7),
        scratch_shapes=[pltpu.SemaphoreType.DMA((6,))],
        compiler_params=params(16),
        cost_estimate=cost(30 * n * n * 1024, 8 * n * 256),
        name="steps",
    )(dt_own, dt_other, columns, points, xbc_here, in_hbm(conv_weight), in_hbm(conv_bias))

    if chips == 2:
        later = pl.pallas_call(
            later_kernel,
            out_shape=shape((16, 128), BF16),
            in_specs=[VMEM] * 4,
            out_specs=VMEM,
            compiler_params=params(16),
            cost_estimate=cost(10 * n * n * 1024, 8 * n * 256),
            name="later",
        )(edge_b, edge_a, tied(columns, ws), points)
    else:
        small = small[0]
        later = jnp.zeros_like(small)
        for step in range(chips - 1):
            out = small.at[0:1].add(small[1:2] * later[0:1])
            later = lax.ppermute(out, "seq", [(i, (i - 2) % places) for i in range(places)])
            later = jnp.where(place < places - 2, later, 0.0)
        later = pack(jnp.broadcast_to(later[0, :H, None], (H, 16)))

    if split:
        ones = join(tied(mark, later), mark, lax.ppermute(mark, "dp", swap(4)))
    else:
        ones = mark

    read_rows = (2 * LEAD, 2 * LEAD + 8, D // 4 - 2 * LEAD, D // 4 - 2 * LEAD + 8) if split else (HALF,)
    state, early, act_own, act_other, bc, *reads = pl.pallas_call(
        functools.partial(state_kernel, split=split),
        out_shape=(
            shape((N, HALF), BF16), shape((N, HALF), BF16),
            shape((n, HALF), BF16), shape((n, HALF), BF16), shape((n, BC), BF16),
        ) + tuple(shape((count, N), F32) for count in read_rows),
        in_specs=[VMEM] * 11,
        out_specs=(VMEM,) * (5 + len(read_rows)),
        scratch_shapes=[pltpu.VMEM((n, BC), BF16), pltpu.VMEM((HALF, N), F32)],
        compiler_params=params(24),
        cost_estimate=cost(50 * n * n * D, 4 * 2 * n * SIDE),
        name="states",
    )(x, xbc_other, edge_a, edge_b, ws, wr, rows, later, taps, bias, ones)

    h = state
    for step in range(chips - 1):
        if step:
            scale = jnp.repeat(lax.dynamic_slice_in_dim(small[1, :H], core * (H // 2), H // 2), P_SIZE)
            h = (h.astype(F32) * scale + state.astype(F32)).astype(BF16)
        h = lax.ppermute(h, "seq", two_back)
        if chips > 2:
            h = jnp.where(place >= 2, h, jnp.zeros_like(h))
    act_in = lax.ppermute(act_other, "seq", pair)
    if split:
        keep_x, send_x, keep_z, send_z = reads
        came_x = lax.ppermute(send_x, "dp", swap(1))
        came_z = lax.ppermute(send_z, "dp", swap(2))
        across = lax.ppermute(tied(ones, send_x), "dp", swap(3))

    if split:
        keep_a, send_a, keep_b, send_b = small_call(
            functools.partial(halves_kernel, sequences=float(sequences)), "halves", (LEAD, LEAD, D // 8 - LEAD, D // 8 - LEAD),
            keep_x, came_x, keep_z, came_z, ones, across,
        )
        came_a = lax.ppermute(send_a, "dp", swap(2))
        came_b = lax.ppermute(send_b, "dp", swap(1))
        act_in = tied(act_in, keep_a)
        near, reach = pl.pallas_call(
            diagonal_kernel,
            out_shape=(shape((2, n, HALF), F32), shape((2, n, HALF), F32)),
            in_specs=[VMEM] * 7,
            out_specs=(VMEM, VMEM),
            compiler_params=params(24),
            cost_estimate=cost(28 * n * n * D, 4 * n * D),
            name="diagonal",
        )(act_own, act_in, bc, ws, e, rows, gate_input)
        keep_b, near, reach = lax.optimization_barrier((keep_b, near, reach))
        keep, to_core, to_same, to_cross = small_call(chunks_kernel, "chunks", (D // 32,) * 4, keep_a, came_a, keep_b, came_b)
        from_core = lax.ppermute(to_core, "seq", pair)
        from_same = lax.ppermute(to_same, "seq", [(i, i ^ 2) for i in range(places)])
        from_cross = lax.ppermute(to_cross, "seq", [(i, i ^ 3) for i in range(places)])
    else:
        near, reach = pl.pallas_call(
            diagonal_kernel,
            out_shape=(shape((2, n, HALF), F32), shape((2, n, HALF), F32)),
            in_specs=[VMEM] * 7,
            out_specs=(VMEM, VMEM),
            compiler_params=params(24),
            cost_estimate=cost(28 * n * n * D, 4 * n * D),
            name="diagonal",
        )(act_own, act_in, bc, ws, e, rows, gate_input)
    h = tied(h, keep) if split else h
    h_own, h_send = pl.pallas_call(
        carry_kernel, out_shape=(shape((N, HALF), BF16),) * 2, in_specs=[VMEM] * 3, out_specs=(VMEM,) * 2, compiler_params=params(8), name="carry",
        cost_estimate=cost(8 * n * n * D, 4 * N * D),
    )(h, early, rows)
    h_other = lax.ppermute(h_send, "seq", pair)
    layer_out = pl.pallas_call(
        finish_kernel,
        out_shape=shape((1, n, D), BF16),
        in_specs=[VMEM] * 6,
        out_specs=HBM,
        scratch_shapes=[pltpu.VMEM((2, n, HALF), F32), pltpu.VMEM((n, D), BF16), pltpu.SemaphoreType.DMA((4,))],
        compiler_params=params(24),
        cost_estimate=cost(20 * n * n * D, 12 * n * D),
        name="finish",
    )(near, reach, bc, h_own, h_other, norm_gain[None])
    if split:
        keep, send = small_call(planes_kernel, "planes", (D // 32,) * 2, keep, from_same, from_core, from_cross)
        came = lax.ppermute(send, "dp", swap(4))
        keep, layer_out = lax.optimization_barrier((keep, layer_out))
        steering = small_call(sum_kernel, "sum", (D // 32,), keep, came)[0]
    else:
        ones = lax.psum(mark[0, 0], "dp")
        weight = mark[0, 0] / ones - (1.0 - mark[0, 0]) / (sequences - ones)
        whole = lax.dynamic_update_slice_in_dim(jnp.zeros((D, N), F32), weight * reads[0], core * HALF, 0)
        steering = lax.psum_scatter(whole, ("dp", "seq"), scatter_dimension=0, tiled=True)
    return (layer_out, steering)


def solution(mesh):
    return jax.shard_map(
        on_device,
        mesh=mesh,
        in_specs=(
            P("dp", "seq", None),
            P("dp", "seq", None),
            P("dp", "seq", None),
            P(),
            P(),
            P(),
            P(),
            P(),
            P(),
            P("dp"),
            P("dp", None),
        ),
        out_specs=(P("dp", "seq", None), P(("dp", "seq"), None)),
        check_vma=False,
    )
```

```python
import functools

import jax
import jax.numpy as jnp
from jax import lax
from jax.experimental import pallas as pl
from jax.experimental.pallas import tpu as pltpu
from jax.sharding import PartitionSpec as P

H = 40
P_SIZE = 64
N = 128
KW = 4
R = 4
D = H * P_SIZE
HALF = D // 2
BC = 2 * N
SIDE = HALF + BC
CH = D + BC
CHUNK = 256
EDGE = 16
LEAD = 192
F32 = jnp.float32
BF16 = jnp.bfloat16
VMEM = pl.BlockSpec(memory_space=pltpu.VMEM)
SMEM = pl.BlockSpec(memory_space=pltpu.SMEM)
ANY = pl.BlockSpec(memory_space=pl.ANY)
HBM = pl.BlockSpec(memory_space=pltpu.HBM)
MIB = 1024 * 1024


def params(mib):
    return pltpu.CompilerParams(vmem_limit_bytes=mib * MIB)


def cost(flops, read):
    return pl.CostEstimate(flops=flops, bytes_accessed=read, transcendentals=0)


def in_hbm(x):
    return pltpu.with_memory_space_constraint(x, pltpu.HBM)


def tied(x, *others):
    return lax.optimization_barrier((x,) + others)[0]


def dot(a, b):
    return jnp.dot(a, b, preferred_element_type=F32)


def pack(w):
    high = w.astype(BF16).astype(F32)
    gap = jnp.zeros((64 - H, w.shape[1]), F32)
    return jnp.concatenate([high, gap, w - high, gap], axis=0).astype(BF16).T


def stand(w):
    return jnp.concatenate([w, jnp.zeros((128 - H, w.shape[1]), F32)], axis=0).T


def widen(w, first_head):
    head = lax.broadcasted_iota(jnp.int32, w.shape, 1) // P_SIZE + first_head
    picked = [jnp.take_along_axis(w, head + i, axis=1) for i in range(0, CHUNK // P_SIZE, 128 // P_SIZE)]
    return jnp.concatenate(picked, axis=1)


def beside(columns):
    lane = lax.broadcasted_iota(jnp.int32, (H, 128), 1)
    table = jnp.zeros((H, 128), F32)
    for i, column in enumerate(columns):
        table = jnp.where(lane == i, column, table)
    return table


def turned(rows):
    table = jnp.concatenate(list(rows) + [jnp.zeros((8 - len(rows), H), F32)], axis=0)
    return jnp.concatenate([table, jnp.zeros((8, 128 - H), F32)], axis=1).T[:H]


def spread_matrix(first_head):
    row = lax.broadcasted_iota(jnp.int32, (128, CHUNK), 0)
    lane = lax.broadcasted_iota(jnp.int32, (128, CHUNK), 1)
    hit = (row & 63) == first_head + lane // P_SIZE
    return jnp.where(hit, 1.0, 0.0).astype(BF16)


def silu(v):
    half = 0.5 * v
    return half + half * jnp.tanh(half)


def fetch(pairs, sems):
    copies = [pltpu.make_async_copy(source, to, sems.at[i]) for i, (source, to) in enumerate(pairs)]
    for copy in copies:
        copy.start()
    for copy in copies:
        copy.wait()


def step_sizes(raw, bias):
    raw = raw + bias
    return jnp.maximum(raw, 0.0) + jnp.log1p(jnp.exp(-jnp.abs(raw)))


def running_sums(steps):
    n = steps[0].shape[1]
    row = lax.broadcasted_iota(jnp.int32, (n, n), 0)
    lane = lax.broadcasted_iota(jnp.int32, (n, n), 1)
    upper = jnp.where(row <= lane, 1.0, 0.0).astype(BF16)
    parts = []
    for step in steps:
        high = step.astype(BF16).astype(F32)
        middle = (step - high).astype(BF16).astype(F32)
        parts += [high, middle, step - high - middle]
    sums = dot(jnp.concatenate(parts, axis=0).astype(BF16), upper)
    return [sums[i : i + H] + (sums[i + H : i + 2 * H] + sums[i + 2 * H : i + 3 * H]) for i in range(0, 3 * H * len(steps), 3 * H)]


def read_levels(points, base, total):
    n = total[0].shape[1]
    index = lax.broadcasted_iota(jnp.int32, (H, n), 1)
    found = []
    for r in range(R):
        at = points[r : r + 1, 0:1] - base
        inside = jnp.where((at >= 0) & (at < 2 * n), 1.0, 0.0)
        level = jnp.zeros((H, n), F32)
        for block in range(2):
            level += jnp.where(index + block * n == at, total[block], 0.0)
        found.append((at, inside, jnp.sum(level, axis=1, keepdims=True)))
    return found


def carry_of(found):
    carry = jnp.zeros((H, 1), F32)
    for _, inside, level in found:
        carry += inside * jnp.exp(level)
    return carry * (1.0 / R)


def tail_kernel(
    xbc_hbm, dt_hbm, bias_hbm, rate_hbm, skip_hbm, points_hbm, out_a_ref, out_b_ref, dt_ref, columns_ref, points_ref,
    rows_ref, bias_ref, rate_ref, skip_ref, spot_ref, sems,
):
    n = xbc_hbm.shape[1]
    rows = xbc_hbm.at[0, pl.ds(n - EDGE, EDGE)]
    fetch(
        (
            (dt_hbm, dt_ref), (rows, rows_ref), (points_hbm, spot_ref),
            (bias_hbm, bias_ref.at[0]), (rate_hbm, rate_ref.at[0]), (skip_hbm, skip_ref.at[0]),
        ),
        sems,
    )
    tail = rows_ref[...].astype(F32)[EDGE - 8 :]
    steps = jnp.concatenate([dt_ref[0].astype(F32), jnp.zeros((4 * SIDE // 128 - H, n), F32)], axis=0).astype(BF16)
    upper = lax.broadcasted_iota(jnp.int32, (8, 128), 0) < 4
    for half, out_ref in enumerate((out_a_ref, out_b_ref)):
        pieces = [half * HALF + i for i in range(0, HALF, 128)] + [D + i for i in range(0, BC, 128)]
        pieces = [tail[:, i : i + 128] for i in pieces]
        stack = [jnp.where(upper, pltpu.roll(pieces[i], 4, 0), pieces[i + 1]) for i in range(0, len(pieces), 2)]
        out_ref[:, :128] = jnp.concatenate(stack, axis=0).astype(BF16)
        out_ref[:, 128:] = steps
    columns_ref[...] = turned((bias_ref[...], rate_ref[...], skip_ref[...]))
    spot = lax.broadcasted_iota(jnp.int32, points_ref.shape, 0)
    points = jnp.zeros(points_ref.shape, jnp.int32)
    for r in range(R):
        points = jnp.where(spot == r, spot_ref[0, r], points)
    points_ref[...] = points


def mark_kernel(label_ref, mark_ref):
    mark_ref[...] = jnp.zeros(mark_ref.shape, F32) + label_ref[0].astype(F32)


def steps_kernel(
    own_ref, other_ref, columns_ref, points_ref, xbc_hbm, conv_w_hbm, conv_b_hbm,
    ws_ref, wr_ref, e_ref, rows_ref, x_ref, taps_ref, bias_ref, *rest,
):
    place = lax.axis_index("seq")
    core = lax.rem(place, 2)
    n = own_ref.shape[2]
    sems = rest[-1]
    col = pl.multiple_of(core * HALF, 128)
    copies = []
    for from_at, to_at, width in ((D, HALF, BC), (col, 0, HALF)):
        here, there = pl.ds(from_at, width), pl.ds(to_at, width)
        copies.append((xbc_hbm.at[0, :, here], x_ref.at[:, there]))
        copies.append((conv_w_hbm.at[:, here], taps_ref.at[:, there]))
        copies.append((conv_b_hbm.at[here], bias_ref.at[0, there]))
    copies = [pltpu.make_async_copy(source, to, sems.at[i]) for i, (source, to) in enumerate(copies)]
    for copy in copies:
        copy.start()
    own = own_ref[0].astype(F32)
    other = other_ref[0].astype(F32)
    bias, rate, skip = columns_ref[:, 0:1], columns_ref[:, 1:2], columns_ref[:, 2:3]
    first = core == 0
    dts = [step_sizes(jnp.where(first == (block == 0), own, other), bias) for block in range(2)]
    cums = running_sums([-rate * dt for dt in dts])
    ends = [cum[:, n - 1 : n] for cum in cums]

    def store(ref, values):
        ref[:n] = stand(jnp.where(first, values[0], values[1]))
        ref[n:] = stand(jnp.where(first, values[1], values[0]))

    store(ws_ref, [dts[block] * jnp.exp(ends[block] - cums[block]) for block in range(2)])
    total = [cums[0], ends[0] + cums[1]]
    index = lax.broadcasted_iota(jnp.int32, (H, n), 1)
    weight = [jnp.zeros((H, n), F32), jnp.zeros((H, n), F32)]
    found = read_levels(points_ref[...], (place - core) * n, total)
    for at, inside, level in found:
        for block in range(2):
            seen = jnp.where(index + block * n <= at, jnp.exp(jnp.minimum(level - total[block], 0.0)), 0.0)
            weight[block] += inside * seen
    store(wr_ref, [weight[block] * dts[block] * (1.0 / R) for block in range(2)])
    e_ref[...] = stand(jnp.exp(jnp.where(first, cums[0], cums[1])))
    decay = [jnp.exp(end) for end in ends]
    back = jnp.exp(-jnp.where(first, ends[0], ends[1]))
    rows_ref[...] = pack(beside((decay[0], decay[1], skip, back)))[0:16]
    if len(rest) > 1:
        whole = beside((carry_of(found), jnp.exp(ends[0] + ends[1])))
        rest[0][...] = jnp.concatenate([whole, jnp.zeros((128 - H, 128), F32)], axis=0).T[0:8]
    for copy in copies:
        copy.wait()


def later_kernel(same_ref, cross_ref, columns_ref, points_ref, later_ref):
    place = lax.axis_index("seq")
    core = lax.rem(place, 2)
    n = same_ref.shape[1] - 128
    same, cross = same_ref[:, 128:].astype(F32)[:H], cross_ref[:, 128:].astype(F32)[:H]
    bias, rate = columns_ref[:, 0:1], columns_ref[:, 1:2]
    raws = [jnp.where((core == 0) == (block == 0), same, cross) for block in range(2)]
    cums = running_sums([-rate * step_sizes(raw, bias) for raw in raws])
    total = [cums[0], cums[0][:, n - 1 : n] + cums[1]]
    carry = carry_of(read_levels(points_ref[...], 2 * n, total))
    later_ref[...] = pack(beside((jnp.where(place < 2, carry, 0.0),)))[0:16]


def state_kernel(
    x_ref, other_ref, edge_a_ref, edge_b_ref, ws_ref, wr_ref, rows_ref, later_ref, taps_ref, bias_ref, mark_ref,
    state_ref, early_ref, act_own_ref, act_other_ref, bc_ref, *rest,
    split,
):
    reads = rest[:-2]
    bc_other_ref, read_ref = rest[-2:]
    place = lax.axis_index("seq")
    core = lax.rem(place, 2)
    first = core == 0
    n = x_ref.shape[0]
    started = jnp.where(place >= 2, 1.0, 0.0)
    edge = jnp.where(first, edge_a_ref[:, :128].astype(F32), edge_b_ref[:, :128].astype(F32)) * started
    tile = 128

    def before(at):
        pieces = []
        for i in range(at // 128, (at + CHUNK) // 128):
            piece = edge[i // 2 * 8 : i // 2 * 8 + 8]
            pieces.append(pltpu.roll(piece, 4, 0) if i % 2 == 0 else piece)
        return jnp.concatenate(pieces, axis=1)

    def convolve(at, act_refs, to):
        cols = pl.ds(at, CHUNK)
        from_cols = pl.ds(D + at - HALF if at >= HALF else pl.multiple_of(core * HALF + at, 128), CHUNK)
        taps = taps_ref[:, cols]
        bias = bias_ref[:, cols]

        def rows(side, start, count):
            return (x_ref[start : start + count, cols] if side == 0 else other_ref[0, start : start + count, from_cols]).astype(F32)

        ends = [rows(side, n - EDGE, EDGE)[EDGE - 8 :] for side in range(2)]
        chip = before(at)
        for side, act_ref in enumerate(act_refs):
            ahead = jnp.where(first == (side == 0), chip, ends[1 - side])
            for t in range(n // tile):
                if t == 0:
                    seen = jnp.concatenate([ahead, rows(side, 0, tile)], axis=0)
                else:
                    seen = rows(side, t * tile - EDGE, tile + EDGE)[EDGE - 8 :]
                last = pltpu.roll(seen, 1, 0)
                pair = taps[1:2] * seen + taps[0:1] * last
                total = bias + taps[3:4] * seen[8:] + taps[2:3] * last[8:]
                total += pltpu.roll(pair, 2, 0)[8:]
                act_ref[t * tile : (t + 1) * tile, to : to + CHUNK] = silu(total).astype(BF16)

    convolve(HALF, (bc_ref, bc_other_ref), 0)
    b_turned = [ref[:, :N].T for ref in (bc_ref, bc_other_ref)]
    both = jnp.concatenate(b_turned, axis=1)
    rows = jnp.concatenate([rows_ref[...], later_ref[...]], axis=0)

    for j in range(HALF // CHUNK):
        at = j * CHUNK
        cols = pl.ds(at, CHUNK)
        convolve(at, (act_own_ref, act_other_ref), at)
        head = core * (H // 2) + j * (CHUNK // P_SIZE)
        spread = spread_matrix(head)
        wide = dot(rows, spread)
        table, ahead = wide[:16], wide[16:17]
        act = jnp.concatenate([act_own_ref[:, cols], act_other_ref[:, cols]], axis=0).astype(F32)
        scaled = act * widen(ws_ref[...], head)
        weighted = scaled.astype(BF16)
        own = dot(b_turned[0], weighted[:n])
        other = dot(b_turned[1], weighted[n:])
        to_end = [jnp.where(first, table[1:2], 1.0), jnp.where(first, 1.0, table[1:2])]
        state = to_end[0] * own + to_end[1] * other
        early_ref[:, cols] = jnp.where(first, own, other).astype(BF16)
        state_ref[:, cols] = state.astype(BF16)
        beyond = jnp.concatenate([(ahead * to_end[0]) * scaled[:n], (ahead * to_end[1]) * scaled[n:]], axis=0)
        read = act * widen(wr_ref[...], head) + beyond
        high = read.astype(BF16)
        low = (read - high.astype(F32)).astype(BF16)
        seen = dot(both, high) + dot(both, low)
        read_ref[pl.ds(at, CHUNK)] = seen.T

    if split:
        part = D // 8
        x_bit = lax.rem(lax.axis_index("dp"), 2)
        z_bit = lax.rem(lax.axis_index("dp") // 2, 2)

        def rows(z, x, start, count):
            return read_ref[pl.ds(pl.multiple_of((2 * z + x) * part + start, 8), count)]

        rest = part - LEAD
        for q in range(2):
            here = slice(q * LEAD, (q + 1) * LEAD)
            reads[0][here] = rows(q, x_bit, 0, LEAD)
            reads[1][here] = rows(q, 1 - x_bit, 0, LEAD)
            here = slice(q * rest, (q + 1) * rest)
            reads[2][here] = rows(z_bit, q, LEAD, rest)
            reads[3][here] = rows(1 - z_bit, q, LEAD, rest)
        reads[1][2 * LEAD :] = mark_ref[...]
        reads[3][2 * rest :] = mark_ref[...]
    else:
        reads[0][...] = read_ref[...]


def diagonal_kernel(act_own_ref, act_other_ref, bc_ref, ws_ref, e_ref, rows_ref, gate_ref, near_ref, far_ref):
    core = lax.rem(lax.axis_index("seq"), 2)
    n = act_own_ref.shape[0]
    scores = lax.dot_general(bc_ref[:, N:], bc_ref[:, :N], (((1,), (1,)), ((), ())), preferred_element_type=F32)
    row = lax.broadcasted_iota(jnp.int32, (n, n), 0)
    lane = lax.broadcasted_iota(jnp.int32, (n, n), 1)
    masked = jnp.where(row >= lane, scores, 0.0).astype(BF16)
    ws = ws_ref[:n]
    for side, source in enumerate((act_own_ref, act_other_ref)):
        half = core if side == 0 else 1 - core

        @pl.loop(0, HALF // CHUNK, unroll=True)
        def _(j):
            at = pl.multiple_of(j * CHUNK, CHUNK)
            cols = pl.ds(at, CHUNK)
            head = half * (H // 2) + j * (CHUNK // P_SIZE)
            spread = spread_matrix(head)
            act = source[:, cols].astype(F32)
            weighted = (act * widen(ws, head)).astype(BF16)
            table = dot(rows_ref[...], spread)
            decay = widen(e_ref[...], head)
            value = decay * (table[3:4] * dot(masked, weighted)) + table[2:3] * act
            gate = silu(gate_ref[0, :, pl.ds(pl.multiple_of(half * HALF + at, CHUNK), CHUNK)].astype(F32))
            near_ref[side, :, cols] = value * gate
            far_ref[side, :, cols] = decay * gate


def carry_kernel(h_ref, early_ref, rows_ref, keep_ref, send_ref):
    place = lax.axis_index("seq")
    first = lax.rem(place, 2) == 0
    for j in range(HALF // CHUNK):
        cols = pl.ds(j * CHUNK, CHUNK)
        spread = spread_matrix(lax.rem(place, 2) * (H // 2) + j * (CHUNK // P_SIZE))
        chip = jnp.where(place >= 2, h_ref[:, cols].astype(F32), 0.0)
        middle = dot(rows_ref[...], spread)[0:1] * chip + early_ref[:, cols].astype(F32)
        keep_ref[:, cols] = jnp.where(first, chip, middle).astype(BF16)
        send_ref[:, cols] = jnp.where(first, middle, chip).astype(BF16)


def finish_kernel(near_ref, far_ref, bc_ref, h_own_ref, h_other_ref, gain_ref, out_hbm, g_ref, out_ref, sems):
    core = lax.rem(lax.axis_index("seq"), 2)
    n = bc_ref.shape[0]
    squares = jnp.zeros((n, CHUNK), F32)
    c_vals = bc_ref[:, N:]
    for side in range(2):
        h_ref = (h_own_ref, h_other_ref)[side]
        for j in range(HALF // CHUNK):
            cols = pl.ds(j * CHUNK, CHUNK)
            g = near_ref[side, :, cols] + far_ref[side, :, cols] * dot(c_vals, h_ref[:, cols])
            g_ref[side, :, cols] = g
            squares += g * g
    scale = lax.rsqrt(jnp.sum(squares, axis=-1, keepdims=True) * (1.0 / D) + 1e-05)
    tile = n // 4
    copies = []
    for t in range(4):
        rows = pl.ds(t * tile, tile)
        for side in range(2):
            half = core if side == 0 else 1 - core
            for j in range(HALF // CHUNK):
                cols = pl.ds(pl.multiple_of(half * HALF + j * CHUNK, CHUNK), CHUNK)
                g = g_ref[side, rows, pl.ds(j * CHUNK, CHUNK)]
                out_ref[rows, cols] = (g * scale[t * tile : (t + 1) * tile] * gain_ref[:, cols]).astype(BF16)
        copies.append(pltpu.make_async_copy(out_ref.at[rows], out_hbm.at[0, rows], sems.at[t]))
        copies[t].start()
    for copy in copies:
        copy.wait()


def join_kernel(mark_ref, a_ref, b_ref, out_ref):
    row = lax.broadcasted_iota(jnp.int32, out_ref.shape, 0)
    out_ref[...] = jnp.where(row == 0, a_ref[...] + b_ref[...], mark_ref[...])


def join(mark, a, b):
    out = jax.ShapeDtypeStruct(a.shape, a.dtype)
    return pl.pallas_call(
        join_kernel, out_shape=out, in_specs=[VMEM] * 3, out_specs=VMEM, compiler_params=params(8), name="join"
    )(mark, a, b)


def halves_kernel(
    kept_x_ref, came_x_ref, kept_z_ref, came_z_ref, mark_ref, across_ref,
    keep_a_ref, send_a_ref, keep_b_ref, send_b_ref,
    *, sequences,
):
    x_mark_ref = came_x_ref.at[kept_x_ref.shape[0] :]
    z_mark_ref = came_z_ref.at[kept_z_ref.shape[0] :]
    ones = (mark_ref[0:1] + x_mark_ref[0:1]) + (z_mark_ref[0:1] + across_ref[0:1])

    def weight(mark):
        return mark / ones - (1.0 - mark) / (sequences - ones)

    own = weight(mark_ref[1:2])
    place = lax.axis_index("dp")
    x_bit = lax.rem(place, 2)
    z_bit = lax.rem(place // 2, 2)
    work = (
        (kept_x_ref, came_x_ref, x_mark_ref, z_bit, keep_a_ref, send_a_ref),
        (kept_z_ref, came_z_ref, z_mark_ref, x_bit, keep_b_ref, send_b_ref),
    )
    for kept, came, other_mark, bit, keep, send in work:
        other = weight(other_mark[1:2])
        part = keep.shape[0]
        mine = pl.ds(pl.multiple_of(bit * part, 8), part)
        yours = pl.ds(pl.multiple_of((1 - bit) * part, 8), part)
        send[...] = own * kept[yours] + other * came[yours]
        keep[...] = own * kept[mine] + other * came[mine]


def chunks_kernel(keep_a_ref, came_a_ref, keep_b_ref, came_b_ref, keep_ref, core_ref, same_ref, cross_ref):
    place = lax.axis_index("seq")
    part = keep_ref.shape[0]
    upper = lax.rem(place // 2, 2) == 0
    first = lax.rem(place, 2) == 0
    rows = jnp.concatenate([keep_a_ref[...] + came_a_ref[...], keep_b_ref[...] + came_b_ref[...]], axis=0)
    here = jnp.where(upper, rows[: 2 * part], rows[2 * part :])
    there = jnp.where(upper, rows[2 * part :], rows[: 2 * part])
    keep_ref[...] = jnp.where(first, here[:part], here[part:])
    core_ref[...] = jnp.where(first, here[part:], here[:part])
    same_ref[...] = jnp.where(first, there[:part], there[part:])
    cross_ref[...] = jnp.where(first, there[part:], there[:part])


def planes_kernel(own_ref, same_ref, core_ref, cross_ref, keep_ref, send_ref):
    stays = lax.rem(lax.axis_index("dp") // 4, 2) == lax.rem(lax.axis_index("seq"), 2)
    own = own_ref[...] + same_ref[...]
    other = core_ref[...] + cross_ref[...]
    keep_ref[...] = jnp.where(stays, own, other)
    send_ref[...] = jnp.where(stays, other, own)


def sum_kernel(keep_ref, came_ref, out_ref):
    out_ref[...] = keep_ref[...] + came_ref[...]


def swap(k):
    return [(i, i ^ k) for i in range(8)]


def small_call(kernel, name, counts, *args):
    parts = tuple(jax.ShapeDtypeStruct((rows, N), F32) for rows in counts)
    return pl.pallas_call(
        kernel, out_shape=parts, in_specs=[VMEM] * len(args), out_specs=(VMEM,) * len(parts), compiler_params=params(8), name=name
    )(*args)


def on_device(xbc, gate_input, dt_raw, conv_weight, conv_bias, dt_bias, a_rate, d_skip, norm_gain, labels, readout):
    n = xbc.shape[1]
    places = lax.axis_size("seq")
    sequences = lax.axis_size("dp")
    chips = places // 2
    place = lax.axis_index("seq")
    core = place % 2
    split = sequences == 8 and places == 4
    pair = [(i, i ^ 1) for i in range(places)]
    shape = jax.ShapeDtypeStruct

    one_back = [(i, i ^ 3) for i in range(4)] if chips == 2 else [(i, (i + 1) % places) for i in range(places)]
    two_back = [(i, (i + 2) % places) for i in range(places)]
    dt_turned = jnp.swapaxes(dt_raw, 1, 2)
    dt_other = lax.ppermute(dt_turned, "seq", pair)
    xbc_other = lax.ppermute(xbc, "seq", pair)
    xbc_here = in_hbm(xbc)
    payload = shape((4 * SIDE // 128, 128 + n), BF16)
    tail_a, tail_b, dt_own, columns, points = pl.pallas_call(
        tail_kernel,
        out_shape=(payload, payload, shape((1, H, n), BF16), shape((H, 8), F32), shape((8, 128), jnp.int32)),
        in_specs=[HBM] * 6,
        out_specs=(VMEM,) * 5,
        scratch_shapes=[pltpu.VMEM((EDGE, CH), BF16)]
        + [pltpu.VMEM((1, H), F32)] * 3
        + [pltpu.SMEM((1, R), jnp.int32), pltpu.SemaphoreType.DMA((6,))],
        compiler_params=params(8),
        name="tail",
    )(xbc_here, in_hbm(dt_turned), in_hbm(dt_bias), in_hbm(a_rate), in_hbm(d_skip), in_hbm(readout))
    edge_a = lax.ppermute(tail_a, "seq", one_back)
    edge_b = lax.ppermute(tail_b, "seq", two_back)
    mark = pl.pallas_call(
        mark_kernel, out_shape=shape((8, N), F32), in_specs=[SMEM], out_specs=VMEM, compiler_params=params(8), name="mark"
    )(tied(labels, points))

    ws, wr, e, rows, x, taps, bias, *small = pl.pallas_call(
        steps_kernel,
        out_shape=(
            shape((2 * n, 128), F32), shape((2 * n, 128), F32), shape((n, 128), F32), shape((16, 128), BF16),
            shape((n, SIDE), BF16), shape((KW, SIDE), F32), shape((1, SIDE), F32),
        ) + ((shape((8, 128), F32),) if chips != 2 else ()),
        in_specs=[VMEM] * 4 + [HBM] * 3,
        out_specs=(VMEM,) * (8 if chips != 2 else 7),
        scratch_shapes=[pltpu.SemaphoreType.DMA((6,))],
        compiler_params=params(16),
        cost_estimate=cost(30 * n * n * 1024, 8 * n * 256),
        name="steps",
    )(dt_own, dt_other, columns, points, xbc_here, in_hbm(conv_weight), in_hbm(conv_bias))

    if chips == 2:
        later = pl.pallas_call(
            later_kernel,
            out_shape=shape((16, 128), BF16),
            in_specs=[VMEM] * 4,
            out_specs=VMEM,
            compiler_params=params(16),
            cost_estimate=cost(10 * n * n * 1024, 8 * n * 256),
            name="later",
        )(edge_b, edge_a, tied(columns, ws), points)
    else:
        small = small[0]
        later = jnp.zeros_like(small)
        for step in range(chips - 1):
            out = small.at[0:1].add(small[1:2] * later[0:1])
            later = lax.ppermute(out, "seq", [(i, (i - 2) % places) for i in range(places)])
            later = jnp.where(place < places - 2, later, 0.0)
        high = lax.reduce_precision(later[0, :H], 8, 7)
        gap = jnp.zeros(64 - H, F32)
        packed = jnp.concatenate([high, gap, later[0, :H] - high, gap])
        later = jnp.broadcast_to(packed, (16, 128)).astype(BF16)

    if split:
        ones = join(tied(mark, later), mark, lax.ppermute(mark, "dp", swap(4)))
    else:
        ones = mark

    read_rows = (2 * LEAD, 2 * LEAD + 8, D // 4 - 2 * LEAD, D // 4 - 2 * LEAD + 8) if split else (HALF,)
    state, early, act_own, act_other, bc, *reads = pl.pallas_call(
        functools.partial(state_kernel, split=split),
        out_shape=(
            shape((N, HALF), BF16), shape((N, HALF), BF16),
            shape((n, HALF), BF16), shape((n, HALF), BF16), shape((n, BC), BF16),
        ) + tuple(shape((count, N), F32) for count in read_rows),
        in_specs=[VMEM] * 11,
        out_specs=(VMEM,) * (5 + len(read_rows)),
        scratch_shapes=[pltpu.VMEM((n, BC), BF16), pltpu.VMEM((HALF, N), F32)],
        compiler_params=params(24),
        cost_estimate=cost(50 * n * n * D, 4 * 2 * n * SIDE),
        name="states",
    )(x, xbc_other, edge_a, edge_b, ws, wr, rows, later, taps, bias, ones)

    h = state
    for step in range(chips - 1):
        if step:
            scale = jnp.repeat(lax.dynamic_slice_in_dim(small[1, :H], core * (H // 2), H // 2), P_SIZE)
            h = (h.astype(F32) * scale + state.astype(F32)).astype(BF16)
        h = lax.ppermute(h, "seq", two_back)
        if chips > 2:
            h = jnp.where(place >= 2, h, jnp.zeros_like(h))
    act_in = lax.ppermute(act_other, "seq", pair)
    if split:
        keep_x, send_x, keep_z, send_z = reads
        came_x = lax.ppermute(send_x, "dp", swap(1))
        came_z = lax.ppermute(send_z, "dp", swap(2))
        across = lax.ppermute(tied(ones, send_x), "dp", swap(3))

    if split:
        keep_a, send_a, keep_b, send_b = small_call(
            functools.partial(halves_kernel, sequences=float(sequences)), "halves", (LEAD, LEAD, D // 8 - LEAD, D // 8 - LEAD),
            keep_x, came_x, keep_z, came_z, ones, across,
        )
        came_a = lax.ppermute(send_a, "dp", swap(2))
        came_b = lax.ppermute(send_b, "dp", swap(1))
        act_in = tied(act_in, keep_a)
        near, reach = pl.pallas_call(
            diagonal_kernel,
            out_shape=(shape((2, n, HALF), F32), shape((2, n, HALF), F32)),
            in_specs=[VMEM] * 7,
            out_specs=(VMEM, VMEM),
            compiler_params=params(24),
            cost_estimate=cost(28 * n * n * D, 4 * n * D),
            name="diagonal",
        )(act_own, act_in, bc, ws, e, rows, gate_input)
        keep_b, near, reach = lax.optimization_barrier((keep_b, near, reach))
        keep, to_core, to_same, to_cross = small_call(chunks_kernel, "chunks", (D // 32,) * 4, keep_a, came_a, keep_b, came_b)
        from_core = lax.ppermute(to_core, "seq", pair)
        from_same = lax.ppermute(to_same, "seq", [(i, i ^ 2) for i in range(places)])
        from_cross = lax.ppermute(to_cross, "seq", [(i, i ^ 3) for i in range(places)])
    else:
        near, reach = pl.pallas_call(
            diagonal_kernel,
            out_shape=(shape((2, n, HALF), F32), shape((2, n, HALF), F32)),
            in_specs=[VMEM] * 7,
            out_specs=(VMEM, VMEM),
            compiler_params=params(24),
            cost_estimate=cost(28 * n * n * D, 4 * n * D),
            name="diagonal",
        )(act_own, act_in, bc, ws, e, rows, gate_input)
    h = tied(h, keep) if split else h
    h_own, h_send = pl.pallas_call(
        carry_kernel, out_shape=(shape((N, HALF), BF16),) * 2, in_specs=[VMEM] * 3, out_specs=(VMEM,) * 2, compiler_params=params(8), name="carry",
        cost_estimate=cost(8 * n * n * D, 4 * N * D),
    )(h, early, rows)
    h_other = lax.ppermute(h_send, "seq", pair)
    layer_out = pl.pallas_call(
        finish_kernel,
        out_shape=shape((1, n, D), BF16),
        in_specs=[VMEM] * 6,
        out_specs=HBM,
        scratch_shapes=[pltpu.VMEM((2, n, HALF), F32), pltpu.VMEM((n, D), BF16), pltpu.SemaphoreType.DMA((4,))],
        compiler_params=params(24),
        cost_estimate=cost(20 * n * n * D, 12 * n * D),
        name="finish",
    )(near, reach, bc, h_own, h_other, norm_gain[None])
    if split:
        keep, send = small_call(planes_kernel, "planes", (D // 32,) * 2, keep, from_same, from_core, from_cross)
        came = lax.ppermute(send, "dp", swap(4))
        keep, layer_out = lax.optimization_barrier((keep, layer_out))
        steering = small_call(sum_kernel, "sum", (D // 32,), keep, came)[0]
    else:
        ones = lax.psum(mark[0, 0], "dp")
        weight = mark[0, 0] / ones - (1.0 - mark[0, 0]) / (sequences - ones)
        whole = lax.dynamic_update_slice_in_dim(jnp.zeros((D, N), F32), weight * reads[0], core * HALF, 0)
        steering = lax.psum_scatter(whole, ("dp", "seq"), scatter_dimension=0, tiled=True)
    return (layer_out, steering)


def solution(mesh):
    return jax.shard_map(
        on_device,
        mesh=mesh,
        in_specs=(
            P("dp", "seq", None),
            P("dp", "seq", None),
            P("dp", "seq", None),
            P(),
            P(),
            P(),
            P(),
            P(),
            P(),
            P("dp"),
            P("dp", None),
        ),
        out_specs=(P("dp", "seq", None), P(("dp", "seq"), None)),
        check_vma=False,
    )
```

```python
import functools

import jax
import jax.numpy as jnp
from jax import lax
from jax.experimental import pallas as pl
from jax.experimental.pallas import tpu as pltpu
from jax.sharding import PartitionSpec as P

H = 40
P_SIZE = 64
N = 128
KW = 4
R = 4
D = H * P_SIZE
HALF = D // 2
BC = 2 * N
SIDE = HALF + BC
CH = D + BC
CHUNK = 256
EDGE = 16
LEAD = 192
F32 = jnp.float32
BF16 = jnp.bfloat16
VMEM = pl.BlockSpec(memory_space=pltpu.VMEM)
SMEM = pl.BlockSpec(memory_space=pltpu.SMEM)
ANY = pl.BlockSpec(memory_space=pl.ANY)
HBM = pl.BlockSpec(memory_space=pltpu.HBM)
MIB = 1024 * 1024


def params(mib):
    return pltpu.CompilerParams(vmem_limit_bytes=mib * MIB)


def cost(flops, read):
    return pl.CostEstimate(flops=flops, bytes_accessed=read, transcendentals=0)


def in_hbm(x):
    return pltpu.with_memory_space_constraint(x, pltpu.HBM)


def tied(x, *others):
    return lax.optimization_barrier((x,) + others)[0]


def dot(a, b):
    return jnp.dot(a, b, preferred_element_type=F32)


def pack(w):
    high = w.astype(BF16).astype(F32)
    gap = jnp.zeros((64 - H, w.shape[1]), F32)
    return jnp.concatenate([high, gap, w - high, gap], axis=0).astype(BF16).T


def stand(w):
    return jnp.concatenate([w, jnp.zeros((128 - H, w.shape[1]), F32)], axis=0).T


def widen(w, first_head):
    head = lax.broadcasted_iota(jnp.int32, w.shape, 1) // P_SIZE + first_head
    picked = [jnp.take_along_axis(w, head + i, axis=1) for i in range(0, CHUNK // P_SIZE, 128 // P_SIZE)]
    return jnp.concatenate(picked, axis=1)


def beside(columns):
    lane = lax.broadcasted_iota(jnp.int32, (H, 128), 1)
    table = jnp.zeros((H, 128), F32)
    for i, column in enumerate(columns):
        table = jnp.where(lane == i, column, table)
    return table


def turned(rows):
    table = jnp.concatenate(list(rows) + [jnp.zeros((8 - len(rows), H), F32)], axis=0)
    return jnp.concatenate([table, jnp.zeros((8, 128 - H), F32)], axis=1).T[:H]


def spread_matrix(first_head):
    row = lax.broadcasted_iota(jnp.int32, (128, CHUNK), 0)
    lane = lax.broadcasted_iota(jnp.int32, (128, CHUNK), 1)
    hit = (row & 63) == first_head + lane // P_SIZE
    return jnp.where(hit, 1.0, 0.0).astype(BF16)


def silu(v):
    half = 0.5 * v
    return half + half * jnp.tanh(half)


def fetch(pairs, sems):
    copies = [pltpu.make_async_copy(source, to, sems.at[i]) for i, (source, to) in enumerate(pairs)]
    for copy in copies:
        copy.start()
    for copy in copies:
        copy.wait()


def step_sizes(raw, bias):
    raw = raw + bias
    return jnp.maximum(raw, 0.0) + jnp.log1p(jnp.exp(-jnp.abs(raw)))


def running_sums(steps):
    n = steps[0].shape[1]
    row = lax.broadcasted_iota(jnp.int32, (n, n), 0)
    lane = lax.broadcasted_iota(jnp.int32, (n, n), 1)
    upper = jnp.where(row <= lane, 1.0, 0.0).astype(BF16)
    parts = []
    for step in steps:
        high = step.astype(BF16).astype(F32)
        middle = (step - high).astype(BF16).astype(F32)
        parts += [high, middle, step - high - middle]
    sums = dot(jnp.concatenate(parts, axis=0).astype(BF16), upper)
    return [sums[i : i + H] + (sums[i + H : i + 2 * H] + sums[i + 2 * H : i + 3 * H]) for i in range(0, 3 * H * len(steps), 3 * H)]


def read_levels(points, base, total):
    n = total[0].shape[1]
    index = lax.broadcasted_iota(jnp.int32, (H, n), 1)
    found = []
    for r in range(R):
        at = points[r : r + 1, 0:1] - base
        inside = jnp.where((at >= 0) & (at < 2 * n), 1.0, 0.0)
        level = jnp.zeros((H, n), F32)
        for block in range(2):
            level += jnp.where(index + block * n == at, total[block], 0.0)
        found.append((at, inside, jnp.sum(level, axis=1, keepdims=True)))
    return found


def carry_of(found):
    carry = jnp.zeros((H, 1), F32)
    for _, inside, level in found:
        carry += inside * jnp.exp(level)
    return carry * (1.0 / R)


def tail_kernel(
    xbc_hbm, dt_hbm, bias_hbm, rate_hbm, skip_hbm, points_hbm, out_a_ref, out_b_ref, dt_ref, columns_ref, points_ref, x_ref,
    rows_ref, bias_ref, rate_ref, skip_ref, spot_ref, sems,
):
    n = xbc_hbm.shape[1]
    rows = xbc_hbm.at[0, pl.ds(n - EDGE, EDGE)]
    col = pl.multiple_of(lax.rem(lax.axis_index("seq"), 2) * HALF, 128)
    inputs = [
        pltpu.make_async_copy(xbc_hbm.at[0, :, pl.ds(from_at, width)], x_ref.at[:, pl.ds(to_at, width)], sems.at[6 + i])
        for i, (from_at, to_at, width) in enumerate(((D, HALF, BC), (col, 0, HALF)))
    ]
    for copy in inputs:
        copy.start()
    fetch(
        (
            (dt_hbm, dt_ref), (rows, rows_ref), (points_hbm, spot_ref),
            (bias_hbm, bias_ref.at[0]), (rate_hbm, rate_ref.at[0]), (skip_hbm, skip_ref.at[0]),
        ),
        sems,
    )
    tail = rows_ref[...].astype(F32)[EDGE - 8 :]
    steps = jnp.concatenate([dt_ref[0].astype(F32), jnp.zeros((4 * SIDE // 128 - H, n), F32)], axis=0).astype(BF16)
    upper = lax.broadcasted_iota(jnp.int32, (8, 128), 0) < 4
    for half, out_ref in enumerate((out_a_ref, out_b_ref)):
        pieces = [half * HALF + i for i in range(0, HALF, 128)] + [D + i for i in range(0, BC, 128)]
        pieces = [tail[:, i : i + 128] for i in pieces]
        stack = [jnp.where(upper, pltpu.roll(pieces[i], 4, 0), pieces[i + 1]) for i in range(0, len(pieces), 2)]
        out_ref[:, :128] = jnp.concatenate(stack, axis=0).astype(BF16)
        out_ref[:, 128:] = steps
    columns_ref[...] = turned((bias_ref[...], rate_ref[...], skip_ref[...]))
    spot = lax.broadcasted_iota(jnp.int32, points_ref.shape, 0)
    points = jnp.zeros(points_ref.shape, jnp.int32)
    for r in range(R):
        points = jnp.where(spot == r, spot_ref[0, r], points)
    points_ref[...] = points
    for copy in inputs:
        copy.wait()


def mark_kernel(label_ref, mark_ref):
    mark_ref[...] = jnp.zeros(mark_ref.shape, F32) + label_ref[0].astype(F32)


def steps_kernel(
    own_ref, other_ref, columns_ref, points_ref, conv_w_hbm, conv_b_hbm,
    ws_ref, wr_ref, e_ref, rows_ref, taps_ref, bias_ref, *rest,
):
    place = lax.axis_index("seq")
    core = lax.rem(place, 2)
    n = own_ref.shape[2]
    sems = rest[-1]
    col = pl.multiple_of(core * HALF, 128)
    copies = []
    for from_at, to_at, width in ((D, HALF, BC), (col, 0, HALF)):
        here, there = pl.ds(from_at, width), pl.ds(to_at, width)
        copies.append((conv_w_hbm.at[:, here], taps_ref.at[:, there]))
        copies.append((conv_b_hbm.at[here], bias_ref.at[0, there]))
    copies = [pltpu.make_async_copy(source, to, sems.at[i]) for i, (source, to) in enumerate(copies)]
    for copy in copies:
        copy.start()
    own = own_ref[0].astype(F32)
    other = other_ref[0].astype(F32)
    bias, rate, skip = columns_ref[:, 0:1], columns_ref[:, 1:2], columns_ref[:, 2:3]
    first = core == 0
    dts = [step_sizes(jnp.where(first == (block == 0), own, other), bias) for block in range(2)]
    cums = running_sums([-rate * dt for dt in dts])
    ends = [cum[:, n - 1 : n] for cum in cums]

    def store(ref, values):
        ref[:n] = stand(jnp.where(first, values[0], values[1]))
        ref[n:] = stand(jnp.where(first, values[1], values[0]))

    store(ws_ref, [dts[block] * jnp.exp(ends[block] - cums[block]) for block in range(2)])
    total = [cums[0], ends[0] + cums[1]]
    index = lax.broadcasted_iota(jnp.int32, (H, n), 1)
    weight = [jnp.zeros((H, n), F32), jnp.zeros((H, n), F32)]
    found = read_levels(points_ref[...], (place - core) * n, total)
    for at, inside, level in found:
        for block in range(2):
            seen = jnp.where(index + block * n <= at, jnp.exp(jnp.minimum(level - total[block], 0.0)), 0.0)
            weight[block] += inside * seen
    store(wr_ref, [weight[block] * dts[block] * (1.0 / R) for block in range(2)])
    e_ref[...] = stand(jnp.exp(jnp.where(first, cums[0], cums[1])))
    decay = [jnp.exp(end) for end in ends]
    back = jnp.exp(-jnp.where(first, ends[0], ends[1]))
    rows_ref[...] = pack(beside((decay[0], decay[1], skip, back)))[0:16]
    if len(rest) > 1:
        whole = beside((carry_of(found), jnp.exp(ends[0] + ends[1])))
        rest[0][...] = jnp.concatenate([whole, jnp.zeros((128 - H, 128), F32)], axis=0).T[0:8]
    for copy in copies:
        copy.wait()


def later_kernel(same_ref, cross_ref, columns_ref, points_ref, later_ref):
    place = lax.axis_index("seq")
    core = lax.rem(place, 2)
    n = same_ref.shape[1] - 128
    same, cross = same_ref[:, 128:].astype(F32)[:H], cross_ref[:, 128:].astype(F32)[:H]
    bias, rate = columns_ref[:, 0:1], columns_ref[:, 1:2]
    raws = [jnp.where((core == 0) == (block == 0), same, cross) for block in range(2)]
    cums = running_sums([-rate * step_sizes(raw, bias) for raw in raws])
    total = [cums[0], cums[0][:, n - 1 : n] + cums[1]]
    carry = carry_of(read_levels(points_ref[...], 2 * n, total))
    later_ref[...] = pack(beside((jnp.where(place < 2, carry, 0.0),)))[0:16]


def state_kernel(
    x_ref, other_ref, edge_a_ref, edge_b_ref, ws_ref, wr_ref, rows_ref, later_ref, taps_ref, bias_ref, mark_ref,
    state_ref, early_ref, act_own_ref, act_other_ref, bc_ref, *rest,
    split,
):
    reads = rest[:-2]
    bc_other_ref, read_ref = rest[-2:]
    place = lax.axis_index("seq")
    core = lax.rem(place, 2)
    first = core == 0
    n = x_ref.shape[0]
    started = jnp.where(place >= 2, 1.0, 0.0)
    edge = jnp.where(first, edge_a_ref[:, :128].astype(F32), edge_b_ref[:, :128].astype(F32)) * started
    tile = 128

    def before(at):
        pieces = []
        for i in range(at // 128, (at + CHUNK) // 128):
            piece = edge[i // 2 * 8 : i // 2 * 8 + 8]
            pieces.append(pltpu.roll(piece, 4, 0) if i % 2 == 0 else piece)
        return jnp.concatenate(pieces, axis=1)

    def convolve(at, act_refs, to):
        cols = pl.ds(at, CHUNK)
        from_cols = pl.ds(D + at - HALF if at >= HALF else pl.multiple_of(core * HALF + at, 128), CHUNK)
        taps = taps_ref[:, cols]
        bias = bias_ref[:, cols]

        def rows(side, start, count):
            return (x_ref[start : start + count, cols] if side == 0 else other_ref[0, start : start + count, from_cols]).astype(F32)

        ends = [rows(side, n - EDGE, EDGE)[EDGE - 8 :] for side in range(2)]
        chip = before(at)
        for side, act_ref in enumerate(act_refs):
            ahead = jnp.where(first == (side == 0), chip, ends[1 - side])
            for t in range(n // tile):
                if t == 0:
                    seen = jnp.concatenate([ahead, rows(side, 0, tile)], axis=0)
                else:
                    seen = rows(side, t * tile - EDGE, tile + EDGE)[EDGE - 8 :]
                last = pltpu.roll(seen, 1, 0)
                pair = taps[1:2] * seen + taps[0:1] * last
                total = bias + taps[3:4] * seen[8:] + taps[2:3] * last[8:]
                total += pltpu.roll(pair, 2, 0)[8:]
                act_ref[t * tile : (t + 1) * tile, to : to + CHUNK] = silu(total).astype(BF16)

    convolve(HALF, (bc_ref, bc_other_ref), 0)
    b_turned = [ref[:, :N].T for ref in (bc_ref, bc_other_ref)]
    both = jnp.concatenate(b_turned, axis=1)
    rows = jnp.concatenate([rows_ref[...], later_ref[...]], axis=0)

    for j in range(HALF // CHUNK):
        at = j * CHUNK
        cols = pl.ds(at, CHUNK)
        convolve(at, (act_own_ref, act_other_ref), at)
        head = core * (H // 2) + j * (CHUNK // P_SIZE)
        spread = spread_matrix(head)
        wide = dot(rows, spread)
        table, ahead = wide[:16], wide[16:17]
        act = jnp.concatenate([act_own_ref[:, cols], act_other_ref[:, cols]], axis=0).astype(F32)
        scaled = act * widen(ws_ref[...], head)
        weighted = scaled.astype(BF16)
        own = dot(b_turned[0], weighted[:n])
        other = dot(b_turned[1], weighted[n:])
        to_end = [jnp.where(first, table[1:2], 1.0), jnp.where(first, 1.0, table[1:2])]
        state = to_end[0] * own + to_end[1] * other
        early_ref[:, cols] = jnp.where(first, own, other).astype(BF16)
        state_ref[:, cols] = state.astype(BF16)
        beyond = jnp.concatenate([(ahead * to_end[0]) * scaled[:n], (ahead * to_end[1]) * scaled[n:]], axis=0)
        read = act * widen(wr_ref[...], head) + beyond
        high = read.astype(BF16)
        low = (read - high.astype(F32)).astype(BF16)
        seen = dot(both, high) + dot(both, low)
        read_ref[pl.ds(at, CHUNK)] = seen.T

    if split:
        part = D // 8
        x_bit = lax.rem(lax.axis_index("dp"), 2)
        z_bit = lax.rem(lax.axis_index("dp") // 2, 2)

        def rows(z, x, start, count):
            return read_ref[pl.ds(pl.multiple_of((2 * z + x) * part + start, 8), count)]

        rest = part - LEAD
        for q in range(2):
            here = slice(q * LEAD, (q + 1) * LEAD)
            reads[0][here] = rows(q, x_bit, 0, LEAD)
            reads[1][here] = rows(q, 1 - x_bit, 0, LEAD)
            here = slice(q * rest, (q + 1) * rest)
            reads[2][here] = rows(z_bit, q, LEAD, rest)
            reads[3][here] = rows(1 - z_bit, q, LEAD, rest)
        reads[1][2 * LEAD :] = mark_ref[...]
        reads[3][2 * rest :] = mark_ref[...]
    else:
        reads[0][...] = read_ref[...]


def diagonal_kernel(act_own_ref, act_other_ref, bc_ref, ws_ref, e_ref, rows_ref, gate_ref, near_ref, far_ref):
    core = lax.rem(lax.axis_index("seq"), 2)
    n = act_own_ref.shape[0]
    scores = lax.dot_general(bc_ref[:, N:], bc_ref[:, :N], (((1,), (1,)), ((), ())), preferred_element_type=F32)
    row = lax.broadcasted_iota(jnp.int32, (n, n), 0)
    lane = lax.broadcasted_iota(jnp.int32, (n, n), 1)
    masked = jnp.where(row >= lane, scores, 0.0).astype(BF16)
    ws = ws_ref[:n]
    for side, source in enumerate((act_own_ref, act_other_ref)):
        half = core if side == 0 else 1 - core

        @pl.loop(0, HALF // CHUNK, unroll=True)
        def _(j):
            at = pl.multiple_of(j * CHUNK, CHUNK)
            cols = pl.ds(at, CHUNK)
            head = half * (H // 2) + j * (CHUNK // P_SIZE)
            spread = spread_matrix(head)
            act = source[:, cols].astype(F32)
            weighted = (act * widen(ws, head)).astype(BF16)
            table = dot(rows_ref[...], spread)
            decay = widen(e_ref[...], head)
            value = decay * (table[3:4] * dot(masked, weighted)) + table[2:3] * act
            gate = silu(gate_ref[0, :, pl.ds(pl.multiple_of(half * HALF + at, CHUNK), CHUNK)].astype(F32))
            near_ref[side, :, cols] = value * gate
            far_ref[side, :, cols] = decay * gate


def carry_kernel(h_ref, early_ref, rows_ref, keep_ref, send_ref):
    place = lax.axis_index("seq")
    first = lax.rem(place, 2) == 0
    for j in range(HALF // CHUNK):
        cols = pl.ds(j * CHUNK, CHUNK)
        spread = spread_matrix(lax.rem(place, 2) * (H // 2) + j * (CHUNK // P_SIZE))
        chip = jnp.where(place >= 2, h_ref[:, cols].astype(F32), 0.0)
        middle = dot(rows_ref[...], spread)[0:1] * chip + early_ref[:, cols].astype(F32)
        keep_ref[:, cols] = jnp.where(first, chip, middle).astype(BF16)
        send_ref[:, cols] = jnp.where(first, middle, chip).astype(BF16)


def finish_kernel(near_ref, far_ref, bc_ref, h_own_ref, h_other_ref, gain_ref, out_hbm, g_ref, out_ref, sems):
    core = lax.rem(lax.axis_index("seq"), 2)
    n = bc_ref.shape[0]
    squares = jnp.zeros((n, CHUNK), F32)
    c_vals = bc_ref[:, N:]
    for side in range(2):
        h_ref = (h_own_ref, h_other_ref)[side]
        for j in range(HALF // CHUNK):
            cols = pl.ds(j * CHUNK, CHUNK)
            g = near_ref[side, :, cols] + far_ref[side, :, cols] * dot(c_vals, h_ref[:, cols])
            g_ref[side, :, cols] = g
            squares += g * g
    scale = lax.rsqrt(jnp.sum(squares, axis=-1, keepdims=True) * (1.0 / D) + 1e-05)
    tile = n // 4
    copies = []
    for t in range(4):
        rows = pl.ds(t * tile, tile)
        for side in range(2):
            half = core if side == 0 else 1 - core
            for j in range(HALF // CHUNK):
                cols = pl.ds(pl.multiple_of(half * HALF + j * CHUNK, CHUNK), CHUNK)
                g = g_ref[side, rows, pl.ds(j * CHUNK, CHUNK)]
                out_ref[rows, cols] = (g * scale[t * tile : (t + 1) * tile] * gain_ref[:, cols]).astype(BF16)
        copies.append(pltpu.make_async_copy(out_ref.at[rows], out_hbm.at[0, rows], sems.at[t]))
        copies[t].start()
    for copy in copies:
        copy.wait()


def join_kernel(mark_ref, a_ref, b_ref, out_ref):
    row = lax.broadcasted_iota(jnp.int32, out_ref.shape, 0)
    out_ref[...] = jnp.where(row == 0, a_ref[...] + b_ref[...], mark_ref[...])


def join(mark, a, b):
    out = jax.ShapeDtypeStruct(a.shape, a.dtype)
    return pl.pallas_call(
        join_kernel, out_shape=out, in_specs=[VMEM] * 3, out_specs=VMEM, compiler_params=params(8), name="join"
    )(mark, a, b)


def halves_kernel(
    kept_x_ref, came_x_ref, kept_z_ref, came_z_ref, mark_ref, across_ref,
    keep_a_ref, send_a_ref, keep_b_ref, send_b_ref,
    *, sequences,
):
    x_mark_ref = came_x_ref.at[kept_x_ref.shape[0] :]
    z_mark_ref = came_z_ref.at[kept_z_ref.shape[0] :]
    ones = (mark_ref[0:1] + x_mark_ref[0:1]) + (z_mark_ref[0:1] + across_ref[0:1])

    def weight(mark):
        return mark / ones - (1.0 - mark) / (sequences - ones)

    own = weight(mark_ref[1:2])
    place = lax.axis_index("dp")
    x_bit = lax.rem(place, 2)
    z_bit = lax.rem(place // 2, 2)
    work = (
        (kept_x_ref, came_x_ref, x_mark_ref, z_bit, keep_a_ref, send_a_ref),
        (kept_z_ref, came_z_ref, z_mark_ref, x_bit, keep_b_ref, send_b_ref),
    )
    for kept, came, other_mark, bit, keep, send in work:
        other = weight(other_mark[1:2])
        part = keep.shape[0]
        mine = pl.ds(pl.multiple_of(bit * part, 8), part)
        yours = pl.ds(pl.multiple_of((1 - bit) * part, 8), part)
        send[...] = own * kept[yours] + other * came[yours]
        keep[...] = own * kept[mine] + other * came[mine]


def chunks_kernel(keep_a_ref, came_a_ref, keep_b_ref, came_b_ref, keep_ref, core_ref, same_ref, cross_ref):
    place = lax.axis_index("seq")
    part = keep_ref.shape[0]
    upper = lax.rem(place // 2, 2) == 0
    first = lax.rem(place, 2) == 0
    rows = jnp.concatenate([keep_a_ref[...] + came_a_ref[...], keep_b_ref[...] + came_b_ref[...]], axis=0)
    here = jnp.where(upper, rows[: 2 * part], rows[2 * part :])
    there = jnp.where(upper, rows[2 * part :], rows[: 2 * part])
    keep_ref[...] = jnp.where(first, here[:part], here[part:])
    core_ref[...] = jnp.where(first, here[part:], here[:part])
    same_ref[...] = jnp.where(first, there[:part], there[part:])
    cross_ref[...] = jnp.where(first, there[part:], there[:part])


def planes_kernel(own_ref, same_ref, core_ref, cross_ref, keep_ref, send_ref):
    stays = lax.rem(lax.axis_index("dp") // 4, 2) == lax.rem(lax.axis_index("seq"), 2)
    own = own_ref[...] + same_ref[...]
    other = core_ref[...] + cross_ref[...]
    keep_ref[...] = jnp.where(stays, own, other)
    send_ref[...] = jnp.where(stays, other, own)


def sum_kernel(keep_ref, came_ref, out_ref):
    out_ref[...] = keep_ref[...] + came_ref[...]


def swap(k):
    return [(i, i ^ k) for i in range(8)]


def small_call(kernel, name, counts, *args):
    parts = tuple(jax.ShapeDtypeStruct((rows, N), F32) for rows in counts)
    return pl.pallas_call(
        kernel, out_shape=parts, in_specs=[VMEM] * len(args), out_specs=(VMEM,) * len(parts), compiler_params=params(8), name=name
    )(*args)


def on_device(xbc, gate_input, dt_raw, conv_weight, conv_bias, dt_bias, a_rate, d_skip, norm_gain, labels, readout):
    n = xbc.shape[1]
    places = lax.axis_size("seq")
    sequences = lax.axis_size("dp")
    chips = places // 2
    place = lax.axis_index("seq")
    core = place % 2
    split = sequences == 8 and places == 4
    pair = [(i, i ^ 1) for i in range(places)]
    shape = jax.ShapeDtypeStruct

    one_back = [(i, i ^ 3) for i in range(4)] if chips == 2 else [(i, (i + 1) % places) for i in range(places)]
    two_back = [(i, (i + 2) % places) for i in range(places)]
    dt_turned = jnp.swapaxes(dt_raw, 1, 2)
    dt_other = lax.ppermute(dt_turned, "seq", pair)
    xbc_other = lax.ppermute(xbc, "seq", pair)
    xbc_here = in_hbm(xbc)
    payload = shape((4 * SIDE // 128, 128 + n), BF16)
    tail_a, tail_b, dt_own, columns, points, x = pl.pallas_call(
        tail_kernel,
        out_shape=(payload, payload, shape((1, H, n), BF16), shape((H, 8), F32), shape((8, 128), jnp.int32), shape((n, SIDE), BF16)),
        in_specs=[HBM] * 6,
        out_specs=(VMEM,) * 6,
        scratch_shapes=[pltpu.VMEM((EDGE, CH), BF16)]
        + [pltpu.VMEM((1, H), F32)] * 3
        + [pltpu.SMEM((1, R), jnp.int32), pltpu.SemaphoreType.DMA((8,))],
        compiler_params=params(8),
        name="tail",
    )(xbc_here, in_hbm(dt_turned), in_hbm(dt_bias), in_hbm(a_rate), in_hbm(d_skip), in_hbm(readout))
    edge_a = lax.ppermute(tail_a, "seq", one_back)
    edge_b = lax.ppermute(tail_b, "seq", two_back)
    mark = pl.pallas_call(
        mark_kernel, out_shape=shape((8, N), F32), in_specs=[SMEM], out_specs=VMEM, compiler_params=params(8), name="mark"
    )(tied(labels, points))

    ws, wr, e, rows, taps, bias, *small = pl.pallas_call(
        steps_kernel,
        out_shape=(
            shape((2 * n, 128), F32), shape((2 * n, 128), F32), shape((n, 128), F32), shape((16, 128), BF16),
            shape((KW, SIDE), F32), shape((1, SIDE), F32),
        ) + ((shape((8, 128), F32),) if chips != 2 else ()),
        in_specs=[VMEM] * 4 + [HBM] * 2,
        out_specs=(VMEM,) * (7 if chips != 2 else 6),
        scratch_shapes=[pltpu.SemaphoreType.DMA((4,))],
        compiler_params=params(16),
        cost_estimate=cost(30 * n * n * 1024, 8 * n * 256),
        name="steps",
    )(dt_own, dt_other, columns, points, in_hbm(conv_weight), in_hbm(conv_bias))

    if chips == 2:
        later = pl.pallas_call(
            later_kernel,
            out_shape=shape((16, 128), BF16),
            in_specs=[VMEM] * 4,
            out_specs=VMEM,
            compiler_params=params(16),
            cost_estimate=cost(10 * n * n * 1024, 8 * n * 256),
            name="later",
        )(edge_b, edge_a, tied(columns, ws), points)
    else:
        small = small[0]
        later = jnp.zeros_like(small)
        for step in range(chips - 1):
            out = small.at[0:1].add(small[1:2] * later[0:1])
            later = lax.ppermute(out, "seq", [(i, (i - 2) % places) for i in range(places)])
            later = jnp.where(place < places - 2, later, 0.0)
        high = lax.reduce_precision(later[0, :H], 8, 7)
        gap = jnp.zeros(64 - H, F32)
        packed = jnp.concatenate([high, gap, later[0, :H] - high, gap])
        later = jnp.broadcast_to(packed, (16, 128)).astype(BF16)

    if split:
        ones = join(tied(mark, later), mark, lax.ppermute(mark, "dp", swap(4)))
    else:
        ones = mark

    read_rows = (2 * LEAD, 2 * LEAD + 8, D // 4 - 2 * LEAD, D // 4 - 2 * LEAD + 8) if split else (HALF,)
    state, early, act_own, act_other, bc, *reads = pl.pallas_call(
        functools.partial(state_kernel, split=split),
        out_shape=(
            shape((N, HALF), BF16), shape((N, HALF), BF16),
            shape((n, HALF), BF16), shape((n, HALF), BF16), shape((n, BC), BF16),
        ) + tuple(shape((count, N), F32) for count in read_rows),
        in_specs=[VMEM] * 11,
        out_specs=(VMEM,) * (5 + len(read_rows)),
        scratch_shapes=[pltpu.VMEM((n, BC), BF16), pltpu.VMEM((HALF, N), F32)],
        compiler_params=params(24),
        cost_estimate=cost(50 * n * n * D, 4 * 2 * n * SIDE),
        name="states",
    )(x, xbc_other, edge_a, edge_b, ws, wr, rows, later, taps, bias, ones)

    h = state
    for step in range(chips - 1):
        if step:
            scale = jnp.repeat(lax.dynamic_slice_in_dim(small[1, :H], core * (H // 2), H // 2), P_SIZE)
            h = (h.astype(F32) * scale + state.astype(F32)).astype(BF16)
        h = lax.ppermute(h, "seq", two_back)
        if chips > 2:
            h = jnp.where(place >= 2, h, jnp.zeros_like(h))
    act_in = lax.ppermute(act_other, "seq", pair)
    if split:
        keep_x, send_x, keep_z, send_z = reads
        came_x = lax.ppermute(send_x, "dp", swap(1))
        came_z = lax.ppermute(send_z, "dp", swap(2))
        across = lax.ppermute(tied(ones, send_x), "dp", swap(3))

    if split:
        keep_a, send_a, keep_b, send_b = small_call(
            functools.partial(halves_kernel, sequences=float(sequences)), "halves", (LEAD, LEAD, D // 8 - LEAD, D // 8 - LEAD),
            keep_x, came_x, keep_z, came_z, ones, across,
        )
        came_a = lax.ppermute(send_a, "dp", swap(2))
        came_b = lax.ppermute(send_b, "dp", swap(1))
        act_in = tied(act_in, keep_a)
        near, reach = pl.pallas_call(
            diagonal_kernel,
            out_shape=(shape((2, n, HALF), F32), shape((2, n, HALF), F32)),
            in_specs=[VMEM] * 7,
            out_specs=(VMEM, VMEM),
            compiler_params=params(24),
            cost_estimate=cost(28 * n * n * D, 4 * n * D),
            name="diagonal",
        )(act_own, act_in, bc, ws, e, rows, gate_input)
        keep_b, near, reach = lax.optimization_barrier((keep_b, near, reach))
        keep, to_core, to_same, to_cross = small_call(chunks_kernel, "chunks", (D // 32,) * 4, keep_a, came_a, keep_b, came_b)
        from_core = lax.ppermute(to_core, "seq", pair)
        from_same = lax.ppermute(to_same, "seq", [(i, i ^ 2) for i in range(places)])
        from_cross = lax.ppermute(to_cross, "seq", [(i, i ^ 3) for i in range(places)])
    else:
        near, reach = pl.pallas_call(
            diagonal_kernel,
            out_shape=(shape((2, n, HALF), F32), shape((2, n, HALF), F32)),
            in_specs=[VMEM] * 7,
            out_specs=(VMEM, VMEM),
            compiler_params=params(24),
            cost_estimate=cost(28 * n * n * D, 4 * n * D),
            name="diagonal",
        )(act_own, act_in, bc, ws, e, rows, gate_input)
    h = tied(h, keep) if split else h
    h_own, h_send = pl.pallas_call(
        carry_kernel, out_shape=(shape((N, HALF), BF16),) * 2, in_specs=[VMEM] * 3, out_specs=(VMEM,) * 2, compiler_params=params(8), name="carry",
        cost_estimate=cost(8 * n * n * D, 4 * N * D),
    )(h, early, rows)
    h_other = lax.ppermute(h_send, "seq", pair)
    layer_out = pl.pallas_call(
        finish_kernel,
        out_shape=shape((1, n, D), BF16),
        in_specs=[VMEM] * 6,
        out_specs=HBM,
        scratch_shapes=[pltpu.VMEM((2, n, HALF), F32), pltpu.VMEM((n, D), BF16), pltpu.SemaphoreType.DMA((4,))],
        compiler_params=params(24),
        cost_estimate=cost(20 * n * n * D, 12 * n * D),
        name="finish",
    )(near, reach, bc, h_own, h_other, norm_gain[None])
    if split:
        keep, send = small_call(planes_kernel, "planes", (D // 32,) * 2, keep, from_same, from_core, from_cross)
        came = lax.ppermute(send, "dp", swap(4))
        keep, layer_out = lax.optimization_barrier((keep, layer_out))
        steering = small_call(sum_kernel, "sum", (D // 32,), keep, came)[0]
    else:
        ones = lax.psum(mark[0, 0], "dp")
        weight = mark[0, 0] / ones - (1.0 - mark[0, 0]) / (sequences - ones)
        whole = lax.dynamic_update_slice_in_dim(jnp.zeros((D, N), F32), weight * reads[0], core * HALF, 0)
        steering = lax.psum_scatter(whole, ("dp", "seq"), scatter_dimension=0, tiled=True)
    return (layer_out, steering)


def solution(mesh):
    return jax.shard_map(
        on_device,
        mesh=mesh,
        in_specs=(
            P("dp", "seq", None),
            P("dp", "seq", None),
            P("dp", "seq", None),
            P(),
            P(),
            P(),
            P(),
            P(),
            P(),
            P("dp"),
            P("dp", None),
        ),
        out_specs=(P("dp", "seq", None), P(("dp", "seq"), None)),
        check_vma=False,
    )
```

```python
import functools

import jax
import jax.numpy as jnp
from jax import lax
from jax.experimental import pallas as pl
from jax.experimental.pallas import tpu as pltpu
from jax.sharding import PartitionSpec as P

H = 40
P_SIZE = 64
N = 128
KW = 4
R = 4
D = H * P_SIZE
HALF = D // 2
BC = 2 * N
SIDE = HALF + BC
CH = D + BC
CHUNK = 256
EDGE = 16
LEAD = 192
F32 = jnp.float32
BF16 = jnp.bfloat16
VMEM = pl.BlockSpec(memory_space=pltpu.VMEM)
SMEM = pl.BlockSpec(memory_space=pltpu.SMEM)
ANY = pl.BlockSpec(memory_space=pl.ANY)
HBM = pl.BlockSpec(memory_space=pltpu.HBM)
MIB = 1024 * 1024


def params(mib):
    return pltpu.CompilerParams(vmem_limit_bytes=mib * MIB)


def cost(flops, read):
    return pl.CostEstimate(flops=flops, bytes_accessed=read, transcendentals=0)


def in_hbm(x):
    return pltpu.with_memory_space_constraint(x, pltpu.HBM)


def tied(x, *others):
    return lax.optimization_barrier((x,) + others)[0]


def dot(a, b):
    return jnp.dot(a, b, preferred_element_type=F32)


def pack(w):
    high = w.astype(BF16).astype(F32)
    gap = jnp.zeros((64 - H, w.shape[1]), F32)
    return jnp.concatenate([high, gap, w - high, gap], axis=0).astype(BF16).T


def stand(w):
    return jnp.concatenate([w, jnp.zeros((128 - H, w.shape[1]), F32)], axis=0).T


def widen(w, first_head):
    head = lax.broadcasted_iota(jnp.int32, w.shape, 1) // P_SIZE + first_head
    picked = [jnp.take_along_axis(w, head + i, axis=1) for i in range(0, CHUNK // P_SIZE, 128 // P_SIZE)]
    return jnp.concatenate(picked, axis=1)


def beside(columns):
    lane = lax.broadcasted_iota(jnp.int32, (H, 128), 1)
    table = jnp.zeros((H, 128), F32)
    for i, column in enumerate(columns):
        table = jnp.where(lane == i, column, table)
    return table


def turned(rows):
    table = jnp.concatenate(list(rows) + [jnp.zeros((8 - len(rows), H), F32)], axis=0)
    return jnp.concatenate([table, jnp.zeros((8, 128 - H), F32)], axis=1).T[:H]


def spread_matrix(first_head):
    row = lax.broadcasted_iota(jnp.int32, (128, CHUNK), 0)
    lane = lax.broadcasted_iota(jnp.int32, (128, CHUNK), 1)
    hit = (row & 63) == first_head + lane // P_SIZE
    return jnp.where(hit, 1.0, 0.0).astype(BF16)


def silu(v):
    half = 0.5 * v
    return half + half * jnp.tanh(half)


def fetch(pairs, sems):
    copies = [pltpu.make_async_copy(source, to, sems.at[i]) for i, (source, to) in enumerate(pairs)]
    for copy in copies:
        copy.start()
    for copy in copies:
        copy.wait()


def step_sizes(raw, bias):
    raw = raw + bias
    return jnp.maximum(raw, 0.0) + jnp.log1p(jnp.exp(-jnp.abs(raw)))


def running_sums(steps):
    n = steps[0].shape[1]
    row = lax.broadcasted_iota(jnp.int32, (n, n), 0)
    lane = lax.broadcasted_iota(jnp.int32, (n, n), 1)
    upper = jnp.where(row <= lane, 1.0, 0.0).astype(BF16)
    parts = []
    for step in steps:
        high = step.astype(BF16).astype(F32)
        middle = (step - high).astype(BF16).astype(F32)
        parts += [high, middle, step - high - middle]
    sums = dot(jnp.concatenate(parts, axis=0).astype(BF16), upper)
    return [sums[i : i + H] + (sums[i + H : i + 2 * H] + sums[i + 2 * H : i + 3 * H]) for i in range(0, 3 * H * len(steps), 3 * H)]


def read_levels(points, base, total):
    n = total[0].shape[1]
    index = lax.broadcasted_iota(jnp.int32, (H, n), 1)
    found = []
    for r in range(R):
        at = points[r : r + 1, 0:1] - base
        inside = jnp.where((at >= 0) & (at < 2 * n), 1.0, 0.0)
        level = jnp.zeros((H, n), F32)
        for block in range(2):
            level += jnp.where(index + block * n == at, total[block], 0.0)
        found.append((at, inside, jnp.sum(level, axis=1, keepdims=True)))
    return found


def carry_of(found):
    carry = jnp.zeros((H, 1), F32)
    for _, inside, level in found:
        carry += inside * jnp.exp(level)
    return carry * (1.0 / R)


def tail_kernel(
    xbc_hbm, dt_hbm, bias_hbm, rate_hbm, skip_hbm, points_hbm, out_a_ref, out_b_ref, dt_ref, columns_ref, points_ref, x_ref,
    rows_ref, bias_ref, rate_ref, skip_ref, spot_ref, sems,
):
    n = xbc_hbm.shape[1]
    rows = xbc_hbm.at[0, pl.ds(n - EDGE, EDGE)]
    col = pl.multiple_of(lax.rem(lax.axis_index("seq"), 2) * HALF, 128)
    inputs = [
        pltpu.make_async_copy(xbc_hbm.at[0, :, pl.ds(from_at, width)], x_ref.at[:, pl.ds(to_at, width)], sems.at[6 + i])
        for i, (from_at, to_at, width) in enumerate(((D, HALF, BC), (col, 0, HALF)))
    ]
    for copy in inputs:
        copy.start()
    fetch(
        (
            (dt_hbm, dt_ref), (rows, rows_ref), (points_hbm, spot_ref),
            (bias_hbm, bias_ref.at[0]), (rate_hbm, rate_ref.at[0]), (skip_hbm, skip_ref.at[0]),
        ),
        sems,
    )
    tail = rows_ref[...].astype(F32)[EDGE - 8 :]
    steps = jnp.concatenate([dt_ref[0].astype(F32), jnp.zeros((4 * SIDE // 128 - H, n), F32)], axis=0).astype(BF16)
    upper = lax.broadcasted_iota(jnp.int32, (8, 128), 0) < 4
    for half, out_ref in enumerate((out_a_ref, out_b_ref)):
        pieces = [half * HALF + i for i in range(0, HALF, 128)] + [D + i for i in range(0, BC, 128)]
        pieces = [tail[:, i : i + 128] for i in pieces]
        stack = [jnp.where(upper, pltpu.roll(pieces[i], 4, 0), pieces[i + 1]) for i in range(0, len(pieces), 2)]
        out_ref[:, :128] = jnp.concatenate(stack, axis=0).astype(BF16)
        out_ref[:, 128:] = steps
    columns_ref[...] = turned((bias_ref[...], rate_ref[...], skip_ref[...]))
    spot = lax.broadcasted_iota(jnp.int32, points_ref.shape, 0)
    points = jnp.zeros(points_ref.shape, jnp.int32)
    for r in range(R):
        points = jnp.where(spot == r, spot_ref[0, r], points)
    points_ref[...] = points
    for copy in inputs:
        copy.wait()


def mark_kernel(label_ref, mark_ref):
    mark_ref[...] = jnp.zeros(mark_ref.shape, F32) + label_ref[0].astype(F32)


def steps_kernel(
    own_ref, other_ref, columns_ref, points_ref, conv_w_hbm, conv_b_hbm,
    ws_ref, wr_ref, e_ref, rows_ref, taps_ref, bias_ref, *rest,
):
    place = lax.axis_index("seq")
    core = lax.rem(place, 2)
    n = own_ref.shape[2]
    sems = rest[-1]
    col = pl.multiple_of(core * HALF, 128)
    copies = []
    for from_at, to_at, width in ((D, HALF, BC), (col, 0, HALF)):
        here, there = pl.ds(from_at, width), pl.ds(to_at, width)
        copies.append((conv_w_hbm.at[:, here], taps_ref.at[:, there]))
        copies.append((conv_b_hbm.at[here], bias_ref.at[0, there]))
    copies = [pltpu.make_async_copy(source, to, sems.at[i]) for i, (source, to) in enumerate(copies)]
    for copy in copies:
        copy.start()
    own = own_ref[0].astype(F32)
    other = other_ref[0].astype(F32)
    bias, rate, skip = columns_ref[:, 0:1], columns_ref[:, 1:2], columns_ref[:, 2:3]
    first = core == 0
    dts = [step_sizes(jnp.where(first == (block == 0), own, other), bias) for block in range(2)]
    cums = running_sums([-rate * dt for dt in dts])
    ends = [cum[:, n - 1 : n] for cum in cums]

    def store(ref, values):
        ref[:n] = stand(jnp.where(first, values[0], values[1]))
        ref[n:] = stand(jnp.where(first, values[1], values[0]))

    store(ws_ref, [dts[block] * jnp.exp(ends[block] - cums[block]) for block in range(2)])
    total = [cums[0], ends[0] + cums[1]]
    index = lax.broadcasted_iota(jnp.int32, (H, n), 1)
    weight = [jnp.zeros((H, n), F32), jnp.zeros((H, n), F32)]
    found = read_levels(points_ref[...], (place - core) * n, total)
    for at, inside, level in found:
        for block in range(2):
            seen = jnp.where(index + block * n <= at, jnp.exp(jnp.minimum(level - total[block], 0.0)), 0.0)
            weight[block] += inside * seen
    store(wr_ref, [weight[block] * dts[block] * (1.0 / R) for block in range(2)])
    e_ref[...] = stand(jnp.exp(jnp.where(first, cums[0], cums[1])))
    decay = [jnp.exp(end) for end in ends]
    back = jnp.exp(-jnp.where(first, ends[0], ends[1]))
    rows_ref[...] = pack(beside((decay[0], decay[1], skip, back)))[0:16]
    if len(rest) > 1:
        whole = beside((carry_of(found), jnp.exp(ends[0] + ends[1])))
        rest[0][...] = jnp.concatenate([whole, jnp.zeros((128 - H, 128), F32)], axis=0).T[0:8]
    for copy in copies:
        copy.wait()


def later_kernel(same_ref, cross_ref, columns_ref, points_ref, later_ref):
    place = lax.axis_index("seq")
    core = lax.rem(place, 2)
    n = same_ref.shape[1] - 128
    same, cross = same_ref[:, 128:].astype(F32)[:H], cross_ref[:, 128:].astype(F32)[:H]
    bias, rate = columns_ref[:, 0:1], columns_ref[:, 1:2]
    raws = [jnp.where((core == 0) == (block == 0), same, cross) for block in range(2)]
    cums = running_sums([-rate * step_sizes(raw, bias) for raw in raws])
    total = [cums[0], cums[0][:, n - 1 : n] + cums[1]]
    carry = carry_of(read_levels(points_ref[...], 2 * n, total))
    later_ref[...] = pack(beside((jnp.where(place < 2, carry, 0.0),)))[0:16]


def state_kernel(
    x_ref, other_ref, edge_a_ref, edge_b_ref, ws_ref, wr_ref, rows_ref, later_ref, taps_ref, bias_ref, mark_ref,
    state_ref, early_ref, act_own_ref, act_other_ref, bc_ref, *rest,
    split,
):
    reads = rest[:-2]
    bc_other_ref, read_ref = rest[-2:]
    place = lax.axis_index("seq")
    core = lax.rem(place, 2)
    first = core == 0
    n = x_ref.shape[0]
    started = jnp.where(place >= 2, 1.0, 0.0)
    edge = jnp.where(first, edge_a_ref[:, :128].astype(F32), edge_b_ref[:, :128].astype(F32)) * started
    tile = 128

    def before(at):
        pieces = []
        for i in range(at // 128, (at + CHUNK) // 128):
            piece = edge[i // 2 * 8 : i // 2 * 8 + 8]
            pieces.append(pltpu.roll(piece, 4, 0) if i % 2 == 0 else piece)
        return jnp.concatenate(pieces, axis=1)

    def convolve(at, act_refs, to):
        cols = pl.ds(at, CHUNK)
        from_cols = pl.ds(D + at - HALF if at >= HALF else pl.multiple_of(core * HALF + at, 128), CHUNK)
        taps = taps_ref[:, cols]
        bias = bias_ref[:, cols]

        def rows(side, start, count):
            return (x_ref[start : start + count, cols] if side == 0 else other_ref[0, start : start + count, from_cols]).astype(F32)

        ends = [rows(side, n - EDGE, EDGE)[EDGE - 8 :] for side in range(2)]
        chip = before(at)
        for side, act_ref in enumerate(act_refs):
            ahead = jnp.where(first == (side == 0), chip, ends[1 - side])
            for t in range(n // tile):
                if t == 0:
                    seen = jnp.concatenate([ahead, rows(side, 0, tile)], axis=0)
                else:
                    seen = rows(side, t * tile - EDGE, tile + EDGE)[EDGE - 8 :]
                last = pltpu.roll(seen, 1, 0)
                pair = taps[1:2] * seen + taps[0:1] * last
                total = bias + taps[3:4] * seen[8:] + taps[2:3] * last[8:]
                total += pltpu.roll(pair, 2, 0)[8:]
                act_ref[t * tile : (t + 1) * tile, to : to + CHUNK] = silu(total).astype(BF16)

    convolve(HALF, (bc_ref, bc_other_ref), 0)
    b_turned = [ref[:, :N].T for ref in (bc_ref, bc_other_ref)]
    both = jnp.concatenate(b_turned, axis=1)
    rows = jnp.concatenate([rows_ref[...], later_ref[...]], axis=0)

    for j in range(HALF // CHUNK):
        at = j * CHUNK
        cols = pl.ds(at, CHUNK)
        convolve(at, (act_own_ref, act_other_ref), at)
        head = core * (H // 2) + j * (CHUNK // P_SIZE)
        spread = spread_matrix(head)
        wide = dot(rows, spread)
        table, ahead = wide[:16], wide[16:17]
        act = jnp.concatenate([act_own_ref[:, cols], act_other_ref[:, cols]], axis=0).astype(F32)
        scaled = act * widen(ws_ref[...], head)
        weighted = scaled.astype(BF16)
        own = dot(b_turned[0], weighted[:n])
        other = dot(b_turned[1], weighted[n:])
        to_end = [jnp.where(first, table[1:2], 1.0), jnp.where(first, 1.0, table[1:2])]
        state = to_end[0] * own + to_end[1] * other
        early_ref[:, cols] = jnp.where(first, own, other).astype(BF16)
        state_ref[:, cols] = state.astype(BF16)
        beyond = jnp.concatenate([(ahead * to_end[0]) * scaled[:n], (ahead * to_end[1]) * scaled[n:]], axis=0)
        read = act * widen(wr_ref[...], head) + beyond
        high = read.astype(BF16)
        low = (read - high.astype(F32)).astype(BF16)
        seen = dot(both, high) + dot(both, low)
        read_ref[pl.ds(at, CHUNK)] = seen.T

    if split:
        part = D // 8
        x_bit = lax.rem(lax.axis_index("dp"), 2)
        z_bit = lax.rem(lax.axis_index("dp") // 2, 2)

        def rows(z, x, start, count):
            return read_ref[pl.ds(pl.multiple_of((2 * z + x) * part + start, 8), count)]

        rest = part - LEAD
        for q in range(2):
            here = slice(q * LEAD, (q + 1) * LEAD)
            reads[0][here] = rows(q, x_bit, 0, LEAD)
            reads[1][here] = rows(q, 1 - x_bit, 0, LEAD)
            here = slice(q * rest, (q + 1) * rest)
            reads[2][here] = rows(z_bit, q, LEAD, rest)
            reads[3][here] = rows(1 - z_bit, q, LEAD, rest)
        reads[1][2 * LEAD :] = mark_ref[...]
        reads[3][2 * rest :] = mark_ref[...]
    else:
        reads[0][...] = read_ref[...]


def diagonal_kernel(act_own_ref, act_other_ref, bc_ref, ws_ref, e_ref, rows_ref, gate_ref, near_ref, far_ref):
    core = lax.rem(lax.axis_index("seq"), 2)
    n = act_own_ref.shape[0]
    scores = lax.dot_general(bc_ref[:, N:], bc_ref[:, :N], (((1,), (1,)), ((), ())), preferred_element_type=F32)
    row = lax.broadcasted_iota(jnp.int32, (n, n), 0)
    lane = lax.broadcasted_iota(jnp.int32, (n, n), 1)
    masked = jnp.where(row >= lane, scores, 0.0).astype(BF16)
    ws = ws_ref[:n]
    for side, source in enumerate((act_own_ref, act_other_ref)):
        half = core if side == 0 else 1 - core

        @pl.loop(0, HALF // CHUNK, unroll=True)
        def _(j):
            at = pl.multiple_of(j * CHUNK, CHUNK)
            cols = pl.ds(at, CHUNK)
            head = half * (H // 2) + j * (CHUNK // P_SIZE)
            spread = spread_matrix(head)
            act = source[:, cols].astype(F32)
            weighted = (act * widen(ws, head)).astype(BF16)
            table = dot(rows_ref[...], spread)
            decay = widen(e_ref[...], head)
            value = decay * (table[3:4] * dot(masked, weighted)) + table[2:3] * act
            gate = silu(gate_ref[0, :, pl.ds(pl.multiple_of(half * HALF + at, CHUNK), CHUNK)].astype(F32))
            near_ref[side, :, cols] = value * gate
            far_ref[side, :, cols] = decay * gate


def carry_kernel(h_ref, early_ref, rows_ref, keep_ref, send_ref):
    place = lax.axis_index("seq")
    first = lax.rem(place, 2) == 0
    for j in range(HALF // CHUNK):
        cols = pl.ds(j * CHUNK, CHUNK)
        spread = spread_matrix(lax.rem(place, 2) * (H // 2) + j * (CHUNK // P_SIZE))
        chip = jnp.where(place >= 2, h_ref[:, cols].astype(F32), 0.0)
        middle = dot(rows_ref[...], spread)[0:1] * chip + early_ref[:, cols].astype(F32)
        keep_ref[:, cols] = jnp.where(first, chip, middle).astype(BF16)
        send_ref[:, cols] = jnp.where(first, middle, chip).astype(BF16)


def finish_kernel(near_ref, far_ref, bc_ref, h_own_ref, h_other_ref, gain_ref, out_hbm, g_ref, out_ref, sems):
    core = lax.rem(lax.axis_index("seq"), 2)
    n = bc_ref.shape[0]
    squares = jnp.zeros((n, CHUNK), F32)
    c_vals = bc_ref[:, N:]
    for side in range(2):
        h_ref = (h_own_ref, h_other_ref)[side]
        for j in range(HALF // CHUNK):
            cols = pl.ds(j * CHUNK, CHUNK)
            g = near_ref[side, :, cols] + far_ref[side, :, cols] * dot(c_vals, h_ref[:, cols])
            g_ref[side, :, cols] = g
            squares += g * g
    scale = lax.rsqrt(jnp.sum(squares, axis=-1, keepdims=True) * (1.0 / D) + 1e-05)
    tile = n // 4
    copies = []
    for t in range(4):
        rows = pl.ds(t * tile, tile)
        for side in range(2):
            half = core if side == 0 else 1 - core
            for j in range(HALF // CHUNK):
                cols = pl.ds(pl.multiple_of(half * HALF + j * CHUNK, CHUNK), CHUNK)
                g = g_ref[side, rows, pl.ds(j * CHUNK, CHUNK)]
                out_ref[rows, cols] = (g * scale[t * tile : (t + 1) * tile] * gain_ref[:, cols]).astype(BF16)
        copies.append(pltpu.make_async_copy(out_ref.at[rows], out_hbm.at[0, rows], sems.at[t]))
        copies[t].start()
    for copy in copies:
        copy.wait()


def join_kernel(mark_ref, a_ref, b_ref, out_ref):
    row = lax.broadcasted_iota(jnp.int32, out_ref.shape, 0)
    out_ref[...] = jnp.where(row == 0, a_ref[...] + b_ref[...], mark_ref[...])


def join(mark, a, b):
    out = jax.ShapeDtypeStruct(a.shape, a.dtype)
    return pl.pallas_call(
        join_kernel, out_shape=out, in_specs=[VMEM] * 3, out_specs=VMEM, compiler_params=params(8), name="join"
    )(mark, a, b)


def halves_kernel(
    kept_x_ref, came_x_ref, kept_z_ref, came_z_ref, mark_ref, across_ref,
    keep_a_ref, send_a_ref, keep_b_ref, send_b_ref,
    *, sequences,
):
    x_mark_ref = came_x_ref.at[kept_x_ref.shape[0] :]
    z_mark_ref = came_z_ref.at[kept_z_ref.shape[0] :]
    ones = (mark_ref[0:1] + x_mark_ref[0:1]) + (z_mark_ref[0:1] + across_ref[0:1])

    def weight(mark):
        return mark / ones - (1.0 - mark) / (sequences - ones)

    own = weight(mark_ref[1:2])
    place = lax.axis_index("dp")
    x_bit = lax.rem(place, 2)
    z_bit = lax.rem(place // 2, 2)
    work = (
        (kept_x_ref, came_x_ref, x_mark_ref, z_bit, keep_a_ref, send_a_ref),
        (kept_z_ref, came_z_ref, z_mark_ref, x_bit, keep_b_ref, send_b_ref),
    )
    for kept, came, other_mark, bit, keep, send in work:
        other = weight(other_mark[1:2])
        part = keep.shape[0]
        mine = pl.ds(pl.multiple_of(bit * part, 8), part)
        yours = pl.ds(pl.multiple_of((1 - bit) * part, 8), part)
        send[...] = own * kept[yours] + other * came[yours]
        keep[...] = own * kept[mine] + other * came[mine]


def chunks_kernel(keep_a_ref, came_a_ref, keep_b_ref, came_b_ref, keep_ref, core_ref, same_ref, cross_ref):
    place = lax.axis_index("seq")
    part = keep_ref.shape[0]
    upper = lax.rem(place // 2, 2) == 0
    first = lax.rem(place, 2) == 0
    rows = jnp.concatenate([keep_a_ref[...] + came_a_ref[...], keep_b_ref[...] + came_b_ref[...]], axis=0)
    here = jnp.where(upper, rows[: 2 * part], rows[2 * part :])
    there = jnp.where(upper, rows[2 * part :], rows[: 2 * part])
    keep_ref[...] = jnp.where(first, here[:part], here[part:])
    core_ref[...] = jnp.where(first, here[part:], here[:part])
    same_ref[...] = jnp.where(first, there[:part], there[part:])
    cross_ref[...] = jnp.where(first, there[part:], there[:part])


def planes_kernel(own_ref, same_ref, core_ref, cross_ref, keep_ref, send_ref):
    stays = lax.rem(lax.axis_index("dp") // 4, 2) == lax.rem(lax.axis_index("seq"), 2)
    own = own_ref[...] + same_ref[...]
    other = core_ref[...] + cross_ref[...]
    keep_ref[...] = jnp.where(stays, own, other)
    send_ref[...] = jnp.where(stays, other, own)


def sum_kernel(keep_ref, came_ref, out_ref):
    out_ref[...] = keep_ref[...] + came_ref[...]


def swap(k):
    return [(i, i ^ k) for i in range(8)]


def small_call(kernel, name, counts, *args):
    parts = tuple(jax.ShapeDtypeStruct((rows, N), F32) for rows in counts)
    return pl.pallas_call(
        kernel, out_shape=parts, in_specs=[VMEM] * len(args), out_specs=(VMEM,) * len(parts), compiler_params=params(8), name=name
    )(*args)


def on_device(xbc, gate_input, dt_raw, conv_weight, conv_bias, dt_bias, a_rate, d_skip, norm_gain, labels, readout):
    n = xbc.shape[1]
    places = lax.axis_size("seq")
    sequences = lax.axis_size("dp")
    chips = places // 2
    place = lax.axis_index("seq")
    core = place % 2
    split = sequences == 8 and places == 4
    pair = [(i, i ^ 1) for i in range(places)]
    shape = jax.ShapeDtypeStruct

    one_back = [(i, i ^ 3) for i in range(4)] if chips == 2 else [(i, (i + 1) % places) for i in range(places)]
    two_back = [(i, (i + 2) % places) for i in range(places)]
    dt_turned = jnp.swapaxes(dt_raw, 1, 2)
    dt_other = lax.ppermute(dt_turned, "seq", pair)
    xbc_other = lax.ppermute(xbc, "seq", pair)
    xbc_here = in_hbm(xbc)
    payload = shape((4 * SIDE // 128, 128 + n), BF16)
    tail_a, tail_b, dt_own, columns, points, x = pl.pallas_call(
        tail_kernel,
        out_shape=(payload, payload, shape((1, H, n), BF16), shape((H, 8), F32), shape((8, 128), jnp.int32), shape((n, SIDE), BF16)),
        in_specs=[HBM] * 6,
        out_specs=(VMEM,) * 6,
        scratch_shapes=[pltpu.VMEM((EDGE, CH), BF16)]
        + [pltpu.VMEM((1, H), F32)] * 3
        + [pltpu.SMEM((1, R), jnp.int32), pltpu.SemaphoreType.DMA((8,))],
        compiler_params=params(8),
        name="tail",
    )(xbc_here, in_hbm(dt_turned), in_hbm(dt_bias), in_hbm(a_rate), in_hbm(d_skip), in_hbm(readout))
    edge_a = lax.ppermute(tail_a, "seq", one_back)
    edge_b = lax.ppermute(tail_b, "seq", two_back)
    mark = pl.pallas_call(
        mark_kernel, out_shape=shape((8, N), F32), in_specs=[SMEM], out_specs=VMEM, compiler_params=params(8), name="mark"
    )(tied(labels, points))

    ws, wr, e, rows, taps, bias, *small = pl.pallas_call(
        steps_kernel,
        out_shape=(
            shape((2 * n, 128), F32), shape((2 * n, 128), F32), shape((n, 128), F32), shape((16, 128), BF16),
            shape((KW, SIDE), F32), shape((1, SIDE), F32),
        ) + ((shape((8, 128), F32),) if chips != 2 else ()),
        in_specs=[VMEM] * 4 + [HBM] * 2,
        out_specs=(VMEM,) * (7 if chips != 2 else 6),
        scratch_shapes=[pltpu.SemaphoreType.DMA((4,))],
        compiler_params=params(16),
        cost_estimate=cost(30 * n * n * 1024, 8 * n * 256),
        name="steps",
    )(dt_own, dt_other, columns, points, in_hbm(conv_weight), in_hbm(conv_bias))

    if chips == 2:
        later = pl.pallas_call(
            later_kernel,
            out_shape=shape((16, 128), BF16),
            in_specs=[VMEM] * 4,
            out_specs=VMEM,
            compiler_params=params(16),
            cost_estimate=cost(10 * n * n * 1024, 8 * n * 256),
            name="later",
        )(edge_b, edge_a, tied(columns, ws), points)
    else:
        small = small[0]
        later = jnp.zeros_like(small)
        for step in range(chips - 1):
            out = small.at[0:1].add(small[1:2] * later[0:1])
            later = lax.ppermute(out, "seq", [(i, (i - 2) % places) for i in range(places)])
            later = jnp.where(place < places - 2, later, 0.0)
        high = lax.reduce_precision(later[0, :H], 8, 7)
        gap = jnp.zeros(64 - H, F32)
        packed = jnp.concatenate([high, gap, later[0, :H] - high, gap])
        later = jnp.broadcast_to(packed, (16, 128)).astype(BF16)

    if split:
        ones = join(tied(mark, later), mark, lax.ppermute(mark, "dp", swap(4)))
    else:
        ones = mark

    read_rows = (2 * LEAD, 2 * LEAD + 8, D // 4 - 2 * LEAD, D // 4 - 2 * LEAD + 8) if split else (HALF,)
    state, early, act_own, act_other, bc, *reads = pl.pallas_call(
        functools.partial(state_kernel, split=split),
        out_shape=(
            shape((N, HALF), BF16), shape((N, HALF), BF16),
            shape((n, HALF), BF16), shape((n, HALF), BF16), shape((n, BC), BF16),
        ) + tuple(shape((count, N), F32) for count in read_rows),
        in_specs=[VMEM] * 11,
        out_specs=(VMEM,) * (5 + len(read_rows)),
        scratch_shapes=[pltpu.VMEM((n, BC), BF16), pltpu.VMEM((HALF, N), F32)],
        compiler_params=params(24),
        cost_estimate=cost(50 * n * n * D, 4 * 2 * n * SIDE),
        name="states",
    )(x, xbc_other, edge_a, edge_b, ws, wr, rows, later, taps, bias, ones)

    h = state
    for step in range(chips - 1):
        if step:
            scale = jnp.repeat(lax.dynamic_slice_in_dim(small[1, :H], core * (H // 2), H // 2), P_SIZE)
            h = (h.astype(F32) * scale + state.astype(F32)).astype(BF16)
        h = lax.ppermute(h, "seq", two_back)
        if chips > 2:
            h = jnp.where(place >= 2, h, jnp.zeros_like(h))
    act_in = lax.ppermute(act_other, "seq", pair)
    if split:
        keep_x, send_x, keep_z, send_z = reads
        came_x = lax.ppermute(send_x, "dp", swap(1))
        came_z = lax.ppermute(send_z, "dp", swap(2))
        across = lax.ppermute(tied(ones, send_x), "dp", swap(3))

    if split:
        near, reach = pl.pallas_call(
            diagonal_kernel,
            out_shape=(shape((2, n, HALF), F32), shape((2, n, HALF), F32)),
            in_specs=[VMEM] * 7,
            out_specs=(VMEM, VMEM),
            compiler_params=params(24),
            cost_estimate=cost(28 * n * n * D, 4 * n * D),
            name="diagonal",
        )(act_own, act_in, bc, ws, e, rows, gate_input)
        keep_x, near, reach = lax.optimization_barrier((keep_x, near, reach))
        keep_a, send_a, keep_b, send_b = small_call(
            functools.partial(halves_kernel, sequences=float(sequences)), "halves", (LEAD, LEAD, D // 8 - LEAD, D // 8 - LEAD),
            keep_x, came_x, keep_z, came_z, ones, across,
        )
        came_a = lax.ppermute(send_a, "dp", swap(2))
        came_b = lax.ppermute(send_b, "dp", swap(1))
        keep, to_core, to_same, to_cross = small_call(chunks_kernel, "chunks", (D // 32,) * 4, keep_a, came_a, keep_b, came_b)
        from_core = lax.ppermute(to_core, "seq", pair)
        from_same = lax.ppermute(to_same, "seq", [(i, i ^ 2) for i in range(places)])
        from_cross = lax.ppermute(to_cross, "seq", [(i, i ^ 3) for i in range(places)])
    else:
        near, reach = pl.pallas_call(
            diagonal_kernel,
            out_shape=(shape((2, n, HALF), F32), shape((2, n, HALF), F32)),
            in_specs=[VMEM] * 7,
            out_specs=(VMEM, VMEM),
            compiler_params=params(24),
            cost_estimate=cost(28 * n * n * D, 4 * n * D),
            name="diagonal",
        )(act_own, act_in, bc, ws, e, rows, gate_input)
    h = tied(h, keep) if split else h
    h_own, h_send = pl.pallas_call(
        carry_kernel, out_shape=(shape((N, HALF), BF16),) * 2, in_specs=[VMEM] * 3, out_specs=(VMEM,) * 2, compiler_params=params(8), name="carry",
        cost_estimate=cost(8 * n * n * D, 4 * N * D),
    )(h, early, rows)
    h_other = lax.ppermute(h_send, "seq", pair)
    layer_out = pl.pallas_call(
        finish_kernel,
        out_shape=shape((1, n, D), BF16),
        in_specs=[VMEM] * 6,
        out_specs=HBM,
        scratch_shapes=[pltpu.VMEM((2, n, HALF), F32), pltpu.VMEM((n, D), BF16), pltpu.SemaphoreType.DMA((4,))],
        compiler_params=params(24),
        cost_estimate=cost(20 * n * n * D, 12 * n * D),
        name="finish",
    )(near, reach, bc, h_own, h_other, norm_gain[None])
    if split:
        keep, send = small_call(planes_kernel, "planes", (D // 32,) * 2, keep, from_same, from_core, from_cross)
        came = lax.ppermute(send, "dp", swap(4))
        keep, layer_out = lax.optimization_barrier((keep, layer_out))
        steering = small_call(sum_kernel, "sum", (D // 32,), keep, came)[0]
    else:
        ones = lax.psum(mark[0, 0], "dp")
        weight = mark[0, 0] / ones - (1.0 - mark[0, 0]) / (sequences - ones)
        whole = lax.dynamic_update_slice_in_dim(jnp.zeros((D, N), F32), weight * reads[0], core * HALF, 0)
        steering = lax.psum_scatter(whole, ("dp", "seq"), scatter_dimension=0, tiled=True)
    return (layer_out, steering)


def solution(mesh):
    return jax.shard_map(
        on_device,
        mesh=mesh,
        in_specs=(
            P("dp", "seq", None),
            P("dp", "seq", None),
            P("dp", "seq", None),
            P(),
            P(),
            P(),
            P(),
            P(),
            P(),
            P("dp"),
            P("dp", None),
        ),
        out_specs=(P("dp", "seq", None), P(("dp", "seq"), None)),
        check_vma=False,
    )
```

```python
import functools

import jax
import jax.numpy as jnp
from jax import lax
from jax.experimental import pallas as pl
from jax.experimental.pallas import tpu as pltpu
from jax.sharding import PartitionSpec as P

H = 40
P_SIZE = 64
N = 128
KW = 4
R = 4
D = H * P_SIZE
HALF = D // 2
BC = 2 * N
SIDE = HALF + BC
CH = D + BC
CHUNK = 256
EDGE = 16
LEAD = 184
F32 = jnp.float32
BF16 = jnp.bfloat16
VMEM = pl.BlockSpec(memory_space=pltpu.VMEM)
SMEM = pl.BlockSpec(memory_space=pltpu.SMEM)
ANY = pl.BlockSpec(memory_space=pl.ANY)
HBM = pl.BlockSpec(memory_space=pltpu.HBM)
MIB = 1024 * 1024


def params(mib):
    return pltpu.CompilerParams(vmem_limit_bytes=mib * MIB)


def cost(flops, read):
    return pl.CostEstimate(flops=flops, bytes_accessed=read, transcendentals=0)


def in_hbm(x):
    return pltpu.with_memory_space_constraint(x, pltpu.HBM)


def tied(x, *others):
    return lax.optimization_barrier((x,) + others)[0]


def dot(a, b):
    return jnp.dot(a, b, preferred_element_type=F32)


def pack(w):
    high = w.astype(BF16).astype(F32)
    gap = jnp.zeros((64 - H, w.shape[1]), F32)
    return jnp.concatenate([high, gap, w - high, gap], axis=0).astype(BF16).T


def stand(w):
    return jnp.concatenate([w, jnp.zeros((128 - H, w.shape[1]), F32)], axis=0).T


def widen(w, first_head):
    head = lax.broadcasted_iota(jnp.int32, w.shape, 1) // P_SIZE + first_head
    picked = [jnp.take_along_axis(w, head + i, axis=1) for i in range(0, CHUNK // P_SIZE, 128 // P_SIZE)]
    return jnp.concatenate(picked, axis=1)


def beside(columns):
    lane = lax.broadcasted_iota(jnp.int32, (H, 128), 1)
    table = jnp.zeros((H, 128), F32)
    for i, column in enumerate(columns):
        table = jnp.where(lane == i, column, table)
    return table


def turned(rows):
    table = jnp.concatenate(list(rows) + [jnp.zeros((8 - len(rows), H), F32)], axis=0)
    return jnp.concatenate([table, jnp.zeros((8, 128 - H), F32)], axis=1).T[:H]


def spread_matrix(first_head):
    row = lax.broadcasted_iota(jnp.int32, (128, CHUNK), 0)
    lane = lax.broadcasted_iota(jnp.int32, (128, CHUNK), 1)
    hit = (row & 63) == first_head + lane // P_SIZE
    return jnp.where(hit, 1.0, 0.0).astype(BF16)


def silu(v):
    half = 0.5 * v
    return half + half * jnp.tanh(half)


def fetch(pairs, sems):
    copies = [pltpu.make_async_copy(source, to, sems.at[i]) for i, (source, to) in enumerate(pairs)]
    for copy in copies:
        copy.start()
    for copy in copies:
        copy.wait()


def step_sizes(raw, bias):
    raw = raw + bias
    return jnp.maximum(raw, 0.0) + jnp.log1p(jnp.exp(-jnp.abs(raw)))


def running_sums(steps):
    n = steps[0].shape[1]
    row = lax.broadcasted_iota(jnp.int32, (n, n), 0)
    lane = lax.broadcasted_iota(jnp.int32, (n, n), 1)
    upper = jnp.where(row <= lane, 1.0, 0.0).astype(BF16)
    parts = []
    for step in steps:
        high = step.astype(BF16).astype(F32)
        middle = (step - high).astype(BF16).astype(F32)
        parts += [high, middle, step - high - middle]
    sums = dot(jnp.concatenate(parts, axis=0).astype(BF16), upper)
    return [sums[i : i + H] + (sums[i + H : i + 2 * H] + sums[i + 2 * H : i + 3 * H]) for i in range(0, 3 * H * len(steps), 3 * H)]


def read_levels(points, base, total):
    n = total[0].shape[1]
    index = lax.broadcasted_iota(jnp.int32, (H, n), 1)
    found = []
    for r in range(R):
        at = points[r : r + 1, 0:1] - base
        inside = jnp.where((at >= 0) & (at < 2 * n), 1.0, 0.0)
        level = jnp.zeros((H, n), F32)
        for block in range(2):
            level += jnp.where(index + block * n == at, total[block], 0.0)
        found.append((at, inside, jnp.sum(level, axis=1, keepdims=True)))
    return found


def carry_of(found):
    carry = jnp.zeros((H, 1), F32)
    for _, inside, level in found:
        carry += inside * jnp.exp(level)
    return carry * (1.0 / R)


def tail_kernel(
    xbc_hbm, dt_hbm, bias_hbm, rate_hbm, skip_hbm, points_hbm, out_a_ref, out_b_ref, dt_ref, columns_ref, points_ref, x_ref,
    rows_ref, bias_ref, rate_ref, skip_ref, spot_ref, sems,
):
    n = xbc_hbm.shape[1]
    rows = xbc_hbm.at[0, pl.ds(n - EDGE, EDGE)]
    col = pl.multiple_of(lax.rem(lax.axis_index("seq"), 2) * HALF, 128)
    inputs = [
        pltpu.make_async_copy(xbc_hbm.at[0, :, pl.ds(from_at, width)], x_ref.at[:, pl.ds(to_at, width)], sems.at[6 + i])
        for i, (from_at, to_at, width) in enumerate(((D, HALF, BC), (col, 0, HALF)))
    ]
    for copy in inputs:
        copy.start()
    fetch(
        (
            (dt_hbm, dt_ref), (rows, rows_ref), (points_hbm, spot_ref),
            (bias_hbm, bias_ref.at[0]), (rate_hbm, rate_ref.at[0]), (skip_hbm, skip_ref.at[0]),
        ),
        sems,
    )
    tail = rows_ref[...].astype(F32)[EDGE - 8 :]
    steps = jnp.concatenate([dt_ref[0].astype(F32), jnp.zeros((4 * SIDE // 128 - H, n), F32)], axis=0).astype(BF16)
    upper = lax.broadcasted_iota(jnp.int32, (8, 128), 0) < 4
    for half, out_ref in enumerate((out_a_ref, out_b_ref)):
        pieces = [half * HALF + i for i in range(0, HALF, 128)] + [D + i for i in range(0, BC, 128)]
        pieces = [tail[:, i : i + 128] for i in pieces]
        stack = [jnp.where(upper, pltpu.roll(pieces[i], 4, 0), pieces[i + 1]) for i in range(0, len(pieces), 2)]
        out_ref[:, :128] = jnp.concatenate(stack, axis=0).astype(BF16)
        out_ref[:, 128:] = steps
    columns_ref[...] = turned((bias_ref[...], rate_ref[...], skip_ref[...]))
    spot = lax.broadcasted_iota(jnp.int32, points_ref.shape, 0)
    points = jnp.zeros(points_ref.shape, jnp.int32)
    for r in range(R):
        points = jnp.where(spot == r, spot_ref[0, r], points)
    points_ref[...] = points
    for copy in inputs:
        copy.wait()


def mark_kernel(label_ref, mark_ref):
    mark_ref[...] = jnp.zeros(mark_ref.shape, F32) + label_ref[0].astype(F32)


def steps_kernel(
    own_ref, other_ref, columns_ref, points_ref, conv_w_hbm, conv_b_hbm,
    ws_ref, wr_ref, e_ref, rows_ref, taps_ref, bias_ref, *rest,
):
    place = lax.axis_index("seq")
    core = lax.rem(place, 2)
    n = own_ref.shape[2]
    sems = rest[-1]
    col = pl.multiple_of(core * HALF, 128)
    copies = []
    for from_at, to_at, width in ((D, HALF, BC), (col, 0, HALF)):
        here, there = pl.ds(from_at, width), pl.ds(to_at, width)
        copies.append((conv_w_hbm.at[:, here], taps_ref.at[:, there]))
        copies.append((conv_b_hbm.at[here], bias_ref.at[0, there]))
    copies = [pltpu.make_async_copy(source, to, sems.at[i]) for i, (source, to) in enumerate(copies)]
    for copy in copies:
        copy.start()
    own = own_ref[0].astype(F32)
    other = other_ref[0].astype(F32)
    bias, rate, skip = columns_ref[:, 0:1], columns_ref[:, 1:2], columns_ref[:, 2:3]
    first = core == 0
    dts = [step_sizes(jnp.where(first == (block == 0), own, other), bias) for block in range(2)]
    cums = running_sums([-rate * dt for dt in dts])
    ends = [cum[:, n - 1 : n] for cum in cums]

    def store(ref, values):
        ref[:n] = stand(jnp.where(first, values[0], values[1]))
        ref[n:] = stand(jnp.where(first, values[1], values[0]))

    store(ws_ref, [dts[block] * jnp.exp(ends[block] - cums[block]) for block in range(2)])
    total = [cums[0], ends[0] + cums[1]]
    index = lax.broadcasted_iota(jnp.int32, (H, n), 1)
    weight = [jnp.zeros((H, n), F32), jnp.zeros((H, n), F32)]
    found = read_levels(points_ref[...], (place - core) * n, total)
    for at, inside, level in found:
        for block in range(2):
            seen = jnp.where(index + block * n <= at, jnp.exp(jnp.minimum(level - total[block], 0.0)), 0.0)
            weight[block] += inside * seen
    store(wr_ref, [weight[block] * dts[block] * (1.0 / R) for block in range(2)])
    e_ref[...] = stand(jnp.exp(jnp.where(first, cums[0], cums[1])))
    decay = [jnp.exp(end) for end in ends]
    back = jnp.exp(-jnp.where(first, ends[0], ends[1]))
    rows_ref[...] = pack(beside((decay[0], decay[1], skip, back)))[0:16]
    if len(rest) > 1:
        whole = beside((carry_of(found), jnp.exp(ends[0] + ends[1])))
        rest[0][...] = jnp.concatenate([whole, jnp.zeros((128 - H, 128), F32)], axis=0).T[0:8]
    for copy in copies:
        copy.wait()


def later_kernel(same_ref, cross_ref, columns_ref, points_ref, later_ref):
    place = lax.axis_index("seq")
    core = lax.rem(place, 2)
    n = same_ref.shape[1] - 128
    same, cross = same_ref[:, 128:].astype(F32)[:H], cross_ref[:, 128:].astype(F32)[:H]
    bias, rate = columns_ref[:, 0:1], columns_ref[:, 1:2]
    raws = [jnp.where((core == 0) == (block == 0), same, cross) for block in range(2)]
    cums = running_sums([-rate * step_sizes(raw, bias) for raw in raws])
    total = [cums[0], cums[0][:, n - 1 : n] + cums[1]]
    carry = carry_of(read_levels(points_ref[...], 2 * n, total))
    later_ref[...] = pack(beside((jnp.where(place < 2, carry, 0.0),)))[0:16]


def state_kernel(
    x_ref, other_ref, edge_a_ref, edge_b_ref, ws_ref, wr_ref, rows_ref, later_ref, taps_ref, bias_ref, mark_ref,
    state_ref, early_ref, act_own_ref, act_other_ref, bc_ref, *rest,
    split,
):
    reads = rest[:-2]
    bc_other_ref, read_ref = rest[-2:]
    place = lax.axis_index("seq")
    core = lax.rem(place, 2)
    first = core == 0
    n = x_ref.shape[0]
    started = jnp.where(place >= 2, 1.0, 0.0)
    edge = jnp.where(first, edge_a_ref[:, :128].astype(F32), edge_b_ref[:, :128].astype(F32)) * started
    tile = 128

    def before(at):
        pieces = []
        for i in range(at // 128, (at + CHUNK) // 128):
            piece = edge[i // 2 * 8 : i // 2 * 8 + 8]
            pieces.append(pltpu.roll(piece, 4, 0) if i % 2 == 0 else piece)
        return jnp.concatenate(pieces, axis=1)

    def convolve(at, act_refs, to):
        cols = pl.ds(at, CHUNK)
        from_cols = pl.ds(D + at - HALF if at >= HALF else pl.multiple_of(core * HALF + at, 128), CHUNK)
        taps = taps_ref[:, cols]
        bias = bias_ref[:, cols]

        def rows(side, start, count):
            return (x_ref[start : start + count, cols] if side == 0 else other_ref[0, start : start + count, from_cols]).astype(F32)

        ends = [rows(side, n - EDGE, EDGE)[EDGE - 8 :] for side in range(2)]
        chip = before(at)
        for side, act_ref in enumerate(act_refs):
            ahead = jnp.where(first == (side == 0), chip, ends[1 - side])
            for t in range(n // tile):
                if t == 0:
                    seen = jnp.concatenate([ahead, rows(side, 0, tile)], axis=0)
                else:
                    seen = rows(side, t * tile - EDGE, tile + EDGE)[EDGE - 8 :]
                last = pltpu.roll(seen, 1, 0)
                pair = taps[1:2] * seen + taps[0:1] * last
                total = bias + taps[3:4] * seen[8:] + taps[2:3] * last[8:]
                total += pltpu.roll(pair, 2, 0)[8:]
                act_ref[t * tile : (t + 1) * tile, to : to + CHUNK] = silu(total).astype(BF16)

    convolve(HALF, (bc_ref, bc_other_ref), 0)
    b_turned = [ref[:, :N].T for ref in (bc_ref, bc_other_ref)]
    both = jnp.concatenate(b_turned, axis=1)
    rows = jnp.concatenate([rows_ref[...], later_ref[...]], axis=0)

    for j in range(HALF // CHUNK):
        at = j * CHUNK
        cols = pl.ds(at, CHUNK)
        convolve(at, (act_own_ref, act_other_ref), at)
        head = core * (H // 2) + j * (CHUNK // P_SIZE)
        spread = spread_matrix(head)
        wide = dot(rows, spread)
        table, ahead = wide[:16], wide[16:17]
        act = jnp.concatenate([act_own_ref[:, cols], act_other_ref[:, cols]], axis=0).astype(F32)
        scaled = act * widen(ws_ref[...], head)
        weighted = scaled.astype(BF16)
        own = dot(b_turned[0], weighted[:n])
        other = dot(b_turned[1], weighted[n:])
        to_end = [jnp.where(first, table[1:2], 1.0), jnp.where(first, 1.0, table[1:2])]
        state = to_end[0] * own + to_end[1] * other
        early_ref[:, cols] = jnp.where(first, own, other).astype(BF16)
        state_ref[:, cols] = state.astype(BF16)
        beyond = jnp.concatenate([(ahead * to_end[0]) * scaled[:n], (ahead * to_end[1]) * scaled[n:]], axis=0)
        read = act * widen(wr_ref[...], head) + beyond
        high = read.astype(BF16)
        low = (read - high.astype(F32)).astype(BF16)
        seen = dot(both, high) + dot(both, low)
        read_ref[pl.ds(at, CHUNK)] = seen.T

    if split:
        part = D // 8
        x_bit = lax.rem(lax.axis_index("dp"), 2)
        z_bit = lax.rem(lax.axis_index("dp") // 2, 2)

        def rows(z, x, start, count):
            return read_ref[pl.ds(pl.multiple_of((2 * z + x) * part + start, 8), count)]

        rest = part - LEAD
        for q in range(2):
            here = slice(q * LEAD, (q + 1) * LEAD)
            reads[0][here] = rows(q, x_bit, 0, LEAD)
            reads[1][here] = rows(q, 1 - x_bit, 0, LEAD)
            here = slice(q * rest, (q + 1) * rest)
            reads[2][here] = rows(z_bit, q, LEAD, rest)
            reads[3][here] = rows(1 - z_bit, q, LEAD, rest)
        reads[1][2 * LEAD :] = mark_ref[...]
        reads[3][2 * rest :] = mark_ref[...]
    else:
        reads[0][...] = read_ref[...]


def diagonal_kernel(act_own_ref, act_other_ref, bc_ref, ws_ref, e_ref, rows_ref, gate_ref, near_ref, far_ref):
    core = lax.rem(lax.axis_index("seq"), 2)
    n = act_own_ref.shape[0]
    scores = lax.dot_general(bc_ref[:, N:], bc_ref[:, :N], (((1,), (1,)), ((), ())), preferred_element_type=F32)
    row = lax.broadcasted_iota(jnp.int32, (n, n), 0)
    lane = lax.broadcasted_iota(jnp.int32, (n, n), 1)
    masked = jnp.where(row >= lane, scores, 0.0).astype(BF16)
    ws = ws_ref[:n]
    for side, source in enumerate((act_own_ref, act_other_ref)):
        half = core if side == 0 else 1 - core

        @pl.loop(0, HALF // CHUNK, unroll=True)
        def _(j):
            at = pl.multiple_of(j * CHUNK, CHUNK)
            cols = pl.ds(at, CHUNK)
            head = half * (H // 2) + j * (CHUNK // P_SIZE)
            spread = spread_matrix(head)
            act = source[:, cols].astype(F32)
            weighted = (act * widen(ws, head)).astype(BF16)
            table = dot(rows_ref[...], spread)
            decay = widen(e_ref[...], head)
            value = decay * (table[3:4] * dot(masked, weighted)) + table[2:3] * act
            gate = silu(gate_ref[0, :, pl.ds(pl.multiple_of(half * HALF + at, CHUNK), CHUNK)].astype(F32))
            near_ref[side, :, cols] = value * gate
            far_ref[side, :, cols] = decay * gate


def carry_kernel(h_ref, early_ref, rows_ref, keep_ref, send_ref):
    place = lax.axis_index("seq")
    first = lax.rem(place, 2) == 0
    for j in range(HALF // CHUNK):
        cols = pl.ds(j * CHUNK, CHUNK)
        spread = spread_matrix(lax.rem(place, 2) * (H // 2) + j * (CHUNK // P_SIZE))
        chip = jnp.where(place >= 2, h_ref[:, cols].astype(F32), 0.0)
        middle = dot(rows_ref[...], spread)[0:1] * chip + early_ref[:, cols].astype(F32)
        keep_ref[:, cols] = jnp.where(first, chip, middle).astype(BF16)
        send_ref[:, cols] = jnp.where(first, middle, chip).astype(BF16)


def finish_kernel(near_ref, far_ref, bc_ref, h_own_ref, h_other_ref, gain_ref, out_hbm, g_ref, out_ref, sems):
    core = lax.rem(lax.axis_index("seq"), 2)
    n = bc_ref.shape[0]
    squares = jnp.zeros((n, CHUNK), F32)
    c_vals = bc_ref[:, N:]
    for side in range(2):
        h_ref = (h_own_ref, h_other_ref)[side]
        for j in range(HALF // CHUNK):
            cols = pl.ds(j * CHUNK, CHUNK)
            g = near_ref[side, :, cols] + far_ref[side, :, cols] * dot(c_vals, h_ref[:, cols])
            g_ref[side, :, cols] = g
            squares += g * g
    scale = lax.rsqrt(jnp.sum(squares, axis=-1, keepdims=True) * (1.0 / D) + 1e-05)
    tile = n // 4
    copies = []
    for t in range(4):
        rows = pl.ds(t * tile, tile)
        for side in range(2):
            half = core if side == 0 else 1 - core
            for j in range(HALF // CHUNK):
                cols = pl.ds(pl.multiple_of(half * HALF + j * CHUNK, CHUNK), CHUNK)
                g = g_ref[side, rows, pl.ds(j * CHUNK, CHUNK)]
                out_ref[rows, cols] = (g * scale[t * tile : (t + 1) * tile] * gain_ref[:, cols]).astype(BF16)
        copies.append(pltpu.make_async_copy(out_ref.at[rows], out_hbm.at[0, rows], sems.at[t]))
        copies[t].start()
    for copy in copies:
        copy.wait()


def join_kernel(mark_ref, a_ref, b_ref, out_ref):
    row = lax.broadcasted_iota(jnp.int32, out_ref.shape, 0)
    out_ref[...] = jnp.where(row == 0, a_ref[...] + b_ref[...], mark_ref[...])


def join(mark, a, b):
    out = jax.ShapeDtypeStruct(a.shape, a.dtype)
    return pl.pallas_call(
        join_kernel, out_shape=out, in_specs=[VMEM] * 3, out_specs=VMEM, compiler_params=params(8), name="join"
    )(mark, a, b)


def halves_kernel(
    kept_x_ref, came_x_ref, kept_z_ref, came_z_ref, mark_ref, across_ref,
    keep_a_ref, send_a_ref, keep_b_ref, send_b_ref,
    *, sequences,
):
    x_mark_ref = came_x_ref.at[kept_x_ref.shape[0] :]
    z_mark_ref = came_z_ref.at[kept_z_ref.shape[0] :]
    ones = (mark_ref[0:1] + x_mark_ref[0:1]) + (z_mark_ref[0:1] + across_ref[0:1])

    def weight(mark):
        return mark / ones - (1.0 - mark) / (sequences - ones)

    own = weight(mark_ref[1:2])
    place = lax.axis_index("dp")
    x_bit = lax.rem(place, 2)
    z_bit = lax.rem(place // 2, 2)
    work = (
        (kept_x_ref, came_x_ref, x_mark_ref, z_bit, keep_a_ref, send_a_ref),
        (kept_z_ref, came_z_ref, z_mark_ref, x_bit, keep_b_ref, send_b_ref),
    )
    for kept, came, other_mark, bit, keep, send in work:
        other = weight(other_mark[1:2])
        part = keep.shape[0]
        mine = pl.ds(pl.multiple_of(bit * part, 8), part)
        yours = pl.ds(pl.multiple_of((1 - bit) * part, 8), part)
        send[...] = own * kept[yours] + other * came[yours]
        keep[...] = own * kept[mine] + other * came[mine]


def chunks_kernel(keep_a_ref, came_a_ref, keep_b_ref, came_b_ref, keep_ref, core_ref, same_ref, cross_ref):
    place = lax.axis_index("seq")
    part = keep_ref.shape[0]
    upper = lax.rem(place // 2, 2) == 0
    first = lax.rem(place, 2) == 0
    rows = jnp.concatenate([keep_a_ref[...] + came_a_ref[...], keep_b_ref[...] + came_b_ref[...]], axis=0)
    here = jnp.where(upper, rows[: 2 * part], rows[2 * part :])
    there = jnp.where(upper, rows[2 * part :], rows[: 2 * part])
    keep_ref[...] = jnp.where(first, here[:part], here[part:])
    core_ref[...] = jnp.where(first, here[part:], here[:part])
    same_ref[...] = jnp.where(first, there[:part], there[part:])
    cross_ref[...] = jnp.where(first, there[part:], there[:part])


def planes_kernel(own_ref, same_ref, core_ref, cross_ref, keep_ref, send_ref):
    stays = lax.rem(lax.axis_index("dp") // 4, 2) == lax.rem(lax.axis_index("seq"), 2)
    own = own_ref[...] + same_ref[...]
    other = core_ref[...] + cross_ref[...]
    keep_ref[...] = jnp.where(stays, own, other)
    send_ref[...] = jnp.where(stays, other, own)


def sum_kernel(keep_ref, came_ref, out_ref):
    out_ref[...] = keep_ref[...] + came_ref[...]


def swap(k):
    return [(i, i ^ k) for i in range(8)]


def small_call(kernel, name, counts, *args):
    parts = tuple(jax.ShapeDtypeStruct((rows, N), F32) for rows in counts)
    return pl.pallas_call(
        kernel, out_shape=parts, in_specs=[VMEM] * len(args), out_specs=(VMEM,) * len(parts), compiler_params=params(8), name=name
    )(*args)


def on_device(xbc, gate_input, dt_raw, conv_weight, conv_bias, dt_bias, a_rate, d_skip, norm_gain, labels, readout):
    n = xbc.shape[1]
    places = lax.axis_size("seq")
    sequences = lax.axis_size("dp")
    chips = places // 2
    place = lax.axis_index("seq")
    core = place % 2
    split = sequences == 8 and places == 4
    pair = [(i, i ^ 1) for i in range(places)]
    shape = jax.ShapeDtypeStruct

    one_back = [(i, i ^ 3) for i in range(4)] if chips == 2 else [(i, (i + 1) % places) for i in range(places)]
    two_back = [(i, (i + 2) % places) for i in range(places)]
    dt_turned = jnp.swapaxes(dt_raw, 1, 2)
    dt_other = lax.ppermute(dt_turned, "seq", pair)
    xbc_other = lax.ppermute(xbc, "seq", pair)
    xbc_here = in_hbm(xbc)
    payload = shape((4 * SIDE // 128, 128 + n), BF16)
    tail_a, tail_b, dt_own, columns, points, x = pl.pallas_call(
        tail_kernel,
        out_shape=(payload, payload, shape((1, H, n), BF16), shape((H, 8), F32), shape((8, 128), jnp.int32), shape((n, SIDE), BF16)),
        in_specs=[HBM] * 6,
        out_specs=(VMEM,) * 6,
        scratch_shapes=[pltpu.VMEM((EDGE, CH), BF16)]
        + [pltpu.VMEM((1, H), F32)] * 3
        + [pltpu.SMEM((1, R), jnp.int32), pltpu.SemaphoreType.DMA((8,))],
        compiler_params=params(8),
        name="tail",
    )(xbc_here, in_hbm(dt_turned), in_hbm(dt_bias), in_hbm(a_rate), in_hbm(d_skip), in_hbm(readout))
    edge_a = lax.ppermute(tail_a, "seq", one_back)
    edge_b = lax.ppermute(tail_b, "seq", two_back)
    mark = pl.pallas_call(
        mark_kernel, out_shape=shape((8, N), F32), in_specs=[SMEM], out_specs=VMEM, compiler_params=params(8), name="mark"
    )(tied(labels, points))

    ws, wr, e, rows, taps, bias, *small = pl.pallas_call(
        steps_kernel,
        out_shape=(
            shape((2 * n, 128), F32), shape((2 * n, 128), F32), shape((n, 128), F32), shape((16, 128), BF16),
            shape((KW, SIDE), F32), shape((1, SIDE), F32),
        ) + ((shape((8, 128), F32),) if chips != 2 else ()),
        in_specs=[VMEM] * 4 + [HBM] * 2,
        out_specs=(VMEM,) * (7 if chips != 2 else 6),
        scratch_shapes=[pltpu.SemaphoreType.DMA((4,))],
        compiler_params=params(16),
        cost_estimate=cost(30 * n * n * 1024, 8 * n * 256),
        name="steps",
    )(dt_own, dt_other, columns, points, in_hbm(conv_weight), in_hbm(conv_bias))

    if chips == 2:
        later = pl.pallas_call(
            later_kernel,
            out_shape=shape((16, 128), BF16),
            in_specs=[VMEM] * 4,
            out_specs=VMEM,
            compiler_params=params(16),
            cost_estimate=cost(10 * n * n * 1024, 8 * n * 256),
            name="later",
        )(edge_b, edge_a, tied(columns, ws), points)
    else:
        small = small[0]
        later = jnp.zeros_like(small)
        for step in range(chips - 1):
            out = small.at[0:1].add(small[1:2] * later[0:1])
            later = lax.ppermute(out, "seq", [(i, (i - 2) % places) for i in range(places)])
            later = jnp.where(place < places - 2, later, 0.0)
        high = lax.reduce_precision(later[0, :H], 8, 7)
        gap = jnp.zeros(64 - H, F32)
        packed = jnp.concatenate([high, gap, later[0, :H] - high, gap])
        later = jnp.broadcast_to(packed, (16, 128)).astype(BF16)

    if split:
        ones = join(tied(mark, later), mark, lax.ppermute(mark, "dp", swap(4)))
    else:
        ones = mark

    read_rows = (2 * LEAD, 2 * LEAD + 8, D // 4 - 2 * LEAD, D // 4 - 2 * LEAD + 8) if split else (HALF,)
    state, early, act_own, act_other, bc, *reads = pl.pallas_call(
        functools.partial(state_kernel, split=split),
        out_shape=(
            shape((N, HALF), BF16), shape((N, HALF), BF16),
            shape((n, HALF), BF16), shape((n, HALF), BF16), shape((n, BC), BF16),
        ) + tuple(shape((count, N), F32) for count in read_rows),
        in_specs=[VMEM] * 11,
        out_specs=(VMEM,) * (5 + len(read_rows)),
        scratch_shapes=[pltpu.VMEM((n, BC), BF16), pltpu.VMEM((HALF, N), F32)],
        compiler_params=params(24),
        cost_estimate=cost(50 * n * n * D, 4 * 2 * n * SIDE),
        name="states",
    )(x, xbc_other, edge_a, edge_b, ws, wr, rows, later, taps, bias, ones)

    h = state
    for step in range(chips - 1):
        if step:
            scale = jnp.repeat(lax.dynamic_slice_in_dim(small[1, :H], core * (H // 2), H // 2), P_SIZE)
            h = (h.astype(F32) * scale + state.astype(F32)).astype(BF16)
        h = lax.ppermute(h, "seq", two_back)
        if chips > 2:
            h = jnp.where(place >= 2, h, jnp.zeros_like(h))
    act_in = lax.ppermute(act_other, "seq", pair)
    if split:
        keep_x, send_x, keep_z, send_z = reads
        came_x = lax.ppermute(send_x, "dp", swap(1))
        came_z = lax.ppermute(send_z, "dp", swap(2))
        across = lax.ppermute(tied(ones, send_x), "dp", swap(3))

    if split:
        near, reach = pl.pallas_call(
            diagonal_kernel,
            out_shape=(shape((2, n, HALF), F32), shape((2, n, HALF), F32)),
            in_specs=[VMEM] * 7,
            out_specs=(VMEM, VMEM),
            compiler_params=params(24),
            cost_estimate=cost(28 * n * n * D, 4 * n * D),
            name="diagonal",
        )(act_own, act_in, bc, ws, e, rows, gate_input)
        keep_x, near, reach = lax.optimization_barrier((keep_x, near, reach))
        keep_a, send_a, keep_b, send_b = small_call(
            functools.partial(halves_kernel, sequences=float(sequences)), "halves", (LEAD, LEAD, D // 8 - LEAD, D // 8 - LEAD),
            keep_x, came_x, keep_z, came_z, ones, across,
        )
        came_a = lax.ppermute(send_a, "dp", swap(2))
        came_b = lax.ppermute(send_b, "dp", swap(1))
        keep, to_core, to_same, to_cross = small_call(chunks_kernel, "chunks", (D // 32,) * 4, keep_a, came_a, keep_b, came_b)
        from_core = lax.ppermute(to_core, "seq", pair)
        from_same = lax.ppermute(to_same, "seq", [(i, i ^ 2) for i in range(places)])
        from_cross = lax.ppermute(to_cross, "seq", [(i, i ^ 3) for i in range(places)])
    else:
        near, reach = pl.pallas_call(
            diagonal_kernel,
            out_shape=(shape((2, n, HALF), F32), shape((2, n, HALF), F32)),
            in_specs=[VMEM] * 7,
            out_specs=(VMEM, VMEM),
            compiler_params=params(24),
            cost_estimate=cost(28 * n * n * D, 4 * n * D),
            name="diagonal",
        )(act_own, act_in, bc, ws, e, rows, gate_input)
    h = tied(h, keep) if split else h
    h_own, h_send = pl.pallas_call(
        carry_kernel, out_shape=(shape((N, HALF), BF16),) * 2, in_specs=[VMEM] * 3, out_specs=(VMEM,) * 2, compiler_params=params(8), name="carry",
        cost_estimate=cost(8 * n * n * D, 4 * N * D),
    )(h, early, rows)
    h_other = lax.ppermute(h_send, "seq", pair)
    layer_out = pl.pallas_call(
        finish_kernel,
        out_shape=shape((1, n, D), BF16),
        in_specs=[VMEM] * 6,
        out_specs=HBM,
        scratch_shapes=[pltpu.VMEM((2, n, HALF), F32), pltpu.VMEM((n, D), BF16), pltpu.SemaphoreType.DMA((4,))],
        compiler_params=params(24),
        cost_estimate=cost(20 * n * n * D, 12 * n * D),
        name="finish",
    )(near, reach, bc, h_own, h_other, norm_gain[None])
    if split:
        keep, send = small_call(planes_kernel, "planes", (D // 32,) * 2, keep, from_same, from_core, from_cross)
        came = lax.ppermute(send, "dp", swap(4))
        keep, layer_out = lax.optimization_barrier((keep, layer_out))
        steering = small_call(sum_kernel, "sum", (D // 32,), keep, came)[0]
    else:
        ones = lax.psum(mark[0, 0], "dp")
        weight = mark[0, 0] / ones - (1.0 - mark[0, 0]) / (sequences - ones)
        whole = lax.dynamic_update_slice_in_dim(jnp.zeros((D, N), F32), weight * reads[0], core * HALF, 0)
        steering = lax.psum_scatter(whole, ("dp", "seq"), scatter_dimension=0, tiled=True)
    return (layer_out, steering)


def solution(mesh):
    return jax.shard_map(
        on_device,
        mesh=mesh,
        in_specs=(
            P("dp", "seq", None),
            P("dp", "seq", None),
            P("dp", "seq", None),
            P(),
            P(),
            P(),
            P(),
            P(),
            P(),
            P("dp"),
            P("dp", None),
        ),
        out_specs=(P("dp", "seq", None), P(("dp", "seq"), None)),
        check_vma=False,
    )
```
